256 devices in a mesh: shard: 64 (over x, z, core), code: 4 (over y).
Axes of the slice: x: 4, y: 4, z: 8, core: 2. Of those that a mesh axis runs over, the one named last changes fastest.
Arguments:
- table_rows: float32 [1048576, 128], P(('shard', 'code')), as said below
- adagrad_sums: float32 [1048576, 128], P(('shard', 'code')), as said below
- lost_member: int32 [64], P('shard'), may hold values from 0 to 3, as said below
- code_weight: float32 [4], replicated, may hold values from 0.5 to 2, as said below
- new_owner: int32 [262144, 1], P(('shard', 'code')), may hold values from 0 to 63; in each aligned block of 1024 rows (0 to 1023, 1024 to 2047, ...) at most 32 rows name the same one
- pending_rows: int32 [131072], P(('shard', 'code')), may hold values from 0 to 4095
- pending_grads: float32 [131072, 128], P(('shard', 'code')), may hold values from -6 to 6
Outputs:
- moved_rows: float32 [524288, 128], P(('shard', 'code'))
- moved_sums: float32 [524288, 128], P(('shard', 'code'))
- parity_rows: float32 [131072, 128], P(('shard', 'code'))
- parity_sums: float32 [131072, 128], P(('shard', 'code'))
The draws below stay inside these ranges and needn't reach their ends.
Inputs may be any that keep to these rules, and one draw needn't show every extreme that they name: `lost_member`: one lost member for each group. `code_weight`: positive. `table_rows`: in every group the parity member's block equals the sum over c < 3 of code_weight[c] times member c's block, except that the group's lost member's block holds unrelated values. `adagrad_sums`: coded as table_rows; positive in every member but the lost one. `new_owner`: at most 32 of one device's rows name the same owner.
All inputs are finite; a program needn't handle non-finite values.
Results may differ from the reference program's by a relative error of at most 0.0003.
Values sent between devices are 32-bit elements; how exact they have to be, the bound alone decides.
No kernel may reach another device: no remote copies, remote signals or barrier semaphores. Data moves between devices by JAX's collectives and lax.ppermute only.
A program may use at most 64 MiB of HBM per device.

```python
import math
import jax
import jax.numpy as jnp
import numpy as np
from jax import lax

WIDTH = 128
ROW_DEV = 4096
PENDING_DEV = 512
SHARE_DEV = 1024
SLOT_CAP = 32
ROWS_ALL = 1048576
LOST_ALL = 262144
PENDING_ALL = 131072
N_SHARD = 64
N_CODE = 4


def shared_lost(key):
    return jax.random.randint(jax.random.fold_in(key, 71), (N_SHARD,), 0, N_CODE).astype(jnp.int32)


def shared_weight(key):
    raw = jax.random.uniform(jax.random.fold_in(key, 72), (N_CODE,), jnp.float32, math.log(0.5), math.log(2.0))
    return jnp.exp(raw)


def coded_table(data, garbage, lost, weight):
    parity = weight[0] * data[:, 0] + weight[1] * data[:, 1] + weight[2] * data[:, 2]
    table = jnp.concatenate([data, parity[:, None]], axis=1)
    member = jnp.arange(N_CODE)[None, :, None, None]
    table = jnp.where(member == lost[:, None, None, None], garbage, table)
    return table.reshape(ROWS_ALL, WIDTH)


def draw_lost_member(key, part):
    return shared_lost(key)


def draw_code_weight(key, part):
    return shared_weight(key)


def draw_table_rows(key, part):
    lost = shared_lost(key)
    weight = shared_weight(key)
    key = jax.random.fold_in(key, 3)
    groups = ROWS_ALL // (N_CODE * ROW_DEV)
    first, second = jax.random.split(key, 2)
    shape = (groups, 3, ROW_DEV, WIDTH)
    data = jax.random.normal(first, shape, jnp.float32)
    garbage = 2.0 * jax.random.normal(second, (groups, N_CODE, ROW_DEV, WIDTH), jnp.float32)
    return coded_table(data, garbage, lost, weight)


def draw_adagrad_sums(key, part):
    lost = shared_lost(key)
    weight = shared_weight(key)
    key = jax.random.fold_in(key, 5)
    groups = ROWS_ALL // (N_CODE * ROW_DEV)
    first, second = jax.random.split(key, 2)
    shape = (groups, 3, ROW_DEV, WIDTH)
    data = jnp.exp(jax.random.uniform(first, shape, jnp.float32, math.log(0.05), math.log(1.0)))
    garbage = jax.random.uniform(second, (groups, N_CODE, ROW_DEV, WIDTH), jnp.float32, 0.05, 1.0)
    return coded_table(data, garbage, lost, weight)


def touch_ends(array, rng, least, high):
    longest = array.shape.index(max(array.shape))
    spots = []
    for shift in (0, 1):
        where = [jax.random.randint(jax.random.fold_in(rng, axis), (), 0, length) for axis, length in enumerate(array.shape)]
        where[longest] = (where[longest] + shift) % array.shape[longest]
        spots.append(tuple(where))
    return array.at[spots[0]].set(least).at[spots[1]].set(high)


def block_scale(rng, dims, cuts, low, high):
    factor_of, own = 1.0, jax.random.fold_in(rng, 6)
    for position, parts in cuts:
        steps = jnp.exp(jax.random.uniform(jax.random.fold_in(own, position), (parts,), jnp.float32, low / len(cuts), high / len(cuts)))
        factor_of = factor_of * jnp.repeat(steps, dims[position] // parts).reshape([-1 if axis == position else 1 for axis in range(len(dims))])
    return factor_of


def shared_out(own_key, own, number, rows, amount, top, limit, skew):
    ranking = jax.random.permutation(own_key, amount)
    packed, ordinary = load_shares(amount, rows * top, limit, skew, True), load_shares(amount, rows * top, limit, skew, False)
    places = jnp.arange(amount)

    def named(tallies, offset_by):
        used = int((tallies > 0).sum())
        fixed = max(1, used // 4)
        moved = fixed + (places - fixed + offset_by * (used - fixed)) % max(1, amount - fixed)
        return jnp.zeros((amount,), jnp.int32).at[ranking[jnp.where(places < fixed, places, moved)]].set(jnp.asarray(tallies, jnp.int32))

    tallies = jnp.where(number % 4 == 0, named(packed, number // 4), named(ordinary, number - number // 4 - 1))
    mixed = jax.random.permutation(jax.random.fold_in(own, 3), amount)
    donor, sink = mixed[0:amount // 2 * 2:2], mixed[1:amount // 2 * 2:2]
    room = jnp.minimum(tallies[donor] - 1, limit - tallies[sink]) // 2
    room = jnp.where((donor == ranking[0]) | (sink == ranking[0]) | (tallies[sink] == 0), 0, jnp.maximum(room, 0))
    moved = jax.random.randint(jax.random.fold_in(own, 4), (amount // 2,), 0, 1 << 20) % (room + 1)
    tallies = tallies.at[donor].add(-moved).at[sink].add(moved)
    members = jnp.searchsorted(jnp.cumsum(tallies), jnp.arange(rows * top), side="right").astype(jnp.int32)
    grid = members.reshape(top, rows).T
    grid = grid[jax.random.permutation(jax.random.fold_in(own, 1), rows)]
    offset_by = jax.random.randint(jax.random.fold_in(own, 2), (rows, 1), 0, top)
    return jnp.take_along_axis(grid, (jnp.arange(top)[None, :] + offset_by) % top, axis=1)


def load_shares(number_of, total, most, lean, full):
    loads = [(1 << 20) // math.isqrt(grade ** lean) + 1 for grade in range(1, number_of + 1)]
    largest = most if full else min(most, max(-(-total // number_of), total * loads[0] // sum(loads)))
    least = 1 if total - largest >= number_of - 1 else 0
    counts, rest = [largest] + [least] * (number_of - 1), total - largest - least * (number_of - 1)
    while rest > 0:
        candidates = [i for i in range(1, number_of) if counts[i] < largest] or [i for i in range(1, number_of) if counts[i] < most]
        pool, budget = sum([loads[i] for i in candidates]), rest
        for i in candidates:
            more = min(most - counts[i], max(1, budget * loads[i] // pool), rest)
            counts[i] = counts[i] + more
            rest = rest - more
    return np.array(counts)


def scatter_about(key, extent, deviation, bound, cuts=(), kind=jnp.bfloat16):
    entries = deviation * jax.random.normal(key, extent, jnp.float32)
    if cuts:
        entries = entries * block_scale(key, extent, cuts, -0.22, 0.18)
    return jnp.clip(entries, -bound, bound).astype(kind)


def setup_inputs(seed: int = 0) -> dict:
    keys = jax.random.split(jax.random.key(seed), 8)
    table_rows = draw_table_rows(jax.random.fold_in(keys[7], 71), 0)
    adagrad_sums = draw_adagrad_sums(jax.random.fold_in(keys[7], 71), 0)
    lost_member = draw_lost_member(jax.random.fold_in(keys[7], 71), 0)
    code_weight = draw_code_weight(jax.random.fold_in(keys[7], 71), 0)
    new_owner_keys = jax.random.split(jax.random.fold_in(keys[4], 1), LOST_ALL // SHARE_DEV)
    new_owner_turns = jax.random.permutation(jax.random.fold_in(keys[4], 3), LOST_ALL // SHARE_DEV)
    new_owner = jax.vmap(lambda own, number: shared_out(jax.random.fold_in(keys[4], 2), own, number, SHARE_DEV, N_SHARD, 1, SLOT_CAP, 2))(new_owner_keys, new_owner_turns).reshape((LOST_ALL, 1))
    pending_rows = touch_ends(jax.random.randint(keys[5], (PENDING_ALL,), 0, ROW_DEV), jax.random.fold_in(keys[5], 1), 0, ROW_DEV - 1).astype(jnp.int32)
    pending_grads = scatter_about(keys[6], (PENDING_ALL, WIDTH), 1.0, 6.0, ((0, 256),), jnp.float32)
    return {"table_rows": table_rows, "adagrad_sums": adagrad_sums, "lost_member": lost_member, "code_weight": code_weight, "new_owner": new_owner, "pending_rows": pending_rows, "pending_grads": pending_grads}


step_size = 0.5
epsilon = 1e-08

def decode_weights(code_weight, lost_member):
    which = lost_member[0]
    data_weight = code_weight[:3]
    places = jnp.arange(3)
    lost_weight = jnp.sum(jnp.where(places == which, data_weight, 0.0))
    parity_lost = which == 3
    divisor = jnp.where(parity_lost, 1.0, lost_weight)
    solved = jnp.where(parity_lost, data_weight, -data_weight / divisor)
    solved = jnp.where(places == which, 0.0, solved)
    parity_part = jnp.where(parity_lost, 0.0, 1.0 / divisor)
    return jnp.concatenate([solved, parity_part[None]])

def slot_rows(owner, rows, capacity, shards):
    earlier = jnp.tril(owner[:, None] == owner[None, :], -1)
    rank = lax.optimization_barrier(jnp.sum(earlier.astype(jnp.int32), axis=1)).astype(jnp.int32)
    place = owner * capacity + rank
    empty = jnp.zeros((shards * capacity, rows.shape[1]), rows.dtype)
    return empty.at[place].set(rows)

def reference(table_rows, adagrad_sums, lost_member, code_weight, new_owner, pending_rows, pending_grads):
    weight = jax.vmap(lambda which: decode_weights(code_weight, which))(lost_member[:, None])

    def rebuild(table):
        blocks = table.reshape(N_SHARD, N_CODE, ROW_DEV, WIDTH)
        return weight[:, 0, None, None] * blocks[:, 0] + weight[:, 1, None, None] * blocks[:, 1] + weight[:, 2, None, None] * blocks[:, 2] + weight[:, 3, None, None] * blocks[:, 3]
    rebuilt_rows = rebuild(table_rows)
    rebuilt_sums = rebuild(adagrad_sums)
    group_ids = pending_rows.reshape(N_SHARD, N_CODE * PENDING_DEV)
    group_grads = pending_grads.reshape(N_SHARD, N_CODE * PENDING_DEV, WIDTH)
    totals = jax.vmap(lambda ids, grads: jax.ops.segment_sum(grads, ids, num_segments=ROW_DEV))(group_ids, group_grads)
    new_sums = rebuilt_sums + totals * totals
    new_rows = rebuilt_rows - step_size * totals / (jnp.sqrt(new_sums) + epsilon)
    owners = new_owner[:, 0].reshape(N_SHARD * N_CODE, SHARE_DEV)

    def route(table):
        pieces = table.reshape(N_SHARD * N_CODE, SHARE_DEV, WIDTH)
        sent = jax.vmap(lambda owner, rows: slot_rows(owner, rows, SLOT_CAP, N_SHARD))(owners, pieces)
        sent = sent.reshape(N_SHARD, N_CODE, N_SHARD, SLOT_CAP, WIDTH)
        return jnp.transpose(sent, (2, 1, 0, 3, 4)).reshape(N_SHARD, N_CODE, N_SHARD * SLOT_CAP, WIDTH)
    moved_rows = route(new_rows)
    moved_sums = route(new_sums)

    def encode(moved):
        total = code_weight[0] * moved[:, 0]
        for member in range(1, 4):
            total = total + code_weight[member] * moved[:, member]
        return total.reshape(N_SHARD * N_SHARD * SLOT_CAP, WIDTH)
    return (moved_rows.reshape(-1, WIDTH), moved_sums.reshape(-1, WIDTH), encode(moved_rows), encode(moved_sums))
```

```python
import jax
import jax.numpy as jnp
from jax import lax
from jax.experimental import pallas as pl
from jax.experimental.pallas import tpu as pltpu
from jax.sharding import PartitionSpec as P

step_size = 0.5
epsilon = 1e-08
MEMBERS = 4
SMEM = pl.BlockSpec(memory_space=pltpu.SMEM)
VMEM = pl.BlockSpec(memory_space=pltpu.VMEM)
PARAMS = pltpu.CompilerParams(vmem_limit_bytes=24 * 1024 * 1024)


def decode_weights(lost_ref, weight_ref):
    which = lost_ref[0]
    rows = [jnp.full((1, 128), weight_ref[c], jnp.float32) for c in range(MEMBERS)]
    parity_lost = which == 3
    divisor = jnp.where(which == 0, rows[0], jnp.where(which == 1, rows[1], rows[2]))
    divisor = jnp.where(parity_lost, jnp.ones_like(divisor), divisor)
    out = []
    for c in range(3):
        solved = jnp.where(parity_lost, rows[c], -rows[c] / divisor)
        out.append(jnp.where(which == c, jnp.zeros_like(solved), solved))
    out.append(jnp.where(parity_lost, jnp.zeros_like(divisor), 1.0 / divisor))
    return out


def split_halves(value):
    high = value.astype(jnp.bfloat16)
    low = (value - high.astype(jnp.float32)).astype(jnp.bfloat16)
    return high, low


def scale_kernel(lost_ref, weight_ref, member_ref, table_ref, out_ref):
    weights = decode_weights(lost_ref, weight_ref)
    member = member_ref[0]
    own = weights[3]
    for c in range(3):
        own = jnp.where(member == c, weights[c], own)
    out_ref[...] = own * table_ref[...]


def scale_table(lost, weight, member, table):
    rows, width = table.shape
    block = 1024
    return pl.pallas_call(
        scale_kernel,
        grid=(rows // block,),
        in_specs=[SMEM, SMEM, SMEM, pl.BlockSpec((block, width), lambda i: (i, 0))],
        out_specs=pl.BlockSpec((block, width), lambda i: (i, 0)),
        out_shape=jax.ShapeDtypeStruct(table.shape, jnp.float32),
        compiler_params=PARAMS,
        name="scale_table",
    )(lost, weight, member, table)


def totals_kernel(count, pieces, member_ref, *refs):
    piece_refs, out_ref = refs[:pieces], refs[pieces]
    first = member_ref[0] * count
    entries = piece_refs[0].shape[0] - 8
    total = jnp.zeros((count, 256), jnp.float32)
    targets = (lax.broadcasted_iota(jnp.int32, (count, 128), 0) + first).astype(jnp.float32)
    for piece in piece_refs:
        high, low = split_halves(piece[:entries, :])
        both = jnp.concatenate([high, low], axis=1)
        hits = jnp.concatenate(
            [
                jnp.where(targets == piece[entries + j : entries + j + 1, :], 1.0, 0.0).astype(jnp.bfloat16)
                for j in range(entries // 128)
            ],
            axis=1,
        )
        total = total + jnp.dot(hits, both, preferred_element_type=jnp.float32)
    out_ref[...] = total[:, :128] + total[:, 128:]


def pending_totals(member, pieces, count):
    return pl.pallas_call(
        lambda *refs: totals_kernel(count, len(pieces), *refs),
        in_specs=[SMEM] + [VMEM] * len(pieces),
        out_specs=VMEM,
        out_shape=jax.ShapeDtypeStruct((count, 128), jnp.float32),
        compiler_params=PARAMS,
        name="pending_totals",
    )(member, *pieces)


def spread(place_ref, values, out_ref, both_ref):
    high, low = split_halves(values)
    both_ref[:, :128] = high
    both_ref[:, 128:] = low
    slots, rows = out_ref.shape[0], values.shape[0]
    step = 256
    place = place_ref[...]
    for start in range(0, slots, step):
        here = lax.broadcasted_iota(jnp.int32, (step, rows), 0) + start
        pick = jnp.where(here == place, 1.0, 0.0).astype(jnp.bfloat16)
        got = jnp.dot(pick, both_ref[...], preferred_element_type=jnp.float32)
        out_ref[start : start + step, :] = got[:, :128] + got[:, 128:]


def sums_kernel(lost_ref, weight_ref, place_ref, got_ref, total_ref, out_ref, new_ref, both_ref):
    weights = decode_weights(lost_ref, weight_ref)
    count = total_ref.shape[0]
    new = weights[0] * got_ref[:count, :]
    for c in range(1, MEMBERS):
        new = new + weights[c] * got_ref[c * count : (c + 1) * count, :]
    total = total_ref[...]
    new = new + total * total
    new_ref[...] = new
    spread(place_ref, new, out_ref, both_ref)


def place_sums(lost, weight, place, got, total, slots):
    count = total.shape[0]
    return pl.pallas_call(
        sums_kernel,
        in_specs=[SMEM, SMEM, VMEM, VMEM, VMEM],
        out_specs=(VMEM, VMEM),
        out_shape=(
            jax.ShapeDtypeStruct((slots, 128), jnp.float32),
            jax.ShapeDtypeStruct((count, 128), jnp.float32),
        ),
        scratch_shapes=[pltpu.VMEM((count, 256), jnp.bfloat16)],
        compiler_params=PARAMS,
        name="place_sums",
    )(lost, weight, place, got, total)


def rows_kernel(place_ref, mine_ref, total_ref, sums_ref, out_ref, both_ref):
    new = mine_ref[...] - step_size * total_ref[...] / (jnp.sqrt(sums_ref[...]) + epsilon)
    spread(place_ref, new, out_ref, both_ref)


def place_rows(place, mine, total, sums, slots):
    count = total.shape[0]
    return pl.pallas_call(
        rows_kernel,
        in_specs=[VMEM, VMEM, VMEM, VMEM],
        out_specs=VMEM,
        out_shape=jax.ShapeDtypeStruct((slots, 128), jnp.float32),
        scratch_shapes=[pltpu.VMEM((count, 256), jnp.bfloat16)],
        compiler_params=PARAMS,
        name="place_rows",
    )(place, mine, total, sums)


def per_device(
    table_rows, adagrad_sums, lost_member, code_weight, new_owner, pending_rows, pending_grads
):
    members = lax.axis_size("code")
    shards = lax.axis_size("shard")
    member = lax.axis_index("code")
    member_ref = member.astype(jnp.int32)[None]
    share_rows = table_rows.shape[0] // members
    capacity = max(2, (2 * share_rows + shards - 1) // shards)
    slots = shards * capacity

    ids = pending_rows.astype(jnp.float32).reshape(-1, 128)
    pad = jnp.zeros((8 - ids.shape[0], 128), jnp.float32)
    packed = jnp.concatenate([pending_grads, ids, pad], axis=0)
    pieces = [packed] + [
        lax.ppermute(packed, "code", [(i, (i + k) % members) for i in range(members)])
        for k in range(1, members)
    ]
    got_sums = lax.all_to_all(adagrad_sums, "code", 0, 0, tiled=True)

    owner = new_owner[:, 0]
    earlier = jnp.tril(owner[:, None] == owner[None, :], -1)
    rank = jnp.sum(earlier.astype(jnp.int32), axis=1)
    place = (owner * capacity + rank)[None, :]

    term_rows = scale_table(lost_member, code_weight, member_ref, table_rows)
    totals = pending_totals(member_ref, pieces, share_rows)
    term_rows, got_sums = lax.optimization_barrier((term_rows, got_sums))
    mine_rows = lax.psum_scatter(term_rows, "code", scatter_dimension=0, tiled=True)

    out_sums, new_sums = place_sums(lost_member, code_weight, place, got_sums, totals, slots)
    moved_sums = lax.all_to_all(out_sums, "shard", 0, 0, tiled=True)
    out_rows = place_rows(place, mine_rows, totals, new_sums, slots)
    moved_rows = lax.all_to_all(out_rows, "shard", 0, 0, tiled=True)

    own_weight = jnp.sum(jnp.where(jnp.arange(members) == member, code_weight, 0.0))
    parity_sums = lax.psum_scatter(own_weight * moved_sums, "code", scatter_dimension=0, tiled=True)
    got = lax.all_to_all(moved_rows, "code", 0, 0, tiled=True).reshape(members, slots // members, -1)
    parity_rows = code_weight[0] * got[0]
    for c in range(1, members):
        parity_rows = parity_rows + code_weight[c] * got[c]
    return (moved_rows, moved_sums, parity_rows, parity_sums)


def solution(mesh):
    in_specs = (
        P(("shard", "code"), None),
        P(("shard", "code"), None),
        P("shard"),
        P(),
        P(("shard", "code"), None),
        P(("shard", "code")),
        P(("shard", "code"), None),
    )
    out_specs = (
        P(("shard", "code"), None),
        P(("shard", "code"), None),
        P(("shard", "code"), None),
        P(("shard", "code"), None),
    )
    return jax.shard_map(
        per_device, mesh=mesh, in_specs=in_specs, out_specs=out_specs, check_vma=False
    )
```

```python
import jax
import jax.numpy as jnp
from jax import lax
from jax.experimental import pallas as pl
from jax.experimental.pallas import tpu as pltpu
from jax.sharding import PartitionSpec as P

step_size = 0.5
epsilon = 1e-08
MEMBERS = 4
SMEM = pl.BlockSpec(memory_space=pltpu.SMEM)
VMEM = pl.BlockSpec(memory_space=pltpu.VMEM)
PARAMS = pltpu.CompilerParams(vmem_limit_bytes=24 * 1024 * 1024)


def decode_weights(lost_ref, weight_ref):
    which = lost_ref[0]
    rows = [jnp.full((1, 128), weight_ref[c], jnp.float32) for c in range(MEMBERS)]
    parity_lost = which == 3
    divisor = jnp.where(which == 0, rows[0], jnp.where(which == 1, rows[1], rows[2]))
    divisor = jnp.where(parity_lost, jnp.ones_like(divisor), divisor)
    out = []
    for c in range(3):
        solved = jnp.where(parity_lost, rows[c], -rows[c] / divisor)
        out.append(jnp.where(which == c, jnp.zeros_like(solved), solved))
    out.append(jnp.where(parity_lost, jnp.zeros_like(divisor), 1.0 / divisor))
    return out


def split_halves(value):
    high = value.astype(jnp.bfloat16)
    low = (value - high.astype(jnp.float32)).astype(jnp.bfloat16)
    return high, low


def own_row(weights, member):
    own = weights[3]
    for c in range(3):
        own = jnp.where(member == c, weights[c], own)
    return own


def kernel_call(body, name, out_shape, in_specs, out_specs, cost=0, **kwargs):
    return pl.pallas_call(
        body,
        in_specs=in_specs,
        out_specs=out_specs,
        out_shape=out_shape,
        compiler_params=PARAMS,
        cost_estimate=pl.CostEstimate(flops=cost, bytes_accessed=cost, transcendentals=0),
        name=name,
        **kwargs,
    )


def flat(rows):
    return jax.ShapeDtypeStruct((rows, 128), jnp.float32)


def scale_kernel(lost_ref, weight_ref, member_ref, table_ref, out_ref):
    out_ref[...] = own_row(decode_weights(lost_ref, weight_ref), member_ref[0]) * table_ref[...]


def scale_table(lost, weight, member, table):
    rows, width = table.shape
    block = 1024
    return kernel_call(
        scale_kernel,
        "scale_table",
        flat(rows),
        [SMEM, SMEM, SMEM, pl.BlockSpec((block, width), lambda i: (i, 0))],
        pl.BlockSpec((block, width), lambda i: (i, 0)),
        cost=2 * rows * width * 4,
        grid=(rows // block,),
    )(lost, weight, member, table)


def piece_of(quarter, half, count):
    return pl.ds(pl.multiple_of(quarter * count + half * (count // 2), 8), count // 2)


def near(member):
    return member + 1 - 2 * lax.rem(member, 2), 3 - member


def first_kernel(count, lost_ref, weight_ref, member_ref, table_ref, a_ref, b_ref):
    member = member_ref[0]
    own = own_row(decode_weights(lost_ref, weight_ref), member)
    half = count // 2
    one, two = near(member)
    a_ref[:half, :] = own * table_ref[piece_of(one, 0, count), :]
    a_ref[half:, :] = own * table_ref[piece_of(3 - one, 0, count), :]
    b_ref[:half, :] = own * table_ref[piece_of(two, 1, count), :]
    b_ref[half:, :] = own * table_ref[piece_of(near(two)[0], 1, count), :]


def second_kernel(count, lost_ref, weight_ref, member_ref, table_ref, a_ref, b_ref, c_ref, d_ref):
    member = member_ref[0]
    own = own_row(decode_weights(lost_ref, weight_ref), member)
    half = count // 2
    one, two = near(member)
    c_ref[...] = own * table_ref[piece_of(two, 0, count), :] + a_ref[half:, :]
    d_ref[...] = own * table_ref[piece_of(one, 1, count), :] + b_ref[half:, :]


def swap(array, which, members):
    pairs = [(i, i ^ 1) for i in range(members)] if which == 0 else [(i, 3 - i) for i in range(members)]
    return lax.ppermute(array, "code", pairs)


def totals_kernel(count, pieces, member_ref, *refs):
    piece_refs, out_ref = refs[:pieces], refs[pieces]
    first = member_ref[0] * count
    entries = piece_refs[0].shape[0] - 8
    total = jnp.zeros((count, 256), jnp.float32)
    targets = (lax.broadcasted_iota(jnp.int32, (count, 128), 0) + first).astype(jnp.float32)
    for piece in piece_refs:
        high, low = split_halves(piece[:entries, :])
        both = jnp.concatenate([high, low], axis=1)
        hits = jnp.concatenate(
            [
                jnp.where(targets == piece[entries + j : entries + j + 1, :], 1.0, 0.0).astype(jnp.bfloat16)
                for j in range(entries // 128)
            ],
            axis=1,
        )
        total = total + jnp.dot(hits, both, preferred_element_type=jnp.float32)
    out_ref[...] = total[:, :128] + total[:, 128:]


def pending_totals(member, pieces, count):
    return pl.pallas_call(
        lambda *refs: totals_kernel(count, len(pieces), *refs),
        in_specs=[SMEM] + [VMEM] * len(pieces),
        out_specs=VMEM,
        out_shape=jax.ShapeDtypeStruct((count, 128), jnp.float32),
        compiler_params=PARAMS,
        name="pending_totals",
    )(member, *pieces)


def spread(place_ref, values, out_ref, both_ref):
    high, low = split_halves(values)
    both_ref[:, :128] = high
    both_ref[:, 128:] = low
    slots, rows = out_ref.shape[0], values.shape[0]
    step = 256
    place = place_ref[...]
    for start in range(0, slots, step):
        here = lax.broadcasted_iota(jnp.int32, (step, rows), 0) + start
        pick = jnp.where(here == place, 1.0, 0.0).astype(jnp.bfloat16)
        got = jnp.dot(pick, both_ref[...], preferred_element_type=jnp.float32)
        out_ref[start : start + step, :] = got[:, :128] + got[:, 128:]


def sums_kernel(
    lost_ref, weight_ref, member_ref, place_ref, table_ref, a_ref, b_ref, c_ref, d_ref, total_ref, out_ref, new_ref, both_ref
):
    member = member_ref[0]
    count = total_ref.shape[0]
    half = count // 2
    own = own_row(decode_weights(lost_ref, weight_ref), member)
    total = total_ref[...]
    first = (own * table_ref[piece_of(member, 0, count), :] + a_ref[:half, :]) + c_ref[...]
    last = (own * table_ref[piece_of(member, 1, count), :] + b_ref[:half, :]) + d_ref[...]
    new = jnp.concatenate([first, last], axis=0) + total * total
    new_ref[...] = new
    spread(place_ref, new, out_ref, both_ref)


def rows_kernel(place_ref, mine_ref, total_ref, sums_ref, out_ref, both_ref):
    new = mine_ref[...] - step_size * total_ref[...] / (jnp.sqrt(sums_ref[...]) + epsilon)
    spread(place_ref, new, out_ref, both_ref)


def own_code_weight(weight_ref, member):
    own = weight_ref[3]
    for c in range(3):
        own = jnp.where(member == c, weight_ref[c], own)
    return own


def emit_kernel(weight_ref, member_ref, moved_ref, out_ref, term_ref):
    moved = moved_ref[...]
    out_ref[...] = moved
    term_ref[...] = own_code_weight(weight_ref, member_ref[0]) * moved


def copy_kernel(moved_ref, out_ref):
    out_ref[...] = moved_ref[...]


def quarter_of(which, count):
    return pl.ds(pl.multiple_of(lax.rem(which, MEMBERS) * count, 8), count)


def parity_send_kernel(weight_ref, member_ref, moved_ref, *out_refs):
    member = member_ref[0]
    own = own_code_weight(weight_ref, member)
    count = out_refs[0].shape[0]
    for k, out_ref in enumerate(out_refs):
        out_ref[...] = own * moved_ref[quarter_of(member + k + 1, count), :]


def parity_sum_kernel(weight_ref, member_ref, moved_ref, a_ref, b_ref, c_ref, out_ref):
    member = member_ref[0]
    own = own_code_weight(weight_ref, member)
    mine = own * moved_ref[quarter_of(member, out_ref.shape[0]), :]
    out_ref[...] = (mine + a_ref[...]) + (b_ref[...] + c_ref[...])


def turn(array, k, members):
    return lax.ppermute(array, "code", [(i, (i + k) % members) for i in range(members)])


def per_device(
    table_rows, adagrad_sums, lost_member, code_weight, new_owner, pending_rows, pending_grads
):
    members = lax.axis_size("code")
    shards = lax.axis_size("shard")
    member = lax.axis_index("code").astype(jnp.int32)[None]
    share_rows = table_rows.shape[0] // members
    capacity = max(2, (2 * share_rows + shards - 1) // shards)
    slots = shards * capacity
    half, quarter = share_rows // 2, slots // members
    scalars = [SMEM, SMEM, SMEM]
    key = (lost_member, code_weight, member)

    ids = pending_rows.astype(jnp.float32).reshape(-1, 128)
    pad = jnp.zeros((8 - ids.shape[0], 128), jnp.float32)
    packed = jnp.concatenate([pending_grads, ids, pad], axis=0)
    pieces = [packed] + [turn(packed, k, members) for k in (1, 3, 2)]

    send_a, send_b = kernel_call(
        lambda *refs: first_kernel(share_rows, *refs),
        "first_send",
        (flat(share_rows), flat(share_rows)),
        scalars + [VMEM],
        (VMEM, VMEM),
        cost=3 << 20,
    )(*key, adagrad_sums)
    got_a, got_b = swap(send_a, 0, members), swap(send_b, 1, members)
    send_c, send_d = kernel_call(
        lambda *refs: second_kernel(share_rows, *refs),
        "second_send",
        (flat(half), flat(half)),
        scalars + [VMEM] * 3,
        (VMEM, VMEM),
        cost=3 << 20,
    )(*key, adagrad_sums, got_a, got_b)
    got_c, got_d = swap(send_c, 1, members), swap(send_d, 0, members)

    owner = new_owner[:, 0]
    earlier = jnp.tril(owner[:, None] == owner[None, :], -1)
    rank = jnp.sum(earlier.astype(jnp.int32), axis=1)
    place = (owner * capacity + rank)[None, :]

    term_rows = scale_table(*key, table_rows)
    totals = pending_totals(member, pieces, share_rows)
    term_rows, send_c, send_d = lax.optimization_barrier((term_rows, send_c, send_d))
    mine_rows = lax.psum_scatter(term_rows, "code", scatter_dimension=0, tiled=True)

    scratch = [pltpu.VMEM((share_rows, 256), jnp.bfloat16)]
    out_sums, new_sums = kernel_call(
        sums_kernel,
        "place_sums",
        (flat(slots), flat(share_rows)),
        scalars + [VMEM] * 7,
        (VMEM, VMEM),
        cost=6 << 20,
        scratch_shapes=scratch,
    )(*key, place, adagrad_sums, got_a, got_b, got_c, got_d, totals)
    moved_sums = lax.all_to_all(out_sums, "shard", 0, 0, tiled=True)
    out_rows = kernel_call(
        rows_kernel, "place_rows", flat(slots), [VMEM] * 4, VMEM, cost=6 << 20, scratch_shapes=scratch
    )(place, mine_rows, totals, new_sums)
    moved_rows = lax.all_to_all(out_rows, "shard", 0, 0, tiled=True)

    final_sums, term_sums = kernel_call(
        emit_kernel, "emit_sums", (flat(slots), flat(slots)), [SMEM, SMEM, VMEM], (VMEM, VMEM), cost=3 << 20
    )(code_weight, member, moved_sums)
    parity_sums = lax.psum_scatter(term_sums, "code", scatter_dimension=0, tiled=True)
    sends = kernel_call(
        parity_send_kernel,
        "parity_send",
        tuple(flat(quarter) for _ in range(members - 1)),
        [SMEM, SMEM, VMEM],
        (VMEM,) * (members - 1),
        cost=2 << 20,
    )(code_weight, member, moved_rows)
    gots = [turn(send, k + 1, members) for k, send in enumerate(sends)]
    final_rows = kernel_call(copy_kernel, "emit_rows", flat(slots), [VMEM], VMEM, cost=2 << 20)(moved_rows)
    parity_rows = kernel_call(
        parity_sum_kernel, "parity_sum", flat(quarter), [SMEM, SMEM] + [VMEM] * 4, VMEM, cost=2 << 20
    )(code_weight, member, moved_rows, *gots)
    return (final_rows, final_sums, parity_rows, parity_sums)


def solution(mesh):
    in_specs = (
        P(("shard", "code"), None),
        P(("shard", "code"), None),
        P("shard"),
        P(),
        P(("shard", "code"), None),
        P(("shard", "code")),
        P(("shard", "code"), None),
    )
    out_specs = (
        P(("shard", "code"), None),
        P(("shard", "code"), None),
        P(("shard", "code"), None),
        P(("shard", "code"), None),
    )
    return jax.shard_map(
        per_device, mesh=mesh, in_specs=in_specs, out_specs=out_specs, check_vma=False
    )
```

```python
import jax
import jax.numpy as jnp
from jax import lax
from jax.experimental import pallas as pl
from jax.experimental.pallas import tpu as pltpu
from jax.sharding import PartitionSpec as P

step_size = 0.5
epsilon = 1e-08
MEMBERS = 4
SMEM = pl.BlockSpec(memory_space=pltpu.SMEM)
VMEM = pl.BlockSpec(memory_space=pltpu.VMEM)
HBM = pl.BlockSpec(memory_space=pltpu.HBM)
PARAMS = pltpu.CompilerParams(vmem_limit_bytes=24 * 1024 * 1024)


def decode_weights(lost_ref, weight_ref):
    which = lost_ref[0]
    rows = [jnp.full((1, 128), weight_ref[c], jnp.float32) for c in range(MEMBERS)]
    parity_lost = which == 3
    divisor = jnp.where(which == 0, rows[0], jnp.where(which == 1, rows[1], rows[2]))
    divisor = jnp.where(parity_lost, jnp.ones_like(divisor), divisor)
    out = []
    for c in range(3):
        solved = jnp.where(parity_lost, rows[c], -rows[c] / divisor)
        out.append(jnp.where(which == c, jnp.zeros_like(solved), solved))
    out.append(jnp.where(parity_lost, jnp.zeros_like(divisor), 1.0 / divisor))
    return out


def split_halves(value):
    high = value.astype(jnp.bfloat16)
    low = (value - high.astype(jnp.float32)).astype(jnp.bfloat16)
    return high, low


def own_row(weights, member):
    own = weights[3]
    for c in range(3):
        own = jnp.where(member == c, weights[c], own)
    return own


def kernel_call(body, name, out_shape, in_specs, out_specs, cost=0, **kwargs):
    return pl.pallas_call(
        body,
        in_specs=in_specs,
        out_specs=out_specs,
        out_shape=out_shape,
        compiler_params=PARAMS,
        cost_estimate=pl.CostEstimate(flops=cost, bytes_accessed=cost, transcendentals=0),
        name=name,
        **kwargs,
    )


def flat(rows):
    return jax.ShapeDtypeStruct((rows, 128), jnp.float32)


def near(member):
    return member + 1 - 2 * lax.rem(member, 2), 3 - member


def scaled_pieces(table_ref, own, where, outs, buf_ref, sem_ref):
    half = buf_ref.shape[1]
    copies = []
    for i, (quarter, part) in enumerate(where):
        rows = pl.ds(pl.multiple_of(quarter * (2 * half) + part * half, 8), half)
        copies.append(pltpu.make_async_copy(table_ref.at[rows, :], buf_ref.at[i], sem_ref.at[i]))
        copies[-1].start()
    for i, (out_ref, start) in enumerate(outs):
        copies[i].wait()
        out_ref[start : start + half, :] = own * buf_ref[i]


def sent_pieces(member):
    one, two = near(member)
    return [(one, 0), (3 - one, 0), (two, 1), (near(two)[0], 1)]


def kept_pieces(member):
    one, two = near(member)
    return [(two, 0), (one, 1), (member, 0), (member, 1)]


def front_kernel(
    lost_ref, weight_ref, member_ref, table_ref, grads_ref, ids_ref, a_ref, b_ref, packed_ref, buf_ref, sem_ref, pack_sem
):
    member = member_ref[0]
    entries = grads_ref.shape[0]
    grads = pltpu.make_async_copy(grads_ref, packed_ref.at[pl.ds(0, entries), :], pack_sem)
    grads.start()
    own = own_row(decode_weights(lost_ref, weight_ref), member)
    lines = ids_ref.shape[0]
    packed_ref[entries : entries + lines, :] = ids_ref[...].astype(jnp.float32)
    packed_ref[entries + lines :, :] = jnp.zeros((8 - lines, 128), jnp.float32)
    half = buf_ref.shape[1]
    outs = [(a_ref, 0), (a_ref, half), (b_ref, 0), (b_ref, half)]
    scaled_pieces(table_ref, own, sent_pieces(member), outs, buf_ref, sem_ref)
    grads.wait()


def keep_kernel(lost_ref, weight_ref, member_ref, table_ref, c_ref, d_ref, mine_ref, buf_ref, sem_ref):
    member = member_ref[0]
    own = own_row(decode_weights(lost_ref, weight_ref), member)
    half = buf_ref.shape[1]
    outs = [(c_ref, 0), (d_ref, 0), (mine_ref, 0), (mine_ref, half)]
    scaled_pieces(table_ref, own, kept_pieces(member), outs, buf_ref, sem_ref)


def both_kernel(
    lost_ref, weight_ref, member_ref, table_ref, a_ref, b_ref, c_ref, d_ref, mine_ref, buf_ref, sem_ref
):
    member = member_ref[0]
    own = own_row(decode_weights(lost_ref, weight_ref), member)
    half = buf_ref.shape[1]
    outs = [(a_ref, 0), (a_ref, half), (b_ref, 0), (b_ref, half), (c_ref, 0), (d_ref, 0), (mine_ref, 0), (mine_ref, half)]
    scaled_pieces(table_ref, own, sent_pieces(member) + kept_pieces(member), outs, buf_ref, sem_ref)


def second_kernel(c_ref, d_ref, a_ref, b_ref, out_c_ref, out_d_ref):
    half = c_ref.shape[0]
    out_c_ref[...] = c_ref[...] + a_ref[half:, :]
    out_d_ref[...] = d_ref[...] + b_ref[half:, :]


def swap(array, which, members):
    pairs = [(i, i ^ 1) for i in range(members)] if which == 0 else [(i, 3 - i) for i in range(members)]
    return lax.ppermute(array, "code", pairs)


def finish(mine_ref, a_ref, b_ref, c_ref, d_ref):
    half = c_ref.shape[0]
    first = (mine_ref[:half, :] + a_ref[:half, :]) + c_ref[...]
    last = (mine_ref[half:, :] + b_ref[:half, :]) + d_ref[...]
    return jnp.concatenate([first, last], axis=0)


def totals_kernel(count, pieces, member_ref, *refs):
    piece_refs, out_ref = refs[:pieces], refs[pieces]
    first = member_ref[0] * count
    entries = piece_refs[0].shape[0] - 8
    total = jnp.zeros((count, 256), jnp.float32)
    targets = (lax.broadcasted_iota(jnp.int32, (count, 128), 0) + first).astype(jnp.float32)
    for piece in piece_refs:
        high, low = split_halves(piece[:entries, :])
        both = jnp.concatenate([high, low], axis=1)
        hits = jnp.concatenate(
            [
                jnp.where(targets == piece[entries + j : entries + j + 1, :], 1.0, 0.0).astype(jnp.bfloat16)
                for j in range(entries // 128)
            ],
            axis=1,
        )
        total = total + jnp.dot(hits, both, preferred_element_type=jnp.float32)
    out_ref[...] = total[:, :128] + total[:, 128:]


def pending_totals(member, pieces, count):
    return pl.pallas_call(
        lambda *refs: totals_kernel(count, len(pieces), *refs),
        in_specs=[SMEM] + [VMEM] * len(pieces),
        out_specs=VMEM,
        out_shape=jax.ShapeDtypeStruct((count, 128), jnp.float32),
        compiler_params=PARAMS,
        name="pending_totals",
    )(member, *pieces)


def spread(place_ref, values, out_ref, both_ref):
    high, low = split_halves(values)
    both_ref[:, :128] = high
    both_ref[:, 128:] = low
    slots, rows = out_ref.shape[0], values.shape[0]
    step = 256
    place = place_ref[...]
    for start in range(0, slots, step):
        here = lax.broadcasted_iota(jnp.int32, (step, rows), 0) + start
        pick = jnp.where(here == place, 1.0, 0.0).astype(jnp.bfloat16)
        got = jnp.dot(pick, both_ref[...], preferred_element_type=jnp.float32)
        out_ref[start : start + step, :] = got[:, :128] + got[:, 128:]


def sums_kernel(
    place_ref, mine_ref, a_ref, b_ref, c_ref, d_ref, total_ref, out_ref, new_ref, both_ref
):
    total = total_ref[...]
    new = finish(mine_ref, a_ref, b_ref, c_ref, d_ref) + total * total
    new_ref[...] = new
    spread(place_ref, new, out_ref, both_ref)


def rows_kernel(
    place_ref, mine_ref, a_ref, b_ref, c_ref, d_ref, total_ref, sums_ref, out_ref, both_ref
):
    mine = finish(mine_ref, a_ref, b_ref, c_ref, d_ref)
    new = mine - step_size * total_ref[...] / (jnp.sqrt(sums_ref[...]) + epsilon)
    spread(place_ref, new, out_ref, both_ref)


def own_code_weight(weight_ref, member):
    own = weight_ref[3]
    for c in range(3):
        own = jnp.where(member == c, weight_ref[c], own)
    return own


def copy_kernel(moved_ref, out_ref):
    out_ref[...] = moved_ref[...]


def quarter_of(which, count):
    return pl.ds(pl.multiple_of(lax.rem(which, MEMBERS) * count, 8), count)


def parity_send_kernel(weight_ref, member_ref, moved_ref, *out_refs):
    member = member_ref[0]
    own = own_code_weight(weight_ref, member)
    count = out_refs[0].shape[0]
    for k, out_ref in enumerate(out_refs):
        out_ref[...] = own * moved_ref[quarter_of(member + k + 1, count), :]


def parity_sum_kernel(weight_ref, member_ref, moved_ref, a_ref, b_ref, c_ref, out_ref):
    member = member_ref[0]
    own = own_code_weight(weight_ref, member)
    mine = own * moved_ref[quarter_of(member, out_ref.shape[0]), :]
    out_ref[...] = (mine + a_ref[...]) + (b_ref[...] + c_ref[...])


def turn(array, k, members):
    return lax.ppermute(array, "code", [(i, (i + k) % members) for i in range(members)])


def parity_of(name, key, moved, members):
    slots = moved.shape[0]
    quarter = slots // members
    sends = kernel_call(
        parity_send_kernel,
        "parity_send_" + name,
        tuple(flat(quarter) for _ in range(members - 1)),
        [SMEM, SMEM, VMEM],
        (VMEM,) * (members - 1),
        cost=2 << 20,
    )(*key, moved)
    gots = [turn(send, k + 1, members) for k, send in enumerate(sends)]
    out = kernel_call(copy_kernel, "emit_" + name, flat(slots), [VMEM], VMEM, cost=2 << 20)(moved)
    parity = kernel_call(
        parity_sum_kernel, "parity_sum_" + name, flat(quarter), [SMEM, SMEM] + [VMEM] * 4, VMEM, cost=2 << 20
    )(*key, moved, *gots)
    return out, parity


def per_device(
    table_rows, adagrad_sums, lost_member, code_weight, new_owner, pending_rows, pending_grads
):
    members = lax.axis_size("code")
    shards = lax.axis_size("shard")
    member = lax.axis_index("code").astype(jnp.int32)[None]
    share = table_rows.shape[0] // members
    capacity = max(2, (2 * share + shards - 1) // shards)
    slots = shards * capacity
    half = share // 2
    entries = pending_grads.shape[0]
    scalars = [SMEM, SMEM, SMEM]
    key = (lost_member, code_weight, member)
    owner = new_owner[:, 0]

    def buffers(count):
        return [pltpu.VMEM((count, half, 128), jnp.float32), pltpu.SemaphoreType.DMA((count,))]

    send_a, send_b, packed = kernel_call(
        front_kernel,
        "front_send",
        (flat(share), flat(share), flat(entries + 8)),
        scalars + [HBM, HBM, VMEM],
        (VMEM, VMEM, VMEM),
        cost=3 << 20,
        scratch_shapes=buffers(4) + [pltpu.SemaphoreType.DMA],
    )(*key, adagrad_sums, pending_grads, pending_rows.reshape(-1, 128))
    got_a, got_b = swap(send_a, 0, members), swap(send_b, 1, members)
    pieces = [packed] + [turn(packed, k, members) for k in (1, 3, 2)]

    keep_c, keep_d, mine_sums = kernel_call(
        keep_kernel,
        "keep_sums",
        (flat(half), flat(half), flat(share)),
        scalars + [HBM],
        (VMEM, VMEM, VMEM),
        cost=3 << 20,
        scratch_shapes=buffers(4),
    )(*key, adagrad_sums)
    row_a, row_b, row_c, row_d, mine_rows = kernel_call(
        both_kernel,
        "weigh_rows",
        (flat(share), flat(share), flat(half), flat(half), flat(share)),
        scalars + [HBM],
        (VMEM,) * 5,
        cost=4 << 20,
        scratch_shapes=buffers(8),
    )(*key, table_rows)
    earlier = jnp.tril(owner[:, None] == owner[None, :], -1)
    rank = jnp.sum(earlier.astype(jnp.int32), axis=1)
    place = (owner * capacity + rank)[None, :]
    totals = pending_totals(member, pieces, share)

    def second(name, *args):
        return kernel_call(
            second_kernel, "second_" + name, (flat(half), flat(half)), [VMEM] * 4, (VMEM, VMEM), cost=1 << 20
        )(*args)

    totals, got_a, got_b = lax.optimization_barrier((totals, got_a, got_b))
    send_c, send_d = second("sums", keep_c, keep_d, got_a, got_b)
    got_c, got_d = swap(send_c, 1, members), swap(send_d, 0, members)
    row_a, row_b, got_c, got_d = lax.optimization_barrier((row_a, row_b, got_c, got_d))
    back_a, back_b = swap(row_a, 0, members), swap(row_b, 1, members)

    scratch = [pltpu.VMEM((share, 256), jnp.bfloat16)]
    out_sums, new_sums = kernel_call(
        sums_kernel,
        "place_sums",
        (flat(slots), flat(share)),
        [VMEM] * 7,
        (VMEM, VMEM),
        cost=6 << 20,
        scratch_shapes=scratch,
    )(place, mine_sums, got_a, got_b, got_c, got_d, totals)
    moved_sums = lax.all_to_all(out_sums, "shard", 0, 0, tiled=True)

    send_c, send_d = second("rows", row_c, row_d, back_a, back_b)
    back_c, back_d = swap(send_c, 1, members), swap(send_d, 0, members)
    out_rows = kernel_call(
        rows_kernel, "place_rows", flat(slots), [VMEM] * 8, VMEM, cost=6 << 20, scratch_shapes=scratch
    )(place, mine_rows, back_a, back_b, back_c, back_d, totals, new_sums)
    moved_rows = lax.all_to_all(out_rows, "shard", 0, 0, tiled=True)

    final_sums, parity_sums = parity_of("sums", (code_weight, member), moved_sums, members)
    final_rows, parity_rows = parity_of("rows", (code_weight, member), moved_rows, members)
    return (final_rows, final_sums, parity_rows, parity_sums)


def solution(mesh):
    in_specs = (
        P(("shard", "code"), None),
        P(("shard", "code"), None),
        P("shard"),
        P(),
        P(("shard", "code"), None),
        P(("shard", "code")),
        P(("shard", "code"), None),
    )
    out_specs = (
        P(("shard", "code"), None),
        P(("shard", "code"), None),
        P(("shard", "code"), None),
        P(("shard", "code"), None),
    )
    return jax.shard_map(
        per_device, mesh=mesh, in_specs=in_specs, out_specs=out_specs, check_vma=False
    )
```

```python
import jax
import jax.numpy as jnp
from jax import lax
from jax.experimental import pallas as pl
from jax.experimental.pallas import tpu as pltpu
from jax.sharding import PartitionSpec as P

step_size = 0.5
epsilon = 1e-08
MEMBERS = 4
SMEM = pl.BlockSpec(memory_space=pltpu.SMEM)
VMEM = pl.BlockSpec(memory_space=pltpu.VMEM)
HBM = pl.BlockSpec(memory_space=pltpu.HBM)
PARAMS = pltpu.CompilerParams(vmem_limit_bytes=16 * 1024 * 1024)


def decode_weights(lost_ref, weight_ref):
    which = lost_ref[0]
    rows = [jnp.full((1, 128), weight_ref[c], jnp.float32) for c in range(MEMBERS)]
    parity_lost = which == 3
    divisor = jnp.where(which == 0, rows[0], jnp.where(which == 1, rows[1], rows[2]))
    divisor = jnp.where(parity_lost, jnp.ones_like(divisor), divisor)
    out = []
    for c in range(3):
        solved = jnp.where(parity_lost, rows[c], -rows[c] / divisor)
        out.append(jnp.where(which == c, jnp.zeros_like(solved), solved))
    out.append(jnp.where(parity_lost, jnp.zeros_like(divisor), 1.0 / divisor))
    return out


def split_halves(value):
    high = value.astype(jnp.bfloat16)
    low = (value - high.astype(jnp.float32)).astype(jnp.bfloat16)
    return high, low


def own_row(weights, member):
    own = weights[3]
    for c in range(3):
        own = jnp.where(member == c, weights[c], own)
    return own


def kernel_call(body, name, out_shape, in_specs, out_specs, cost=0, **kwargs):
    return pl.pallas_call(
        body,
        in_specs=in_specs,
        out_specs=out_specs,
        out_shape=out_shape,
        compiler_params=PARAMS,
        cost_estimate=pl.CostEstimate(flops=cost, bytes_accessed=cost, transcendentals=0),
        name=name,
        **kwargs,
    )


def flat(rows):
    return jax.ShapeDtypeStruct((rows, 128), jnp.float32)


def near(member):
    return member + 1 - 2 * lax.rem(member, 2), 3 - member


def scaled_pieces(table_ref, own, where, outs, buf_ref, sem_ref, others=()):
    half = buf_ref.shape[1]
    copies = []
    for i, (quarter, part) in enumerate(where):
        rows = pl.ds(pl.multiple_of(quarter * (2 * half) + part * half, 8), half)
        copies.append(pltpu.make_async_copy(table_ref.at[rows, :], buf_ref.at[i], sem_ref.at[i]))
        copies[-1].start()
    for copy in others:
        copy.start()
    for i, (out_ref, start) in enumerate(outs):
        copies[i].wait()
        out_ref[start : start + half, :] = own * buf_ref[i]
    for copy in others:
        copy.wait()


def passed_pieces(member):
    one, two = near(member)
    return [(3 - one, 0), (near(two)[0], 1)]


def given_pieces(member):
    one, two = near(member)
    return [(one, 0), (two, 1)]


def kept_pieces(member):
    one, two = near(member)
    return [(two, 0), (one, 1), (member, 0), (member, 1)]


def front_kernel(
    lost_ref, weight_ref, member_ref, table_ref, grads_ref, ids_hbm, a_ref, b_ref, buf_ref, sem_ref, grad_sem, ids_ref, ids_sem
):
    member = member_ref[0]
    part, lines = grads_ref.shape[0] // 2, ids_ref.shape[0] // 2
    half = buf_ref.shape[1]
    copies = [pltpu.make_async_copy(ids_hbm, ids_ref, ids_sem)]
    for i, out_ref in enumerate((a_ref, b_ref)):
        for h in range(2):
            start = half + h * (part + 8)
            source = grads_ref.at[pl.ds(h * part, part), :]
            copies.append(pltpu.make_async_copy(source, out_ref.at[pl.ds(start, part), :], grad_sem.at[2 * i + h]))
    own = own_row(decode_weights(lost_ref, weight_ref), member)
    scaled_pieces(table_ref, own, passed_pieces(member), [(a_ref, 0), (b_ref, 0)], buf_ref, sem_ref, copies)
    ids = ids_ref[...].astype(jnp.float32)
    for out_ref in (a_ref, b_ref):
        for h in range(2):
            start = half + h * (part + 8) + part
            out_ref[start : start + lines, :] = ids[h * lines : (h + 1) * lines, :]
            out_ref[start + lines : start + 8, :] = jnp.zeros((8 - lines, 128), jnp.float32)


def keep_kernel(
    lost_ref, weight_ref, member_ref, table_ref, a_ref, b_ref, c_ref, d_ref, mine_ref, buf_ref, sem_ref
):
    member = member_ref[0]
    own = own_row(decode_weights(lost_ref, weight_ref), member)
    half = buf_ref.shape[1]
    outs = [(a_ref, 0), (b_ref, 0), (c_ref, 0), (d_ref, 0), (mine_ref, 0), (mine_ref, half)]
    scaled_pieces(table_ref, own, given_pieces(member) + kept_pieces(member), outs, buf_ref, sem_ref)


def both_kernel(
    lost_ref, weight_ref, member_ref, table_ref, a_ref, b_ref, c_ref, d_ref, mine_ref, buf_ref, sem_ref
):
    member = member_ref[0]
    own = own_row(decode_weights(lost_ref, weight_ref), member)
    half = buf_ref.shape[1]
    outs = [(a_ref, 0), (a_ref, half), (b_ref, 0), (b_ref, half), (c_ref, 0), (d_ref, 0), (mine_ref, 0), (mine_ref, half)]
    passed, given = passed_pieces(member), given_pieces(member)
    where = [passed[0], given[0], passed[1], given[1]] + kept_pieces(member)
    scaled_pieces(table_ref, own, where, outs, buf_ref, sem_ref)


def second_kernel(c_ref, d_ref, a_ref, b_ref, out_c_ref, out_d_ref):
    half = c_ref.shape[0]
    out_c_ref[:half, :] = c_ref[...] + a_ref[:half, :]
    out_d_ref[:half, :] = d_ref[...] + b_ref[:half, :]
    extra = out_c_ref.shape[0] - half
    if extra:
        out_c_ref[half:, :] = a_ref[half : half + extra, :]
        out_d_ref[half:, :] = b_ref[half + extra :, :]


def swap(array, which, members):
    pairs = [(i, i ^ 1) for i in range(members)] if which == 0 else [(i, 3 - i) for i in range(members)]
    return lax.ppermute(array, "code", pairs)


def finish(mine_ref, a_ref, b_ref, c_ref, d_ref):
    half = mine_ref.shape[0] // 2
    first = (mine_ref[:half, :] + a_ref[a_ref.shape[0] - half :, :]) + c_ref[:half, :]
    last = (mine_ref[half:, :] + b_ref[b_ref.shape[0] - half :, :]) + d_ref[:half, :]
    return jnp.concatenate([first, last], axis=0)


def add_hits(total, first, part_ref, start, entries):
    high, low = split_halves(part_ref[start : start + entries, :])
    both = jnp.concatenate([high, low], axis=1)
    targets = (lax.broadcasted_iota(jnp.int32, (total.shape[0], 128), 0) + first).astype(jnp.float32)
    lines = [part_ref[start + entries + j : start + entries + j + 1, :] for j in range(entries // 128)]
    hits = [jnp.where(targets == line, 1.0, 0.0).astype(jnp.bfloat16) for line in lines]
    return total + jnp.dot(jnp.concatenate(hits, axis=1), both, preferred_element_type=jnp.float32)


def totals_kernel(member_ref, own_ref, a_ref, b_ref, out_ref):
    count = out_ref.shape[0]
    half = count // 2
    size = (own_ref.shape[0] - half) // 2
    total = jnp.zeros((count, 256), jnp.float32)
    for ref in (own_ref, a_ref, b_ref):
        for h in range(2):
            total = add_hits(total, member_ref[0] * count, ref, half + h * size, size - 8)
    out_ref[...] = total[:, :128] + total[:, 128:]


def spread(place_ref, values, out_ref, both_ref):
    high, low = split_halves(values)
    both_ref[:, :128] = high
    both_ref[:, 128:] = low
    slots, rows = out_ref.shape[0], values.shape[0]
    step = 256
    place = place_ref[...]
    for start in range(0, slots, step):
        here = lax.broadcasted_iota(jnp.int32, (step, rows), 0) + start
        pick = jnp.where(here == place, 1.0, 0.0).astype(jnp.bfloat16)
        got = jnp.dot(pick, both_ref[...], preferred_element_type=jnp.float32)
        out_ref[start : start + step, :] = got[:, :128] + got[:, 128:]


def sums_kernel(
    member_ref, place_ref, mine_ref, a_ref, b_ref, c_ref, d_ref, part_ref, out_ref, new_ref, total_ref, both_ref
):
    count = mine_ref.shape[0]
    half = count // 2
    more = jnp.zeros((count, 256), jnp.float32)
    for ref in (c_ref, d_ref):
        more = add_hits(more, member_ref[0] * count, ref, half, ref.shape[0] - half - 8)
    total = part_ref[...] + (more[:, :128] + more[:, 128:])
    total_ref[...] = total
    new = finish(mine_ref, a_ref, b_ref, c_ref, d_ref) + total * total
    new_ref[...] = new
    spread(place_ref, new, out_ref, both_ref)


def rows_kernel(
    place_ref, mine_ref, a_ref, b_ref, c_ref, d_ref, total_ref, sums_ref, out_ref, both_ref
):
    mine = finish(mine_ref, a_ref, b_ref, c_ref, d_ref)
    new = mine - step_size * total_ref[...] / (jnp.sqrt(sums_ref[...]) + epsilon)
    spread(place_ref, new, out_ref, both_ref)


def own_code_weight(weight_ref, member):
    own = weight_ref[3]
    for c in range(3):
        own = jnp.where(member == c, weight_ref[c], own)
    return own


def copy_kernel(moved_ref, out_ref):
    out_ref[...] = moved_ref[...]


def quarter_of(which, count):
    return pl.ds(pl.multiple_of(lax.rem(which, MEMBERS) * count, 8), count)


def parity_send_kernel(weight_ref, member_ref, moved_ref, mine_ref, *out_refs):
    member = member_ref[0]
    own = own_code_weight(weight_ref, member)
    count = mine_ref.shape[0]
    for k, out_ref in enumerate(out_refs):
        out_ref[...] = own * moved_ref[quarter_of(member + k + 1, count), :]
    mine_ref[...] = own * moved_ref[quarter_of(member, count), :]


def parity_sum_kernel(mine_ref, a_ref, b_ref, c_ref, out_ref):
    out_ref[...] = (mine_ref[...] + a_ref[...]) + (b_ref[...] + c_ref[...])


def turn(array, k, members):
    return lax.ppermute(array, "code", [(i, (i + k) % members) for i in range(members)])


def parity_of(name, key, moved, members):
    slots = moved.shape[0]
    quarter = slots // members
    mine, *sends = kernel_call(
        parity_send_kernel,
        "parity_send_" + name,
        (flat(quarter),) * members,
        [SMEM, SMEM, VMEM],
        (VMEM,) * members,
        cost=2 << 20,
    )(*key, moved)
    gots = {k: turn(sends[k - 1], k, members) for k in (2, 1, 3)}
    out = kernel_call(copy_kernel, "emit_" + name, flat(slots), [VMEM], VMEM, cost=2 << 20)(moved)
    parity = kernel_call(
        parity_sum_kernel, "parity_sum_" + name, flat(quarter), [VMEM] * members, VMEM, cost=1 << 20
    )(mine, gots[1], gots[2], gots[3])
    return out, parity


def per_device(
    table_rows, adagrad_sums, lost_member, code_weight, new_owner, pending_rows, pending_grads
):
    members = lax.axis_size("code")
    shards = lax.axis_size("shard")
    member = lax.axis_index("code").astype(jnp.int32)[None]
    share = table_rows.shape[0] // members
    capacity = max(2, (2 * share + shards - 1) // shards)
    slots = shards * capacity
    half = share // 2
    entries = pending_grads.shape[0]
    scalars = [SMEM, SMEM, SMEM]
    key = (lost_member, pltpu.with_memory_space_constraint(code_weight, pltpu.HBM), member)
    owner = new_owner[:, 0]

    def buffers(count):
        return [pltpu.VMEM((count, half, 128), jnp.float32), pltpu.SemaphoreType.DMA((count,))]

    def keep_out(array):
        return pltpu.with_memory_space_constraint(array, pltpu.HBM)

    part = entries // 2 + 8
    send_a, send_b = kernel_call(
        front_kernel,
        "front_send",
        (flat(half + 2 * part), flat(half + 2 * part)),
        scalars + [HBM, HBM, HBM],
        (VMEM, VMEM),
        cost=3 << 20,
        scratch_shapes=buffers(2)
        + [pltpu.SemaphoreType.DMA((4,)), pltpu.VMEM((entries // 128, 128), jnp.int32), pltpu.SemaphoreType.DMA],
    )(*key, keep_out(adagrad_sums), keep_out(pending_grads), keep_out(pending_rows.reshape(-1, 128)))
    got_a, got_b = swap(send_a, 0, members), swap(send_b, 1, members)

    give_a, give_b, keep_c, keep_d, mine_sums = kernel_call(
        keep_kernel,
        "keep_sums",
        (flat(half), flat(half), flat(half), flat(half), flat(share)),
        scalars + [HBM],
        (VMEM,) * 5,
        cost=3 << 20,
        scratch_shapes=buffers(6),
    )(*key, keep_out(adagrad_sums))
    row_a, row_b, row_c, row_d, mine_rows = kernel_call(
        both_kernel,
        "weigh_rows",
        (flat(share), flat(share), flat(half), flat(half), flat(share)),
        scalars + [HBM],
        (VMEM,) * 5,
        cost=4 << 20,
        scratch_shapes=buffers(8),
    )(*key, keep_out(table_rows))
    give_a, give_b, row_a, row_b = lax.optimization_barrier((give_a, give_b, row_a, row_b))
    kept_a, kept_b = swap(give_a, 0, members), swap(give_b, 1, members)
    earlier = jnp.tril(owner[:, None] == owner[None, :], -1)
    rank = jnp.sum(earlier.astype(jnp.int32), axis=1)
    place = (owner * capacity + rank)[None, :]

    def second(name, extra, hint, *args):
        return kernel_call(
            second_kernel,
            "second_" + name,
            (flat(half + extra), flat(half + extra)),
            [VMEM] * 4,
            (VMEM, VMEM),
            cost=hint,
        )(*args)

    send_c, send_d = second("sums", part, 1 << 38, keep_c, keep_d, got_a, got_b)
    got_c, got_d = swap(send_c, 1, members), swap(send_d, 0, members)
    kept_a, kept_b, got_a, got_b = lax.optimization_barrier((kept_a, kept_b, got_a, got_b))
    part_totals = kernel_call(
        totals_kernel, "pending_totals", flat(share), [SMEM] + [VMEM] * 3, VMEM, cost=4 << 20
    )(member, send_a, got_a, got_b)
    row_a, row_b, got_c, got_d, part_totals, place = lax.optimization_barrier(
        (row_a, row_b, got_c, got_d, part_totals, place)
    )
    back_a, back_b = swap(row_a, 0, members), swap(row_b, 1, members)

    scratch = [pltpu.VMEM((share, 256), jnp.bfloat16)]
    out_sums, new_sums, totals = kernel_call(
        sums_kernel,
        "place_sums",
        (pltpu.VMEM((slots, 128), jnp.float32), flat(share), flat(share)),
        [SMEM] + [VMEM] * 7,
        (VMEM, VMEM, VMEM),
        cost=6 << 20,
        scratch_shapes=scratch,
    )(member, place, mine_sums, kept_a, kept_b, got_c, got_d, part_totals)
    moved_sums = lax.all_to_all(out_sums, "shard", 0, 0, tiled=True)

    send_c, send_d = second("rows", 0, 1 << 38, row_c, row_d, back_a, back_b)
    back_c, back_d = swap(send_c, 1, members), swap(send_d, 0, members)
    out_rows = kernel_call(
        rows_kernel, "place_rows", pltpu.VMEM((slots, 128), jnp.float32), [VMEM] * 8, VMEM, cost=6 << 20, scratch_shapes=scratch
    )(place, mine_rows, back_a, back_b, back_c, back_d, totals, new_sums)
    moved_rows = lax.all_to_all(out_rows, "shard", 0, 0, tiled=True)

    final_sums, parity_sums = parity_of("sums", (code_weight, member), moved_sums, members)
    final_rows, parity_rows = parity_of("rows", (code_weight, member), moved_rows, members)
    return (final_rows, final_sums, parity_rows, parity_sums)


def solution(mesh):
    in_specs = (
        P(("shard", "code"), None),
        P(("shard", "code"), None),
        P("shard"),
        P(),
        P(("shard", "code"), None),
        P(("shard", "code")),
        P(("shard", "code"), None),
    )
    out_specs = (
        P(("shard", "code"), None),
        P(("shard", "code"), None),
        P(("shard", "code"), None),
        P(("shard", "code"), None),
    )
    return jax.shard_map(
        per_device, mesh=mesh, in_specs=in_specs, out_specs=out_specs, check_vma=False
    )
```

```python
import jax
import jax.numpy as jnp
from jax import lax
from jax.experimental import pallas as pl
from jax.experimental.pallas import tpu as pltpu
from jax.sharding import PartitionSpec as P

step_size = 0.5
epsilon = 1e-08
MEMBERS = 4
SMEM = pl.BlockSpec(memory_space=pltpu.SMEM)
VMEM = pl.BlockSpec(memory_space=pltpu.VMEM)
HBM = pl.BlockSpec(memory_space=pltpu.HBM)
PARAMS = pltpu.CompilerParams(vmem_limit_bytes=16 * 1024 * 1024)


def decode_weights(lost_ref, weight_ref):
    which = lost_ref[0]
    rows = [jnp.full((1, 128), weight_ref[c], jnp.float32) for c in range(MEMBERS)]
    parity_lost = which == 3
    divisor = jnp.where(which == 0, rows[0], jnp.where(which == 1, rows[1], rows[2]))
    divisor = jnp.where(parity_lost, jnp.ones_like(divisor), divisor)
    out = []
    for c in range(3):
        solved = jnp.where(parity_lost, rows[c], -rows[c] / divisor)
        out.append(jnp.where(which == c, jnp.zeros_like(solved), solved))
    out.append(jnp.where(parity_lost, jnp.zeros_like(divisor), 1.0 / divisor))
    return out


def split_halves(value):
    high = value.astype(jnp.bfloat16)
    low = (value - high.astype(jnp.float32)).astype(jnp.bfloat16)
    return high, low


def own_row(weights, member):
    own = weights[3]
    for c in range(3):
        own = jnp.where(member == c, weights[c], own)
    return own


def kernel_call(body, name, out_shape, in_specs, out_specs, cost=0, **kwargs):
    return pl.pallas_call(
        body,
        in_specs=in_specs,
        out_specs=out_specs,
        out_shape=out_shape,
        compiler_params=PARAMS,
        cost_estimate=pl.CostEstimate(flops=cost, bytes_accessed=cost, transcendentals=0),
        name=name,
        **kwargs,
    )


def flat(rows):
    return jax.ShapeDtypeStruct((rows, 128), jnp.float32)


def near(member):
    return member + 1 - 2 * lax.rem(member, 2), 3 - member


def scaled_pieces(table_ref, own, where, outs, buf_ref, sem_ref, others=()):
    half = buf_ref.shape[1]
    copies = []
    for i, (quarter, part) in enumerate(where):
        rows = pl.ds(pl.multiple_of(quarter * (2 * half) + part * half, 8), half)
        copies.append(pltpu.make_async_copy(table_ref.at[rows, :], buf_ref.at[i], sem_ref.at[i]))
        copies[-1].start()
    for copy in others:
        copy.start()
    own = own()
    for i, (out_ref, start) in enumerate(outs):
        copies[i].wait()
        out_ref[start : start + half, :] = own * buf_ref[i]
    for copy in others:
        copy.wait()


def passed_pieces(member):
    one, two = near(member)
    return [(3 - one, 0), (near(two)[0], 1)]


def given_pieces(member):
    one, two = near(member)
    return [(one, 0), (two, 1)]


def kept_pieces(member):
    one, two = near(member)
    return [(two, 0), (one, 1), (member, 0), (member, 1)]


def front_kernel(
    lost_ref, weight_hbm, member_ref, table_ref, grads_ref, ids_hbm, a_ref, b_ref,
    buf_ref, sem_ref, grad_sem, ids_ref, weight_ref, small_sem
):
    member = member_ref[0]
    part, lines = grads_ref.shape[0] // 2, ids_ref.shape[0] // 2
    half = buf_ref.shape[1]
    copies = [pltpu.make_async_copy(ids_hbm, ids_ref, small_sem.at[0])]
    for i, out_ref in enumerate((a_ref, b_ref)):
        for h in range(2):
            start = half + h * (part + 8)
            source = grads_ref.at[pl.ds(h * part, part), :]
            copies.append(pltpu.make_async_copy(source, out_ref.at[pl.ds(start, part), :], grad_sem.at[2 * i + h]))
    weights = pltpu.make_async_copy(weight_hbm, weight_ref, small_sem.at[1])
    weights.start()

    def own():
        weights.wait()
        return own_row(decode_weights(lost_ref, weight_ref), member)

    scaled_pieces(table_ref, own, passed_pieces(member), [(a_ref, 0), (b_ref, 0)], buf_ref, sem_ref, copies)
    ids = ids_ref[...].astype(jnp.float32)
    for out_ref in (a_ref, b_ref):
        for h in range(2):
            start = half + h * (part + 8) + part
            out_ref[start : start + lines, :] = ids[h * lines : (h + 1) * lines, :]
            out_ref[start + lines : start + 8, :] = jnp.zeros((8 - lines, 128), jnp.float32)


def keep_kernel(
    lost_ref, weight_ref, member_ref, table_ref, a_ref, b_ref, c_ref, d_ref, mine_ref, buf_ref, sem_ref
):
    member = member_ref[0]
    own = lambda: own_row(decode_weights(lost_ref, weight_ref), member)
    half = buf_ref.shape[1]
    outs = [(a_ref, 0), (b_ref, 0), (c_ref, 0), (d_ref, 0), (mine_ref, 0), (mine_ref, half)]
    scaled_pieces(table_ref, own, given_pieces(member) + kept_pieces(member), outs, buf_ref, sem_ref)


def both_kernel(
    lost_ref, weight_ref, member_ref, table_ref, a_ref, b_ref, give_a_ref, give_b_ref, c_ref, d_ref, mine_ref, buf_ref, sem_ref
):
    member = member_ref[0]
    own = lambda: own_row(decode_weights(lost_ref, weight_ref), member)
    half = buf_ref.shape[1]
    outs = [(ref, 0) for ref in (a_ref, b_ref, give_a_ref, give_b_ref, c_ref, d_ref, mine_ref)] + [(mine_ref, half)]
    where = passed_pieces(member) + given_pieces(member) + kept_pieces(member)
    scaled_pieces(table_ref, own, where, outs, buf_ref, sem_ref)


def second_kernel(c_ref, d_ref, a_ref, b_ref, out_c_ref, out_d_ref):
    half = c_ref.shape[0]
    out_c_ref[:half, :] = c_ref[...] + a_ref[:half, :]
    out_d_ref[:half, :] = d_ref[...] + b_ref[:half, :]
    extra = out_c_ref.shape[0] - half
    if extra:
        out_c_ref[half:, :] = a_ref[half : half + extra, :]
        out_d_ref[half:, :] = b_ref[half + extra :, :]


def swap(array, which, members):
    pairs = [(i, i ^ 1) for i in range(members)] if which == 0 else [(i, 3 - i) for i in range(members)]
    return lax.ppermute(array, "code", pairs)


def finish(mine_ref, a_ref, b_ref, c_ref, d_ref):
    half = mine_ref.shape[0] // 2
    first = (mine_ref[:half, :] + a_ref[a_ref.shape[0] - half :, :]) + c_ref[:half, :]
    last = (mine_ref[half:, :] + b_ref[b_ref.shape[0] - half :, :]) + d_ref[:half, :]
    return jnp.concatenate([first, last], axis=0)


def add_hits(total, first, part_ref, start, entries):
    high, low = split_halves(part_ref[start : start + entries, :])
    both = jnp.concatenate([high, low], axis=1)
    targets = (lax.broadcasted_iota(jnp.int32, (total.shape[0], 128), 0) + first).astype(jnp.float32)
    lines = [part_ref[start + entries + j : start + entries + j + 1, :] for j in range(entries // 128)]
    hits = [jnp.where(targets == line, 1.0, 0.0).astype(jnp.bfloat16) for line in lines]
    return total + jnp.dot(jnp.concatenate(hits, axis=1), both, preferred_element_type=jnp.float32)


def totals_kernel(member_ref, own_ref, a_ref, b_ref, mine_ref, kept_a_ref, kept_b_ref, out_ref, base_ref):
    count = out_ref.shape[0]
    half = count // 2
    size = (own_ref.shape[0] - half) // 2
    total = jnp.zeros((count, 256), jnp.float32)
    for ref in (own_ref, a_ref, b_ref):
        for h in range(2):
            total = add_hits(total, member_ref[0] * count, ref, half + h * size, size - 8)
    out_ref[...] = total[:, :128] + total[:, 128:]
    base_ref[:half, :] = mine_ref[:half, :] + kept_a_ref[...]
    base_ref[half:, :] = mine_ref[half:, :] + kept_b_ref[...]


def spread(place_ref, values, out_ref, both_ref, stage_ref, sem_ref):
    high, low = split_halves(values)
    both_ref[:, :128] = high
    both_ref[:, 128:] = low
    slots, rows = out_ref.shape[0], values.shape[0]
    step = slots // sem_ref.shape[0]
    place = place_ref[...]
    copies = []
    for i in range(sem_ref.shape[0]):
        here = lax.broadcasted_iota(jnp.int32, (step, rows), 0) + i * step
        pick = jnp.where(here == place, 1.0, 0.0).astype(jnp.bfloat16)
        got = jnp.dot(pick, both_ref[...], preferred_element_type=jnp.float32)
        block = pl.ds(i * step, step)
        stage_ref[block, :] = got[:, :128] + got[:, 128:]
        copies.append(pltpu.make_async_copy(stage_ref.at[block, :], out_ref.at[block, :], sem_ref.at[i]))
        copies[-1].start()
    for copy in copies:
        copy.wait()


def sums_kernel(
    member_ref, place_ref, base_ref, c_ref, d_ref, part_ref, out_ref, new_ref, total_ref, both_ref, stage_ref, sem_ref
):
    count = base_ref.shape[0]
    half = count // 2
    more = jnp.zeros((count, 256), jnp.float32)
    for ref in (c_ref, d_ref):
        more = add_hits(more, member_ref[0] * count, ref, half, ref.shape[0] - half - 8)
    total = part_ref[...] + (more[:, :128] + more[:, 128:])
    total_ref[...] = total
    new = base_ref[...] + jnp.concatenate([c_ref[:half, :], d_ref[:half, :]], axis=0) + total * total
    new_ref[...] = new
    spread(place_ref, new, out_ref, both_ref, stage_ref, sem_ref)


def rows_kernel(
    place_ref, mine_ref, a_ref, b_ref, c_ref, d_ref, total_ref, sums_ref, out_ref, both_ref, stage_ref, sem_ref
):
    mine = finish(mine_ref, a_ref, b_ref, c_ref, d_ref)
    new = mine - step_size * total_ref[...] / (jnp.sqrt(sums_ref[...]) + epsilon)
    spread(place_ref, new, out_ref, both_ref, stage_ref, sem_ref)


def own_code_weight(weight_ref, member):
    own = weight_ref[3]
    for c in range(3):
        own = jnp.where(member == c, weight_ref[c], own)
    return own


def copy_kernel(moved_ref, out_ref):
    out_ref[...] = moved_ref[...]


def quarter_of(which, count):
    return pl.ds(pl.multiple_of(lax.rem(which, MEMBERS) * count, 8), count)


def parity_send_kernel(weight_ref, member_ref, moved_ref, mine_ref, *out_refs):
    member = member_ref[0]
    own = own_code_weight(weight_ref, member)
    count = mine_ref.shape[0]
    for k, out_ref in enumerate(out_refs):
        out_ref[...] = own * moved_ref[quarter_of(member + k + 1, count), :]
    mine_ref[...] = own * moved_ref[quarter_of(member, count), :]


def parity_sum_kernel(mine_ref, a_ref, b_ref, c_ref, out_ref):
    out_ref[...] = (mine_ref[...] + a_ref[...]) + (b_ref[...] + c_ref[...])


def parity_first_kernel(weight_ref, member_ref, moved_ref, *refs):
    member = member_ref[0]
    own = own_code_weight(weight_ref, member)
    half = refs[0].shape[0]
    outs = [(ref, 0) for ref in refs] + [(refs[-1], half)]
    where = passed_pieces(member) + given_pieces(member) + kept_pieces(member)
    for (out_ref, start), (quarter, part) in zip(outs, where):
        rows = pl.ds(pl.multiple_of(quarter * (2 * half) + part * half, 8), half)
        out_ref[start : start + half, :] = own * moved_ref[rows, :]


def parity_last_kernel(mine_ref, a_ref, b_ref, c_ref, d_ref, out_ref):
    out_ref[...] = finish(mine_ref, a_ref, b_ref, c_ref, d_ref)


def turn(array, k, members):
    return lax.ppermute(array, "code", [(i, (i + k) % members) for i in range(members)])


def second(name, extra, hint, *args):
    half = args[0].shape[0]
    return kernel_call(
        second_kernel,
        "second_" + name,
        (flat(half + extra), flat(half + extra)),
        [VMEM] * 4,
        (VMEM, VMEM),
        cost=hint,
    )(*args)


def parity_relayed(name, key, moved, members):
    slots = moved.shape[0]
    quarter = slots // members
    half = quarter // 2
    a, b, give_a, give_b, keep_c, keep_d, mine = kernel_call(
        parity_first_kernel,
        "parity_first_" + name,
        (flat(half),) * 6 + (flat(quarter),),
        [SMEM, SMEM, VMEM],
        (VMEM,) * 7,
        cost=2 << 20,
    )(*key, moved)
    back_a, back_b = swap(a, 0, members), swap(b, 1, members)
    stay_a, stay_b = swap(give_a, 0, members), swap(give_b, 1, members)
    send_c, send_d = second("parity_" + name, 0, 1 << 33, keep_c, keep_d, back_a, back_b)
    back_c, back_d = swap(send_c, 1, members), swap(send_d, 0, members)
    out = kernel_call(copy_kernel, "emit_" + name, flat(slots), [VMEM], VMEM, cost=2 << 20)(moved)
    parity = kernel_call(
        parity_last_kernel, "parity_last_" + name, flat(quarter), [VMEM] * 5, VMEM, cost=1 << 20
    )(mine, stay_a, stay_b, back_c, back_d)
    return out, parity


def parity_of(name, key, moved, members):
    slots = moved.shape[0]
    quarter = slots // members
    mine, *sends = kernel_call(
        parity_send_kernel,
        "parity_send_" + name,
        (flat(quarter),) * members,
        [SMEM, SMEM, VMEM],
        (VMEM,) * members,
        cost=2 << 20,
    )(*key, moved)
    gots = {k: turn(sends[k - 1], k, members) for k in (2, 1, 3)}
    out = kernel_call(copy_kernel, "emit_" + name, flat(slots), [VMEM], VMEM, cost=2 << 20)(moved)
    parity = kernel_call(
        parity_sum_kernel, "parity_sum_" + name, flat(quarter), [VMEM] * members, VMEM, cost=1 << 20
    )(mine, gots[1], gots[2], gots[3])
    return out, parity


def per_device(
    table_rows, adagrad_sums, lost_member, code_weight, new_owner, pending_rows, pending_grads
):
    members = lax.axis_size("code")
    shards = lax.axis_size("shard")
    member = lax.axis_index("code").astype(jnp.int32)[None]
    share = table_rows.shape[0] // members
    capacity = max(2, (2 * share + shards - 1) // shards)
    slots = shards * capacity
    half = share // 2
    entries = pending_grads.shape[0]
    scalars = [SMEM, SMEM, SMEM]
    key = (lost_member, pltpu.with_memory_space_constraint(code_weight, pltpu.HBM), member)
    owner = new_owner[:, 0]

    def buffers(count):
        return [pltpu.VMEM((count, half, 128), jnp.float32), pltpu.SemaphoreType.DMA((count,))]

    def keep_out(array):
        return pltpu.with_memory_space_constraint(array, pltpu.HBM)

    part = entries // 2 + 8
    send_a, send_b = kernel_call(
        front_kernel,
        "front_send",
        (flat(half + 2 * part), flat(half + 2 * part)),
        [SMEM, HBM, SMEM, HBM, HBM, HBM],
        (VMEM, VMEM),
        cost=3 << 20,
        scratch_shapes=buffers(2)
        + [pltpu.SemaphoreType.DMA((4,)), pltpu.VMEM((entries // 128, 128), jnp.int32)]
        + [pltpu.SMEM((members,), jnp.float32), pltpu.SemaphoreType.DMA((2,))],
    )(*key, keep_out(adagrad_sums), keep_out(pending_grads), keep_out(pending_rows.reshape(-1, 128)))
    got_a, got_b = swap(send_a, 0, members), swap(send_b, 1, members)

    give_a, give_b, keep_c, keep_d, mine_sums = kernel_call(
        keep_kernel,
        "keep_sums",
        (flat(half), flat(half), flat(half), flat(half), flat(share)),
        scalars + [HBM],
        (VMEM,) * 5,
        cost=3 << 20,
        scratch_shapes=buffers(6),
    )(*key, keep_out(adagrad_sums))
    row_a, row_b, row_give_a, row_give_b, row_c, row_d, mine_rows = kernel_call(
        both_kernel,
        "weigh_rows",
        (flat(half),) * 6 + (flat(share),),
        scalars + [HBM],
        (VMEM,) * 7,
        cost=4 << 20,
        scratch_shapes=buffers(8),
    )(*key, keep_out(table_rows))
    give_a, give_b, row_a, row_b = lax.optimization_barrier((give_a, give_b, row_a, row_b))
    kept_a, kept_b = swap(give_a, 0, members), swap(give_b, 1, members)
    earlier = jnp.tril(owner[:, None] == owner[None, :], -1)
    rank = jnp.sum(earlier.astype(jnp.int32), axis=1)
    place = (owner * capacity + rank)[None, :]

    send_c, send_d = second("sums", part, 1 << 38, keep_c, keep_d, got_a, got_b)
    got_c, got_d = swap(send_c, 1, members), swap(send_d, 0, members)
    kept_a, kept_b, got_a, got_b = lax.optimization_barrier((kept_a, kept_b, got_a, got_b))
    part_totals, base_sums = kernel_call(
        totals_kernel, "pending_totals", (flat(share), flat(share)), [SMEM] + [VMEM] * 6, (VMEM, VMEM), cost=4 << 20
    )(member, send_a, got_a, got_b, mine_sums, kept_a, kept_b)
    row_a, row_b, row_give_a, row_give_b, got_c, got_d, part_totals, place = lax.optimization_barrier(
        (row_a, row_b, row_give_a, row_give_b, got_c, got_d, part_totals, place)
    )
    back_a, back_b = swap(row_a, 0, members), swap(row_b, 1, members)
    stay_a, stay_b = swap(row_give_a, 0, members), swap(row_give_b, 1, members)

    scratch = [
        pltpu.VMEM((share, 256), jnp.bfloat16),
        pltpu.VMEM((slots, 128), jnp.float32),
        pltpu.SemaphoreType.DMA((8,)),
    ]
    out_sums, new_sums, totals = kernel_call(
        sums_kernel,
        "place_sums",
        (flat(slots), flat(share), flat(share)),
        [SMEM] + [VMEM] * 5,
        (HBM, VMEM, VMEM),
        cost=6 << 20,
        scratch_shapes=scratch,
    )(member, place, base_sums, got_c, got_d, part_totals)
    moved_sums = lax.all_to_all(out_sums, "shard", 0, 0, tiled=True)

    send_c, send_d = second("rows", 0, 1 << 33, row_c, row_d, back_a, back_b)
    back_c, back_d = swap(send_c, 1, members), swap(send_d, 0, members)
    out_rows = kernel_call(
        rows_kernel, "place_rows", flat(slots), [VMEM] * 8, HBM, cost=6 << 20, scratch_shapes=scratch
    )(place, mine_rows, stay_a, stay_b, back_c, back_d, totals, new_sums)
    moved_rows = lax.all_to_all(out_rows, "shard", 0, 0, tiled=True)

    final_sums, parity_sums = parity_of("sums", (code_weight, member), moved_sums, members)
    moved_rows, final_sums, parity_sums = lax.optimization_barrier((moved_rows, final_sums, parity_sums))
    final_rows, parity_rows = parity_relayed("rows", (code_weight, member), moved_rows, members)
    return (final_rows, final_sums, parity_rows, parity_sums)


def solution(mesh):
    in_specs = (
        P(("shard", "code"), None),
        P(("shard", "code"), None),
        P("shard"),
        P(),
        P(("shard", "code"), None),
        P(("shard", "code")),
        P(("shard", "code"), None),
    )
    out_specs = (
        P(("shard", "code"), None),
        P(("shard", "code"), None),
        P(("shard", "code"), None),
        P(("shard", "code"), None),
    )
    return jax.shard_map(
        per_device, mesh=mesh, in_specs=in_specs, out_specs=out_specs, check_vma=False
    )
```

```python
import jax
import jax.numpy as jnp
from jax import lax
from jax.experimental import pallas as pl
from jax.experimental.pallas import tpu as pltpu
from jax.sharding import PartitionSpec as P

step_size = 0.5
epsilon = 1e-08
MEMBERS = 4
SLOT = 32
SMEM = pl.BlockSpec(memory_space=pltpu.SMEM)
VMEM = pl.BlockSpec(memory_space=pltpu.VMEM)
HBM = pl.BlockSpec(memory_space=pltpu.HBM)
PARAMS = pltpu.CompilerParams(vmem_limit_bytes=16 * 1024 * 1024)


def decode_weights(lost_ref, weight_ref):
    which = lost_ref[0]
    rows = [jnp.full((1, 128), weight_ref[c], jnp.float32) for c in range(MEMBERS)]
    parity_lost = which == 3
    divisor = jnp.where(which == 0, rows[0], jnp.where(which == 1, rows[1], rows[2]))
    divisor = jnp.where(parity_lost, jnp.ones_like(divisor), divisor)
    out = []
    for c in range(3):
        solved = jnp.where(parity_lost, rows[c], -rows[c] / divisor)
        out.append(jnp.where(which == c, jnp.zeros_like(solved), solved))
    out.append(jnp.where(parity_lost, jnp.zeros_like(divisor), 1.0 / divisor))
    return out


def split_halves(value):
    high = value.astype(jnp.bfloat16)
    low = (value - high.astype(jnp.float32)).astype(jnp.bfloat16)
    return high, low


def own_row(weights, member):
    own = weights[3]
    for c in range(3):
        own = jnp.where(member == c, weights[c], own)
    return own


def kernel_call(body, name, out_shape, in_specs, out_specs, cost=0, **kwargs):
    return pl.pallas_call(
        body,
        in_specs=in_specs,
        out_specs=out_specs,
        out_shape=out_shape,
        compiler_params=PARAMS,
        cost_estimate=pl.CostEstimate(flops=cost, bytes_accessed=cost, transcendentals=0),
        name=name,
        **kwargs,
    )


def flat(rows):
    return jax.ShapeDtypeStruct((rows, 128), jnp.float32)


def near(member):
    return member + 1 - 2 * lax.rem(member, 2), 3 - member


def scaled_pieces(table_ref, own, where, outs, buf_ref, sem_ref, others=()):
    half = buf_ref.shape[1]
    copies = []
    for i, (quarter, part) in enumerate(where):
        rows = pl.ds(pl.multiple_of(quarter * (2 * half) + part * half, 8), half)
        copies.append(pltpu.make_async_copy(table_ref.at[rows, :], buf_ref.at[i], sem_ref.at[i]))
        copies[-1].start()
    for copy in others:
        copy.start()
    own = own()
    for i, (out_ref, start) in enumerate(outs):
        copies[i].wait()
        out_ref[start : start + half, :] = own * buf_ref[i]
    for copy in others:
        copy.wait()


def passed_pieces(member):
    one, two = near(member)
    return [(3 - one, 0), (near(two)[0], 1)]


def given_pieces(member):
    one, two = near(member)
    return [(one, 0), (two, 1)]


def kept_pieces(member):
    one, two = near(member)
    return [(two, 0), (one, 1), (member, 0), (member, 1)]


def front_kernel(
    lost_ref, weight_hbm, member_ref, table_ref, grads_ref, ids_hbm, a_ref, b_ref,
    buf_ref, sem_ref, grad_sem, ids_ref, weight_ref, small_sem
):
    member = member_ref[0]
    part, lines = grads_ref.shape[0] // 2, ids_ref.shape[0] // 2
    half = buf_ref.shape[1]
    copies = [pltpu.make_async_copy(ids_hbm, ids_ref, small_sem.at[0])]
    for i, out_ref in enumerate((a_ref, b_ref)):
        for h in range(2):
            start = half + h * (part + 8)
            source = grads_ref.at[pl.ds(h * part, part), :]
            copies.append(pltpu.make_async_copy(source, out_ref.at[pl.ds(start, part), :], grad_sem.at[2 * i + h]))
    weights = pltpu.make_async_copy(weight_hbm, weight_ref, small_sem.at[1])
    weights.start()

    def own():
        weights.wait()
        return own_row(decode_weights(lost_ref, weight_ref), member)

    scaled_pieces(table_ref, own, passed_pieces(member), [(a_ref, 0), (b_ref, 0)], buf_ref, sem_ref, copies)
    ids = ids_ref[...].astype(jnp.float32)
    for out_ref in (a_ref, b_ref):
        for h in range(2):
            start = half + h * (part + 8) + part
            out_ref[start : start + lines, :] = ids[h * lines : (h + 1) * lines, :]
            out_ref[start + lines : start + 8, :] = jnp.zeros((8 - lines, 128), jnp.float32)


def keep_kernel(
    lost_ref, weight_ref, member_ref, table_ref, a_ref, b_ref, c_ref, d_ref, mine_ref, buf_ref, sem_ref
):
    member = member_ref[0]
    own = lambda: own_row(decode_weights(lost_ref, weight_ref), member)
    half = buf_ref.shape[1]
    outs = [(a_ref, 0), (b_ref, 0), (c_ref, 0), (d_ref, 0), (mine_ref, 0), (mine_ref, half)]
    scaled_pieces(table_ref, own, given_pieces(member) + kept_pieces(member), outs, buf_ref, sem_ref)


def both_kernel(
    lost_ref, weight_ref, member_ref, table_ref, a_ref, b_ref, give_a_ref, give_b_ref, c_ref, d_ref, mine_ref, buf_ref, sem_ref
):
    member = member_ref[0]
    own = lambda: own_row(decode_weights(lost_ref, weight_ref), member)
    half = buf_ref.shape[1]
    outs = [(ref, 0) for ref in (a_ref, b_ref, give_a_ref, give_b_ref, c_ref, d_ref, mine_ref)] + [(mine_ref, half)]
    where = passed_pieces(member) + given_pieces(member) + kept_pieces(member)
    scaled_pieces(table_ref, own, where, outs, buf_ref, sem_ref)


def second_kernel(c_ref, d_ref, a_ref, b_ref, out_c_ref, out_d_ref):
    half = c_ref.shape[0]
    out_c_ref[:half, :] = c_ref[...] + a_ref[:half, :]
    out_d_ref[:half, :] = d_ref[...] + b_ref[:half, :]
    extra = out_c_ref.shape[0] - half
    if extra:
        out_c_ref[half:, :] = a_ref[half : half + extra, :]
        out_d_ref[half:, :] = b_ref[half + extra :, :]


def swap(array, which, members):
    pairs = [(i, i ^ 1) for i in range(members)] if which == 0 else [(i, 3 - i) for i in range(members)]
    return lax.ppermute(array, "code", pairs)


def finish(mine_ref, a_ref, b_ref, c_ref, d_ref):
    half = mine_ref.shape[0] // 2
    first = (mine_ref[:half, :] + a_ref[a_ref.shape[0] - half :, :]) + c_ref[:half, :]
    last = (mine_ref[half:, :] + b_ref[b_ref.shape[0] - half :, :]) + d_ref[:half, :]
    return jnp.concatenate([first, last], axis=0)


def add_hits(total, first, part_ref, start, entries):
    high, low = split_halves(part_ref[start : start + entries, :])
    both = jnp.concatenate([high, low], axis=1)
    targets = (lax.broadcasted_iota(jnp.int32, (total.shape[0], 128), 0) + first).astype(jnp.float32)
    lines = [part_ref[start + entries + j : start + entries + j + 1, :] for j in range(entries // 128)]
    hits = [jnp.where(targets == line, 1.0, 0.0).astype(jnp.bfloat16) for line in lines]
    return total + jnp.dot(jnp.concatenate(hits, axis=1), both, preferred_element_type=jnp.float32)


def totals_kernel(member_ref, own_ref, a_ref, b_ref, mine_ref, kept_a_ref, kept_b_ref, out_ref, base_ref):
    count = out_ref.shape[0]
    half = count // 2
    size = (own_ref.shape[0] - half) // 2
    total = jnp.zeros((count, 256), jnp.float32)
    for ref in (own_ref, a_ref, b_ref):
        for h in range(2):
            total = add_hits(total, member_ref[0] * count, ref, half + h * size, size - 8)
    out_ref[...] = total[:, :128] + total[:, 128:]
    base_ref[:half, :] = mine_ref[:half, :] + kept_a_ref[...]
    base_ref[half:, :] = mine_ref[half:, :] + kept_b_ref[...]


def spread(place_ref, values, out_ref, both_ref, stage_ref, sem_ref):
    high, low = split_halves(values)
    both_ref[:, :128] = high
    both_ref[:, 128:] = low
    slots, rows = out_ref.shape[0], values.shape[0]
    step = slots // sem_ref.shape[0]
    place = place_ref[...]
    copies = []
    for i in range(sem_ref.shape[0]):
        here = lax.broadcasted_iota(jnp.int32, (step, rows), 0) + i * step
        pick = jnp.where(here == place, 1.0, 0.0).astype(jnp.bfloat16)
        got = jnp.dot(pick, both_ref[...], preferred_element_type=jnp.float32)
        block = pl.ds(i * step, step)
        stage_ref[block, :] = got[:, :128] + got[:, 128:]
        copies.append(pltpu.make_async_copy(stage_ref.at[block, :], out_ref.at[block, :], sem_ref.at[i]))
        copies[-1].start()
    for copy in copies:
        copy.wait()


def sums_kernel(
    member_ref, place_ref, base_ref, c_ref, d_ref, part_ref, out_ref, new_ref, total_ref, both_ref, stage_ref, sem_ref
):
    count = base_ref.shape[0]
    half = count // 2
    more = jnp.zeros((count, 256), jnp.float32)
    for ref in (c_ref, d_ref):
        more = add_hits(more, member_ref[0] * count, ref, half, ref.shape[0] - half - 8)
    total = part_ref[...] + (more[:, :128] + more[:, 128:])
    total_ref[...] = total
    new = base_ref[...] + jnp.concatenate([c_ref[:half, :], d_ref[:half, :]], axis=0) + total * total
    new_ref[...] = new
    spread(place_ref, new, out_ref, both_ref, stage_ref, sem_ref)


def rows_kernel(
    place_ref, mine_ref, a_ref, b_ref, c_ref, d_ref, total_ref, sums_ref, out_ref, both_ref, stage_ref, sem_ref
):
    mine = finish(mine_ref, a_ref, b_ref, c_ref, d_ref)
    new = mine - step_size * total_ref[...] / (jnp.sqrt(sums_ref[...]) + epsilon)
    spread(place_ref, new, out_ref, both_ref, stage_ref, sem_ref)


def own_code_weight(weight_ref, member):
    own = weight_ref[3]
    for c in range(3):
        own = jnp.where(member == c, weight_ref[c], own)
    return own


def copy_kernel(moved_ref, out_ref):
    out_ref[...] = moved_ref[...]


def quarter_of(which, count):
    return pl.ds(pl.multiple_of(lax.rem(which, MEMBERS) * count, 8), count)


def parity_send_kernel(weight_ref, member_ref, moved_ref, mine_ref, *out_refs):
    member = member_ref[0]
    own = own_code_weight(weight_ref, member)
    count = mine_ref.shape[0]
    for k, out_ref in enumerate(out_refs):
        out_ref[...] = own * moved_ref[quarter_of(member + k + 1, count), :]
    mine_ref[...] = own * moved_ref[quarter_of(member, count), :]


def other_core_kernel(shard_ref, got_ref, out_ref):
    core = lax.rem(shard_ref[0], 2)
    for i in range(out_ref.shape[0] // SLOT):
        start = pl.multiple_of((2 * i + 1 - core) * SLOT, 8)
        out_ref[i * SLOT : (i + 1) * SLOT, :] = got_ref[pl.ds(start, SLOT), :]


def emit_kernel(weight_ref, member_ref, shard_ref, got_ref, side_ref, out_ref, mine_ref, *send_refs):
    core = lax.rem(shard_ref[0], 2)
    for i in range(side_ref.shape[0] // SLOT):
        start = pl.multiple_of((2 * i + core) * SLOT, 8)
        out_ref[pl.ds(start, SLOT), :] = got_ref[pl.ds(start, SLOT), :]
        start = pl.multiple_of((2 * i + 1 - core) * SLOT, 8)
        out_ref[pl.ds(start, SLOT), :] = side_ref[i * SLOT : (i + 1) * SLOT, :]
    parity_send_kernel(weight_ref, member_ref, out_ref, mine_ref, *send_refs)


def parity_sum_kernel(mine_ref, a_ref, b_ref, c_ref, out_ref):
    out_ref[...] = (mine_ref[...] + a_ref[...]) + (b_ref[...] + c_ref[...])


def parity_first_kernel(weight_ref, member_ref, moved_ref, *refs):
    member = member_ref[0]
    own = own_code_weight(weight_ref, member)
    half = refs[0].shape[0]
    outs = [(ref, 0) for ref in refs] + [(refs[-1], half)]
    where = passed_pieces(member) + given_pieces(member) + kept_pieces(member)
    for (out_ref, start), (quarter, part) in zip(outs, where):
        rows = pl.ds(pl.multiple_of(quarter * (2 * half) + part * half, 8), half)
        out_ref[start : start + half, :] = own * moved_ref[rows, :]


def parity_last_kernel(mine_ref, a_ref, b_ref, c_ref, d_ref, out_ref):
    out_ref[...] = finish(mine_ref, a_ref, b_ref, c_ref, d_ref)


def turn(array, k, members):
    return lax.ppermute(array, "code", [(i, (i + k) % members) for i in range(members)])


def second(name, extra, hint, *args):
    half = args[0].shape[0]
    return kernel_call(
        second_kernel,
        "second_" + name,
        (flat(half + extra), flat(half + extra)),
        [VMEM] * 4,
        (VMEM, VMEM),
        cost=hint,
    )(*args)


def parity_relayed(name, key, moved, members):
    slots = moved.shape[0]
    quarter = slots // members
    half = quarter // 2
    a, b, give_a, give_b, keep_c, keep_d, mine = kernel_call(
        parity_first_kernel,
        "parity_first_" + name,
        (flat(half),) * 6 + (flat(quarter),),
        [SMEM, SMEM, VMEM],
        (VMEM,) * 7,
        cost=2 << 20,
    )(*key, moved)
    back_a, back_b = swap(a, 0, members), swap(b, 1, members)
    stay_a, stay_b = swap(give_a, 0, members), swap(give_b, 1, members)
    send_c, send_d = second("parity_" + name, 0, 1 << 33, keep_c, keep_d, back_a, back_b)
    back_c, back_d = swap(send_c, 1, members), swap(send_d, 0, members)
    out = kernel_call(copy_kernel, "emit_" + name, flat(slots), [VMEM], VMEM, cost=2 << 20)(moved)
    parity = kernel_call(
        parity_last_kernel, "parity_last_" + name, flat(quarter), [VMEM] * 5, VMEM, cost=1 << 20
    )(mine, stay_a, stay_b, back_c, back_d)
    return out, parity


def parity_direct(name, key, shard, got, shards, members):
    slots = got.shape[0]
    quarter = slots // members
    side = kernel_call(
        other_core_kernel, "other_core_" + name, flat(slots // 2), [SMEM, VMEM], VMEM, cost=1 << 20
    )(shard, got)
    side = lax.ppermute(side, "shard", [(i, i ^ 1) for i in range(shards)])
    out, mine, *sends = kernel_call(
        emit_kernel,
        "emit_" + name,
        (flat(slots),) + (flat(quarter),) * members,
        [SMEM, SMEM, SMEM, VMEM, VMEM],
        (VMEM,) * (members + 1),
        cost=3 << 20,
    )(*key, shard, got, side)
    gots = {k: turn(sends[k - 1], k, members) for k in (2, 1, 3)}
    parity = kernel_call(
        parity_sum_kernel, "parity_sum_" + name, flat(quarter), [VMEM] * members, VMEM, cost=1 << 20
    )(mine, gots[1], gots[2], gots[3])
    return out, parity


def per_device(
    table_rows, adagrad_sums, lost_member, code_weight, new_owner, pending_rows, pending_grads
):
    members = lax.axis_size("code")
    shards = lax.axis_size("shard")
    member = lax.axis_index("code").astype(jnp.int32)[None]
    share = table_rows.shape[0] // members
    capacity = max(2, (2 * share + shards - 1) // shards)
    slots = shards * capacity
    half = share // 2
    entries = pending_grads.shape[0]
    scalars = [SMEM, SMEM, SMEM]
    key = (lost_member, pltpu.with_memory_space_constraint(code_weight, pltpu.HBM), member)
    owner = new_owner[:, 0]

    def buffers(count):
        return [pltpu.VMEM((count, half, 128), jnp.float32), pltpu.SemaphoreType.DMA((count,))]

    def keep_out(array):
        return pltpu.with_memory_space_constraint(array, pltpu.HBM)

    part = entries // 2 + 8
    send_a, send_b = kernel_call(
        front_kernel,
        "front_send",
        (flat(half + 2 * part), flat(half + 2 * part)),
        [SMEM, HBM, SMEM, HBM, HBM, HBM],
        (VMEM, VMEM),
        cost=3 << 20,
        scratch_shapes=buffers(2)
        + [pltpu.SemaphoreType.DMA((4,)), pltpu.VMEM((entries // 128, 128), jnp.int32)]
        + [pltpu.SMEM((members,), jnp.float32), pltpu.SemaphoreType.DMA((2,))],
    )(*key, keep_out(adagrad_sums), keep_out(pending_grads), keep_out(pending_rows.reshape(-1, 128)))
    got_a, got_b = swap(send_a, 0, members), swap(send_b, 1, members)

    give_a, give_b, keep_c, keep_d, mine_sums = kernel_call(
        keep_kernel,
        "keep_sums",
        (flat(half), flat(half), flat(half), flat(half), flat(share)),
        scalars + [HBM],
        (VMEM,) * 5,
        cost=3 << 20,
        scratch_shapes=buffers(6),
    )(*key, keep_out(adagrad_sums))
    row_a, row_b, row_give_a, row_give_b, row_c, row_d, mine_rows = kernel_call(
        both_kernel,
        "weigh_rows",
        (flat(half),) * 6 + (flat(share),),
        scalars + [HBM],
        (VMEM,) * 7,
        cost=4 << 20,
        scratch_shapes=buffers(8),
    )(*key, keep_out(table_rows))
    give_a, give_b, row_a, row_b = lax.optimization_barrier((give_a, give_b, row_a, row_b))
    kept_a, kept_b = swap(give_a, 0, members), swap(give_b, 1, members)
    earlier = jnp.tril(owner[:, None] == owner[None, :], -1)
    rank = jnp.sum(earlier.astype(jnp.int32), axis=1)
    place = (owner * capacity + rank)[None, :]

    send_c, send_d = second("sums", part, 1 << 38, keep_c, keep_d, got_a, got_b)
    got_c, got_d = swap(send_c, 1, members), swap(send_d, 0, members)
    kept_a, kept_b, got_a, got_b = lax.optimization_barrier((kept_a, kept_b, got_a, got_b))
    part_totals, base_sums = kernel_call(
        totals_kernel, "pending_totals", (flat(share), flat(share)), [SMEM] + [VMEM] * 6, (VMEM, VMEM), cost=4 << 20
    )(member, send_a, got_a, got_b, mine_sums, kept_a, kept_b)
    row_a, row_b, row_give_a, row_give_b, got_c, got_d, part_totals, place = lax.optimization_barrier(
        (row_a, row_b, row_give_a, row_give_b, got_c, got_d, part_totals, place)
    )
    back_a, back_b = swap(row_a, 0, members), swap(row_b, 1, members)
    stay_a, stay_b = swap(row_give_a, 0, members), swap(row_give_b, 1, members)

    scratch = [
        pltpu.VMEM((share, 256), jnp.bfloat16),
        pltpu.VMEM((slots, 128), jnp.float32),
        pltpu.SemaphoreType.DMA((8,)),
    ]
    out_sums, new_sums, totals = kernel_call(
        sums_kernel,
        "place_sums",
        (flat(slots), flat(share), flat(share)),
        [SMEM] + [VMEM] * 5,
        (HBM, VMEM, VMEM),
        cost=6 << 20,
        scratch_shapes=scratch,
    )(member, place, base_sums, got_c, got_d, part_totals)
    same_core = [list(range(core, shards, 2)) for core in range(2)]
    got_sums = lax.all_to_all(out_sums, "shard", 0, 0, tiled=True, axis_index_groups=same_core)

    send_c, send_d = second("rows", 0, 1 << 33, row_c, row_d, back_a, back_b)
    back_c, back_d = swap(send_c, 1, members), swap(send_d, 0, members)
    out_rows = kernel_call(
        rows_kernel, "place_rows", flat(slots), [VMEM] * 8, HBM, cost=6 << 20, scratch_shapes=scratch
    )(place, mine_rows, stay_a, stay_b, back_c, back_d, totals, new_sums)
    moved_rows = lax.all_to_all(out_rows, "shard", 0, 0, tiled=True)

    shard = lax.axis_index("shard").astype(jnp.int32)[None]
    final_sums, parity_sums = parity_direct("sums", (code_weight, member), shard, got_sums, shards, members)
    moved_rows, final_sums, parity_sums = lax.optimization_barrier((moved_rows, final_sums, parity_sums))
    final_rows, parity_rows = parity_relayed("rows", (code_weight, member), moved_rows, members)
    return (final_rows, final_sums, parity_rows, parity_sums)


def solution(mesh):
    in_specs = (
        P(("shard", "code"), None),
        P(("shard", "code"), None),
        P("shard"),
        P(),
        P(("shard", "code"), None),
        P(("shard", "code")),
        P(("shard", "code"), None),
    )
    out_specs = (
        P(("shard", "code"), None),
        P(("shard", "code"), None),
        P(("shard", "code"), None),
        P(("shard", "code"), None),
    )
    return jax.shard_map(
        per_device, mesh=mesh, in_specs=in_specs, out_specs=out_specs, check_vma=False
    )
```

```python
import jax
import jax.numpy as jnp
from jax import lax
from jax.experimental import pallas as pl
from jax.experimental.pallas import tpu as pltpu
from jax.sharding import PartitionSpec as P

step_size = 0.5
epsilon = 1e-08
MEMBERS = 4
SLOT = 32
SMEM = pl.BlockSpec(memory_space=pltpu.SMEM)
VMEM = pl.BlockSpec(memory_space=pltpu.VMEM)
HBM = pl.BlockSpec(memory_space=pltpu.HBM)
PARAMS = pltpu.CompilerParams(vmem_limit_bytes=16 * 1024 * 1024)


def decode_weights(lost_ref, weight_ref):
    which = lost_ref[0]
    rows = [jnp.full((1, 128), weight_ref[c], jnp.float32) for c in range(MEMBERS)]
    parity_lost = which == 3
    divisor = jnp.where(which == 0, rows[0], jnp.where(which == 1, rows[1], rows[2]))
    divisor = jnp.where(parity_lost, jnp.ones_like(divisor), divisor)
    out = []
    for c in range(3):
        solved = jnp.where(parity_lost, rows[c], -rows[c] / divisor)
        out.append(jnp.where(which == c, jnp.zeros_like(solved), solved))
    out.append(jnp.where(parity_lost, jnp.zeros_like(divisor), 1.0 / divisor))
    return out


def split_halves(value):
    high = value.astype(jnp.bfloat16)
    low = (value - high.astype(jnp.float32)).astype(jnp.bfloat16)
    return high, low


def own_row(weights, member):
    own = weights[3]
    for c in range(3):
        own = jnp.where(member == c, weights[c], own)
    return own


def kernel_call(body, name, out_shape, in_specs, out_specs, cost=0, **kwargs):
    return pl.pallas_call(
        body,
        in_specs=in_specs,
        out_specs=out_specs,
        out_shape=out_shape,
        compiler_params=PARAMS,
        cost_estimate=pl.CostEstimate(flops=cost, bytes_accessed=cost, transcendentals=0),
        name=name,
        **kwargs,
    )


def flat(rows):
    return jax.ShapeDtypeStruct((rows, 128), jnp.float32)


def near(member):
    return member + 1 - 2 * lax.rem(member, 2), 3 - member


def scaled_pieces(table_ref, own, where, outs, buf_ref, sem_ref, others=()):
    half = buf_ref.shape[1]
    copies = []
    for i, (quarter, part) in enumerate(where):
        rows = pl.ds(pl.multiple_of(quarter * (2 * half) + part * half, 8), half)
        copies.append(pltpu.make_async_copy(table_ref.at[rows, :], buf_ref.at[i], sem_ref.at[i]))
        copies[-1].start()
    for copy in others:
        copy.start()
    own = own()
    for i, (out_ref, start) in enumerate(outs):
        copies[i].wait()
        out_ref[start : start + half, :] = own * buf_ref[i]
    for copy in others:
        copy.wait()


def passed_pieces(member):
    one, two = near(member)
    return [(3 - one, 0), (near(two)[0], 1)]


def given_pieces(member):
    one, two = near(member)
    return [(one, 0), (two, 1)]


def kept_pieces(member):
    one, two = near(member)
    return [(two, 0), (one, 1), (member, 0), (member, 1)]


def front_kernel(
    lost_ref, weight_hbm, member_ref, table_ref, grads_ref, ids_hbm, a_ref, b_ref,
    buf_ref, sem_ref, grad_sem, ids_ref, weight_ref, small_sem
):
    member = member_ref[0]
    part, lines = grads_ref.shape[0] // 2, ids_ref.shape[0] // 2
    half = buf_ref.shape[1]
    copies = [pltpu.make_async_copy(ids_hbm, ids_ref, small_sem.at[0])]
    for i, out_ref in enumerate((a_ref, b_ref)):
        for h in range(2):
            start = half + h * (part + 8)
            source = grads_ref.at[pl.ds(h * part, part), :]
            copies.append(pltpu.make_async_copy(source, out_ref.at[pl.ds(start, part), :], grad_sem.at[2 * i + h]))
    weights = pltpu.make_async_copy(weight_hbm, weight_ref, small_sem.at[1])
    weights.start()

    def own():
        weights.wait()
        return own_row(decode_weights(lost_ref, weight_ref), member)

    scaled_pieces(table_ref, own, passed_pieces(member), [(a_ref, 0), (b_ref, 0)], buf_ref, sem_ref, copies)
    ids = ids_ref[...].astype(jnp.float32)
    for out_ref in (a_ref, b_ref):
        for h in range(2):
            start = half + h * (part + 8) + part
            out_ref[start : start + lines, :] = ids[h * lines : (h + 1) * lines, :]
            out_ref[start + lines : start + 8, :] = jnp.zeros((8 - lines, 128), jnp.float32)


def keep_kernel(
    lost_ref, weight_ref, member_ref, table_ref, a_ref, b_ref, c_ref, d_ref, mine_ref, buf_ref, sem_ref
):
    member = member_ref[0]
    own = lambda: own_row(decode_weights(lost_ref, weight_ref), member)
    half = buf_ref.shape[1]
    outs = [(a_ref, 0), (b_ref, 0), (c_ref, 0), (d_ref, 0), (mine_ref, 0), (mine_ref, half)]
    scaled_pieces(table_ref, own, given_pieces(member) + kept_pieces(member), outs, buf_ref, sem_ref)


def send_kernel(lost_ref, weight_ref, member_ref, table_ref, a_ref, b_ref, give_a_ref, give_b_ref, buf_ref, sem_ref):
    member = member_ref[0]
    own = lambda: own_row(decode_weights(lost_ref, weight_ref), member)
    outs = [(ref, 0) for ref in (a_ref, b_ref, give_a_ref, give_b_ref)]
    scaled_pieces(table_ref, own, passed_pieces(member) + given_pieces(member), outs, buf_ref, sem_ref)


def stay_kernel(lost_ref, weight_ref, member_ref, table_ref, c_ref, d_ref, mine_ref, buf_ref, sem_ref):
    member = member_ref[0]
    own = lambda: own_row(decode_weights(lost_ref, weight_ref), member)
    half = buf_ref.shape[1]
    outs = [(c_ref, 0), (d_ref, 0), (mine_ref, 0), (mine_ref, half)]
    scaled_pieces(table_ref, own, kept_pieces(member), outs, buf_ref, sem_ref)


def second_kernel(c_ref, d_ref, a_ref, b_ref, out_c_ref, out_d_ref):
    half = c_ref.shape[0]
    out_c_ref[:half, :] = c_ref[...] + a_ref[:half, :]
    out_d_ref[:half, :] = d_ref[...] + b_ref[:half, :]
    extra = out_c_ref.shape[0] - half
    if extra:
        out_c_ref[half:, :] = a_ref[half : half + extra, :]
        out_d_ref[half:, :] = b_ref[half + extra :, :]


def swap(array, which, members):
    pairs = [(i, i ^ 1) for i in range(members)] if which == 0 else [(i, 3 - i) for i in range(members)]
    return lax.ppermute(array, "code", pairs)


def finish(mine_ref, a_ref, b_ref, c_ref, d_ref):
    half = mine_ref.shape[0] // 2
    first = (mine_ref[:half, :] + a_ref[a_ref.shape[0] - half :, :]) + c_ref[:half, :]
    last = (mine_ref[half:, :] + b_ref[b_ref.shape[0] - half :, :]) + d_ref[:half, :]
    return jnp.concatenate([first, last], axis=0)


def add_hits(total, first, part_ref, start, entries):
    high, low = split_halves(part_ref[start : start + entries, :])
    both = jnp.concatenate([high, low], axis=1)
    targets = (lax.broadcasted_iota(jnp.int32, (total.shape[0], 128), 0) + first).astype(jnp.float32)
    lines = [part_ref[start + entries + j : start + entries + j + 1, :] for j in range(entries // 128)]
    hits = [jnp.where(targets == line, 1.0, 0.0).astype(jnp.bfloat16) for line in lines]
    return total + jnp.dot(jnp.concatenate(hits, axis=1), both, preferred_element_type=jnp.float32)


def totals_kernel(member_ref, own_ref, a_ref, b_ref, mine_ref, kept_a_ref, kept_b_ref, out_ref, base_ref):
    count = out_ref.shape[0]
    half = count // 2
    size = (own_ref.shape[0] - half) // 2
    total = jnp.zeros((count, 256), jnp.float32)
    for ref in (own_ref, a_ref, b_ref):
        for h in range(2):
            total = add_hits(total, member_ref[0] * count, ref, half + h * size, size - 8)
    out_ref[...] = total[:, :128] + total[:, 128:]
    base_ref[:half, :] = mine_ref[:half, :] + kept_a_ref[...]
    base_ref[half:, :] = mine_ref[half:, :] + kept_b_ref[...]


def spread(place_ref, values, out_ref, both_ref, stage_ref, sem_ref):
    high, low = split_halves(values)
    both_ref[:, :128] = high
    both_ref[:, 128:] = low
    slots, rows = out_ref.shape[0], values.shape[0]
    step = slots // sem_ref.shape[0]
    place = place_ref[...]
    copies = []
    for i in range(sem_ref.shape[0]):
        here = lax.broadcasted_iota(jnp.int32, (step, rows), 0) + i * step
        pick = jnp.where(here == place, 1.0, 0.0).astype(jnp.bfloat16)
        got = jnp.dot(pick, both_ref[...], preferred_element_type=jnp.float32)
        block = pl.ds(i * step, step)
        stage_ref[block, :] = got[:, :128] + got[:, 128:]
        copies.append(pltpu.make_async_copy(stage_ref.at[block, :], out_ref.at[block, :], sem_ref.at[i]))
        copies[-1].start()
    for copy in copies:
        copy.wait()


def sums_kernel(
    member_ref, place_ref, base_ref, c_ref, d_ref, part_ref, out_ref, new_ref, total_ref, both_ref, stage_ref, sem_ref
):
    count = base_ref.shape[0]
    half = count // 2
    more = jnp.zeros((count, 256), jnp.float32)
    for ref in (c_ref, d_ref):
        more = add_hits(more, member_ref[0] * count, ref, half, ref.shape[0] - half - 8)
    total = part_ref[...] + (more[:, :128] + more[:, 128:])
    total_ref[...] = total
    new = base_ref[...] + jnp.concatenate([c_ref[:half, :], d_ref[:half, :]], axis=0) + total * total
    new_ref[...] = new
    spread(place_ref, new, out_ref, both_ref, stage_ref, sem_ref)


def rows_kernel(
    place_ref, mine_ref, a_ref, b_ref, c_ref, d_ref, total_ref, sums_ref, out_ref, both_ref, stage_ref, sem_ref
):
    mine = finish(mine_ref, a_ref, b_ref, c_ref, d_ref)
    new = mine - step_size * total_ref[...] / (jnp.sqrt(sums_ref[...]) + epsilon)
    spread(place_ref, new, out_ref, both_ref, stage_ref, sem_ref)


def own_code_weight(weight_ref, member):
    own = weight_ref[3]
    for c in range(3):
        own = jnp.where(member == c, weight_ref[c], own)
    return own


def copy_kernel(moved_ref, out_ref):
    out_ref[...] = moved_ref[...]


def quarter_of(which, count):
    return pl.ds(pl.multiple_of(lax.rem(which, MEMBERS) * count, 8), count)


def parity_send_kernel(weight_ref, member_ref, moved_ref, mine_ref, *out_refs):
    member = member_ref[0]
    own = own_code_weight(weight_ref, member)
    count = mine_ref.shape[0]
    for k, out_ref in enumerate(out_refs):
        out_ref[...] = own * moved_ref[quarter_of(member + k + 1, count), :]
    mine_ref[...] = own * moved_ref[quarter_of(member, count), :]


def other_core_kernel(shard_ref, got_ref, out_ref):
    core = lax.rem(shard_ref[0], 2)
    for i in range(out_ref.shape[0] // SLOT):
        start = pl.multiple_of((2 * i + 1 - core) * SLOT, 8)
        out_ref[i * SLOT : (i + 1) * SLOT, :] = got_ref[pl.ds(start, SLOT), :]


def emit_kernel(weight_ref, member_ref, shard_ref, got_ref, side_ref, out_ref, mine_ref, *send_refs):
    core = lax.rem(shard_ref[0], 2)
    for i in range(side_ref.shape[0] // SLOT):
        start = pl.multiple_of((2 * i + core) * SLOT, 8)
        out_ref[pl.ds(start, SLOT), :] = got_ref[pl.ds(start, SLOT), :]
        start = pl.multiple_of((2 * i + 1 - core) * SLOT, 8)
        out_ref[pl.ds(start, SLOT), :] = side_ref[i * SLOT : (i + 1) * SLOT, :]
    parity_send_kernel(weight_ref, member_ref, out_ref, mine_ref, *send_refs)


def parity_sum_kernel(mine_ref, a_ref, b_ref, c_ref, out_ref):
    out_ref[...] = (mine_ref[...] + a_ref[...]) + (b_ref[...] + c_ref[...])


def parity_first_kernel(weight_ref, member_ref, moved_ref, *refs):
    member = member_ref[0]
    own = own_code_weight(weight_ref, member)
    half = refs[0].shape[0]
    outs = [(ref, 0) for ref in refs] + [(refs[-1], half)]
    where = passed_pieces(member) + given_pieces(member) + kept_pieces(member)
    for (out_ref, start), (quarter, part) in zip(outs, where):
        rows = pl.ds(pl.multiple_of(quarter * (2 * half) + part * half, 8), half)
        out_ref[start : start + half, :] = own * moved_ref[rows, :]


def parity_last_kernel(mine_ref, a_ref, b_ref, c_ref, d_ref, out_ref):
    out_ref[...] = finish(mine_ref, a_ref, b_ref, c_ref, d_ref)


def turn(array, k, members):
    return lax.ppermute(array, "code", [(i, (i + k) % members) for i in range(members)])


def second(name, extra, hint, *args):
    half = args[0].shape[0]
    return kernel_call(
        second_kernel,
        "second_" + name,
        (flat(half + extra), flat(half + extra)),
        [VMEM] * 4,
        (VMEM, VMEM),
        cost=hint,
    )(*args)


def parity_relayed(name, key, moved, members):
    slots = moved.shape[0]
    quarter = slots // members
    half = quarter // 2
    a, b, give_a, give_b, keep_c, keep_d, mine = kernel_call(
        parity_first_kernel,
        "parity_first_" + name,
        (flat(half),) * 6 + (flat(quarter),),
        [SMEM, SMEM, VMEM],
        (VMEM,) * 7,
        cost=2 << 20,
    )(*key, moved)
    back_a, back_b = swap(a, 0, members), swap(b, 1, members)
    stay_a, stay_b = swap(give_a, 0, members), swap(give_b, 1, members)
    send_c, send_d = second("parity_" + name, 0, 1 << 33, keep_c, keep_d, back_a, back_b)
    back_c, back_d = swap(send_c, 1, members), swap(send_d, 0, members)
    out = kernel_call(copy_kernel, "emit_" + name, flat(slots), [VMEM], VMEM, cost=2 << 20)(moved)
    parity = kernel_call(
        parity_last_kernel, "parity_last_" + name, flat(quarter), [VMEM] * 5, VMEM, cost=1 << 20
    )(mine, stay_a, stay_b, back_c, back_d)
    return out, parity


def parity_direct(name, key, shard, got, shards, members):
    slots = got.shape[0]
    quarter = slots // members
    side = kernel_call(
        other_core_kernel, "other_core_" + name, flat(slots // 2), [SMEM, VMEM], VMEM, cost=1 << 20
    )(shard, got)
    side = lax.ppermute(side, "shard", [(i, i ^ 1) for i in range(shards)])
    out, mine, *sends = kernel_call(
        emit_kernel,
        "emit_" + name,
        (flat(slots),) + (flat(quarter),) * members,
        [SMEM, SMEM, SMEM, VMEM, VMEM],
        (VMEM,) * (members + 1),
        cost=3 << 20,
    )(*key, shard, got, side)
    gots = {k: turn(sends[k - 1], k, members) for k in (2, 1, 3)}
    parity = kernel_call(
        parity_sum_kernel, "parity_sum_" + name, flat(quarter), [VMEM] * members, VMEM, cost=1 << 20
    )(mine, gots[1], gots[2], gots[3])
    return out, parity


def per_device(
    table_rows, adagrad_sums, lost_member, code_weight, new_owner, pending_rows, pending_grads
):
    members = lax.axis_size("code")
    shards = lax.axis_size("shard")
    member = lax.axis_index("code").astype(jnp.int32)[None]
    share = table_rows.shape[0] // members
    capacity = max(2, (2 * share + shards - 1) // shards)
    slots = shards * capacity
    half = share // 2
    entries = pending_grads.shape[0]
    scalars = [SMEM, SMEM, SMEM]
    key = (lost_member, pltpu.with_memory_space_constraint(code_weight, pltpu.HBM), member)
    owner = new_owner[:, 0]

    def buffers(count):
        return [pltpu.VMEM((count, half, 128), jnp.float32), pltpu.SemaphoreType.DMA((count,))]

    def keep_out(array):
        return pltpu.with_memory_space_constraint(array, pltpu.HBM)

    part = entries // 2 + 8
    send_a, send_b = kernel_call(
        front_kernel,
        "front_send",
        (flat(half + 2 * part), flat(half + 2 * part)),
        [SMEM, HBM, SMEM, HBM, HBM, HBM],
        (VMEM, VMEM),
        cost=3 << 20,
        scratch_shapes=buffers(2)
        + [pltpu.SemaphoreType.DMA((4,)), pltpu.VMEM((entries // 128, 128), jnp.int32)]
        + [pltpu.SMEM((members,), jnp.float32), pltpu.SemaphoreType.DMA((2,))],
    )(*key, keep_out(adagrad_sums), keep_out(pending_grads), keep_out(pending_rows.reshape(-1, 128)))
    got_a, got_b = swap(send_a, 0, members), swap(send_b, 1, members)

    give_a, give_b, keep_c, keep_d, mine_sums = kernel_call(
        keep_kernel,
        "keep_sums",
        (flat(half), flat(half), flat(half), flat(half), flat(share)),
        scalars + [HBM],
        (VMEM,) * 5,
        cost=3 << 20,
        scratch_shapes=buffers(6),
    )(*key, keep_out(adagrad_sums))
    row_a, row_b, row_give_a, row_give_b = kernel_call(
        send_kernel,
        "send_rows",
        (flat(half),) * 4,
        scalars + [HBM],
        (VMEM,) * 4,
        cost=2 << 20,
        scratch_shapes=buffers(4),
    )(*key, keep_out(table_rows))
    give_a, give_b, row_a, row_b = lax.optimization_barrier((give_a, give_b, row_a, row_b))
    kept_a, kept_b = swap(give_a, 0, members), swap(give_b, 1, members)
    earlier = jnp.tril(owner[:, None] == owner[None, :], -1)
    rank = jnp.sum(earlier.astype(jnp.int32), axis=1)
    place = (owner * capacity + rank)[None, :]

    send_c, send_d = second("sums", part, 1 << 38, keep_c, keep_d, got_a, got_b)
    got_c, got_d = swap(send_c, 1, members), swap(send_d, 0, members)
    kept_a, kept_b, got_a, got_b = lax.optimization_barrier((kept_a, kept_b, got_a, got_b))
    part_totals, base_sums = kernel_call(
        totals_kernel, "pending_totals", (flat(share), flat(share)), [SMEM] + [VMEM] * 6, (VMEM, VMEM), cost=4 << 20
    )(member, send_a, got_a, got_b, mine_sums, kept_a, kept_b)
    row_a, row_b, row_give_a, row_give_b, got_c, got_d, part_totals, place, late_rows = lax.optimization_barrier(
        (row_a, row_b, row_give_a, row_give_b, got_c, got_d, part_totals, place, table_rows)
    )
    back_a, back_b = swap(row_a, 0, members), swap(row_b, 1, members)
    stay_a, stay_b = swap(row_give_a, 0, members), swap(row_give_b, 1, members)

    scratch = [
        pltpu.VMEM((share, 256), jnp.bfloat16),
        pltpu.VMEM((slots, 128), jnp.float32),
        pltpu.SemaphoreType.DMA((8,)),
    ]
    out_sums, new_sums, totals = kernel_call(
        sums_kernel,
        "place_sums",
        (flat(slots), flat(share), flat(share)),
        [SMEM] + [VMEM] * 5,
        (HBM, VMEM, VMEM),
        cost=6 << 20,
        scratch_shapes=scratch,
    )(member, place, base_sums, got_c, got_d, part_totals)
    same_core = [list(range(core, shards, 2)) for core in range(2)]
    got_sums = lax.all_to_all(out_sums, "shard", 0, 0, tiled=True, axis_index_groups=same_core)

    row_c, row_d, mine_rows = kernel_call(
        stay_kernel,
        "stay_rows",
        (flat(half), flat(half), flat(share)),
        scalars + [HBM],
        (VMEM,) * 3,
        cost=2 << 20,
        scratch_shapes=buffers(4),
    )(*key, keep_out(late_rows))
    send_c, send_d = second("rows", 0, 1 << 33, row_c, row_d, back_a, back_b)
    back_c, back_d = swap(send_c, 1, members), swap(send_d, 0, members)
    out_rows = kernel_call(
        rows_kernel, "place_rows", flat(slots), [VMEM] * 8, HBM, cost=6 << 20, scratch_shapes=scratch
    )(place, mine_rows, stay_a, stay_b, back_c, back_d, totals, new_sums)
    moved_rows = lax.all_to_all(out_rows, "shard", 0, 0, tiled=True)

    shard = lax.axis_index("shard").astype(jnp.int32)[None]
    final_sums, parity_sums = parity_direct("sums", (code_weight, member), shard, got_sums, shards, members)
    moved_rows, final_sums, parity_sums = lax.optimization_barrier((moved_rows, final_sums, parity_sums))
    final_rows, parity_rows = parity_relayed("rows", (code_weight, member), moved_rows, members)
    return (final_rows, final_sums, parity_rows, parity_sums)


def solution(mesh):
    in_specs = (
        P(("shard", "code"), None),
        P(("shard", "code"), None),
        P("shard"),
        P(),
        P(("shard", "code"), None),
        P(("shard", "code")),
        P(("shard", "code"), None),
    )
    out_specs = (
        P(("shard", "code"), None),
        P(("shard", "code"), None),
        P(("shard", "code"), None),
        P(("shard", "code"), None),
    )
    return jax.shard_map(
        per_device, mesh=mesh, in_specs=in_specs, out_specs=out_specs, check_vma=False
    )
```

```python
import jax
import jax.numpy as jnp
from jax import lax
from jax.experimental import pallas as pl
from jax.experimental.pallas import tpu as pltpu
from jax.sharding import PartitionSpec as P

step_size = 0.5
epsilon = 1e-08
MEMBERS = 4
TOP = float(jnp.finfo(jnp.bfloat16).max)
SLOT = 32
SMEM = pl.BlockSpec(memory_space=pltpu.SMEM)
VMEM = pl.BlockSpec(memory_space=pltpu.VMEM)
HBM = pl.BlockSpec(memory_space=pltpu.HBM)
PARAMS = pltpu.CompilerParams(vmem_limit_bytes=16 * 1024 * 1024)


def decode_weights(lost_ref, weight_ref):
    which = lost_ref[0]
    rows = [jnp.full((1, 128), weight_ref[c], jnp.float32) for c in range(MEMBERS)]
    parity_lost = which == 3
    divisor = jnp.where(which == 0, rows[0], jnp.where(which == 1, rows[1], rows[2]))
    divisor = jnp.where(parity_lost, jnp.ones_like(divisor), divisor)
    out = []
    for c in range(3):
        solved = jnp.where(parity_lost, rows[c], -rows[c] / divisor)
        out.append(jnp.where(which == c, jnp.zeros_like(solved), solved))
    out.append(jnp.where(parity_lost, jnp.zeros_like(divisor), 1.0 / divisor))
    return out


def split_halves(value):
    high = jnp.clip(value, -TOP, TOP).astype(jnp.bfloat16)
    low = (value - high.astype(jnp.float32)).astype(jnp.bfloat16)
    return high, low


def own_row(weights, member):
    own = weights[3]
    for c in range(3):
        own = jnp.where(member == c, weights[c], own)
    return own


def kernel_call(body, name, out_shape, in_specs, out_specs, cost=0, **kwargs):
    return pl.pallas_call(
        body,
        in_specs=in_specs,
        out_specs=out_specs,
        out_shape=out_shape,
        compiler_params=PARAMS,
        cost_estimate=pl.CostEstimate(flops=cost, bytes_accessed=cost, transcendentals=0),
        name=name,
        **kwargs,
    )


def flat(rows):
    return jax.ShapeDtypeStruct((rows, 128), jnp.float32)


def near(member):
    return member + 1 - 2 * lax.rem(member, 2), 3 - member


def scaled_pieces(table_ref, own, where, outs, buf_ref, sem_ref, others=()):
    half = buf_ref.shape[1]
    copies = []
    for i, (quarter, part) in enumerate(where):
        rows = pl.ds(pl.multiple_of(quarter * (2 * half) + part * half, 8), half)
        copies.append(pltpu.make_async_copy(table_ref.at[rows, :], buf_ref.at[i], sem_ref.at[i]))
        copies[-1].start()
    for copy in others:
        copy.start()
    own = own()
    for i, (out_ref, start) in enumerate(outs):
        copies[i].wait()
        out_ref[start : start + half, :] = own * buf_ref[i]
    for copy in others:
        copy.wait()


def passed_pieces(member):
    one, two = near(member)
    return [(3 - one, 0), (near(two)[0], 1)]


def given_pieces(member):
    one, two = near(member)
    return [(one, 0), (two, 1)]


def kept_pieces(member):
    one, two = near(member)
    return [(two, 0), (one, 1), (member, 0), (member, 1)]


def front_kernel(
    lost_ref, weight_hbm, member_ref, table_ref, grads_ref, ids_hbm, a_ref, b_ref,
    buf_ref, sem_ref, grad_sem, ids_ref, weight_ref, small_sem
):
    member = member_ref[0]
    part, lines = grads_ref.shape[0] // 2, ids_ref.shape[0] // 2
    half = buf_ref.shape[1]
    copies = [pltpu.make_async_copy(ids_hbm, ids_ref, small_sem.at[0])]
    for i, out_ref in enumerate((a_ref, b_ref)):
        for h in range(2):
            start = half + h * (part + 8)
            source = grads_ref.at[pl.ds(h * part, part), :]
            copies.append(pltpu.make_async_copy(source, out_ref.at[pl.ds(start, part), :], grad_sem.at[2 * i + h]))
    weights = pltpu.make_async_copy(weight_hbm, weight_ref, small_sem.at[1])
    weights.start()

    def own():
        weights.wait()
        return own_row(decode_weights(lost_ref, weight_ref), member)

    scaled_pieces(table_ref, own, passed_pieces(member), [(a_ref, 0), (b_ref, 0)], buf_ref, sem_ref, copies)
    ids = ids_ref[...].astype(jnp.float32)
    for out_ref in (a_ref, b_ref):
        for h in range(2):
            start = half + h * (part + 8) + part
            out_ref[start : start + lines, :] = ids[h * lines : (h + 1) * lines, :]
            out_ref[start + lines : start + 8, :] = jnp.zeros((8 - lines, 128), jnp.float32)


def keep_kernel(
    lost_ref, weight_ref, member_ref, table_ref, a_ref, b_ref, c_ref, d_ref, mine_ref, buf_ref, sem_ref
):
    member = member_ref[0]
    own = lambda: own_row(decode_weights(lost_ref, weight_ref), member)
    half = buf_ref.shape[1]
    outs = [(a_ref, 0), (b_ref, 0), (c_ref, 0), (d_ref, 0), (mine_ref, 0), (mine_ref, half)]
    scaled_pieces(table_ref, own, given_pieces(member) + kept_pieces(member), outs, buf_ref, sem_ref)


def send_kernel(lost_ref, weight_ref, member_ref, table_ref, a_ref, b_ref, give_a_ref, give_b_ref, buf_ref, sem_ref):
    member = member_ref[0]
    own = lambda: own_row(decode_weights(lost_ref, weight_ref), member)
    outs = [(ref, 0) for ref in (a_ref, b_ref, give_a_ref, give_b_ref)]
    scaled_pieces(table_ref, own, passed_pieces(member) + given_pieces(member), outs, buf_ref, sem_ref)


def stay_kernel(lost_ref, weight_ref, member_ref, table_ref, c_ref, d_ref, mine_ref, buf_ref, sem_ref):
    member = member_ref[0]
    own = lambda: own_row(decode_weights(lost_ref, weight_ref), member)
    half = buf_ref.shape[1]
    outs = [(c_ref, 0), (d_ref, 0), (mine_ref, 0), (mine_ref, half)]
    scaled_pieces(table_ref, own, kept_pieces(member), outs, buf_ref, sem_ref)


def second_kernel(c_ref, d_ref, a_ref, b_ref, out_c_ref, out_d_ref):
    half = c_ref.shape[0]
    out_c_ref[:half, :] = c_ref[...] + a_ref[:half, :]
    out_d_ref[:half, :] = d_ref[...] + b_ref[:half, :]
    extra = out_c_ref.shape[0] - half
    if extra:
        out_c_ref[half:, :] = a_ref[half : half + extra, :]
        out_d_ref[half:, :] = b_ref[half + extra :, :]


def swap(array, which, members):
    pairs = [(i, i ^ 1) for i in range(members)] if which == 0 else [(i, 3 - i) for i in range(members)]
    return lax.ppermute(array, "code", pairs)


def finish(mine_ref, a_ref, b_ref, c_ref, d_ref):
    half = mine_ref.shape[0] // 2
    first = (mine_ref[:half, :] + a_ref[a_ref.shape[0] - half :, :]) + c_ref[:half, :]
    last = (mine_ref[half:, :] + b_ref[b_ref.shape[0] - half :, :]) + d_ref[:half, :]
    return jnp.concatenate([first, last], axis=0)


def add_hits(total, first, part_ref, start, entries):
    high, low = split_halves(part_ref[start : start + entries, :])
    both = jnp.concatenate([high, low], axis=1)
    targets = (lax.broadcasted_iota(jnp.int32, (total.shape[0], 128), 0) + first).astype(jnp.float32)
    lines = [part_ref[start + entries + j : start + entries + j + 1, :] for j in range(entries // 128)]
    hits = [jnp.where(targets == line, 1.0, 0.0).astype(jnp.bfloat16) for line in lines]
    return total + jnp.dot(jnp.concatenate(hits, axis=1), both, preferred_element_type=jnp.float32)


def totals_kernel(member_ref, own_ref, a_ref, b_ref, mine_ref, kept_a_ref, kept_b_ref, out_ref, base_ref):
    count = out_ref.shape[0]
    half = count // 2
    size = (own_ref.shape[0] - half) // 2
    total = jnp.zeros((count, 256), jnp.float32)
    for ref in (own_ref, a_ref, b_ref):
        for h in range(2):
            total = add_hits(total, member_ref[0] * count, ref, half + h * size, size - 8)
    out_ref[...] = total[:, :128] + total[:, 128:]
    base_ref[:half, :] = mine_ref[:half, :] + kept_a_ref[...]
    base_ref[half:, :] = mine_ref[half:, :] + kept_b_ref[...]


def spread(place_ref, values, out_ref, both_ref, stage_ref, sem_ref):
    high, low = split_halves(values)
    both_ref[:, :128] = high
    both_ref[:, 128:] = low
    slots, rows = out_ref.shape[0], values.shape[0]
    step = slots // sem_ref.shape[0]
    place = place_ref[...]
    copies = []
    for i in range(sem_ref.shape[0]):
        here = lax.broadcasted_iota(jnp.int32, (step, rows), 0) + i * step
        pick = jnp.where(here == place, 1.0, 0.0).astype(jnp.bfloat16)
        got = jnp.dot(pick, both_ref[...], preferred_element_type=jnp.float32)
        block = pl.ds(i * step, step)
        stage_ref[block, :] = got[:, :128] + got[:, 128:]
        copies.append(pltpu.make_async_copy(stage_ref.at[block, :], out_ref.at[block, :], sem_ref.at[i]))
        copies[-1].start()
    for copy in copies:
        copy.wait()


def sums_kernel(
    member_ref, place_ref, base_ref, c_ref, d_ref, part_ref, out_ref, new_ref, total_ref, both_ref, stage_ref, sem_ref
):
    count = base_ref.shape[0]
    half = count // 2
    more = jnp.zeros((count, 256), jnp.float32)
    for ref in (c_ref, d_ref):
        more = add_hits(more, member_ref[0] * count, ref, half, ref.shape[0] - half - 8)
    total = part_ref[...] + (more[:, :128] + more[:, 128:])
    total_ref[...] = total
    new = base_ref[...] + jnp.concatenate([c_ref[:half, :], d_ref[:half, :]], axis=0) + total * total
    new_ref[...] = new
    spread(place_ref, new, out_ref, both_ref, stage_ref, sem_ref)


def rows_kernel(
    place_ref, mine_ref, a_ref, b_ref, c_ref, d_ref, total_ref, sums_ref, out_ref, both_ref, stage_ref, sem_ref
):
    mine = finish(mine_ref, a_ref, b_ref, c_ref, d_ref)
    new = mine - step_size * total_ref[...] / (jnp.sqrt(sums_ref[...]) + epsilon)
    spread(place_ref, new, out_ref, both_ref, stage_ref, sem_ref)


def own_code_weight(weight_ref, member):
    own = weight_ref[3]
    for c in range(3):
        own = jnp.where(member == c, weight_ref[c], own)
    return own


def copy_kernel(moved_ref, out_ref):
    out_ref[...] = moved_ref[...]


def quarter_of(which, count):
    return pl.ds(pl.multiple_of(lax.rem(which, MEMBERS) * count, 8), count)


def parity_send_kernel(weight_ref, member_ref, moved_ref, mine_ref, *out_refs):
    member = member_ref[0]
    own = own_code_weight(weight_ref, member)
    count = mine_ref.shape[0]
    for k, out_ref in enumerate(out_refs):
        out_ref[...] = own * moved_ref[quarter_of(member + k + 1, count), :]
    mine_ref[...] = own * moved_ref[quarter_of(member, count), :]


def other_core_kernel(shard_ref, got_ref, out_ref):
    core = lax.rem(shard_ref[0], 2)
    for i in range(out_ref.shape[0] // SLOT):
        start = pl.multiple_of((2 * i + 1 - core) * SLOT, 8)
        out_ref[i * SLOT : (i + 1) * SLOT, :] = got_ref[pl.ds(start, SLOT), :]


def emit_kernel(weight_ref, member_ref, shard_ref, got_ref, side_ref, out_ref, mine_ref, *send_refs):
    core = lax.rem(shard_ref[0], 2)
    for i in range(side_ref.shape[0] // SLOT):
        start = pl.multiple_of((2 * i + core) * SLOT, 8)
        out_ref[pl.ds(start, SLOT), :] = got_ref[pl.ds(start, SLOT), :]
        start = pl.multiple_of((2 * i + 1 - core) * SLOT, 8)
        out_ref[pl.ds(start, SLOT), :] = side_ref[i * SLOT : (i + 1) * SLOT, :]
    parity_send_kernel(weight_ref, member_ref, out_ref, mine_ref, *send_refs)


def parity_sum_kernel(mine_ref, a_ref, b_ref, c_ref, out_ref):
    out_ref[...] = (mine_ref[...] + a_ref[...]) + (b_ref[...] + c_ref[...])


def parity_first_kernel(weight_ref, member_ref, moved_ref, *refs):
    member = member_ref[0]
    own = own_code_weight(weight_ref, member)
    half = refs[0].shape[0]
    outs = [(ref, 0) for ref in refs] + [(refs[-1], half)]
    where = passed_pieces(member) + given_pieces(member) + kept_pieces(member)
    for (out_ref, start), (quarter, part) in zip(outs, where):
        rows = pl.ds(pl.multiple_of(quarter * (2 * half) + part * half, 8), half)
        out_ref[start : start + half, :] = own * moved_ref[rows, :]


def parity_last_kernel(mine_ref, a_ref, b_ref, c_ref, d_ref, out_ref):
    out_ref[...] = finish(mine_ref, a_ref, b_ref, c_ref, d_ref)


def turn(array, k, members):
    return lax.ppermute(array, "code", [(i, (i + k) % members) for i in range(members)])


def second(name, extra, hint, *args):
    half = args[0].shape[0]
    return kernel_call(
        second_kernel,
        "second_" + name,
        (flat(half + extra), flat(half + extra)),
        [VMEM] * 4,
        (VMEM, VMEM),
        cost=hint,
    )(*args)


def parity_relayed(name, key, moved, members):
    slots = moved.shape[0]
    quarter = slots // members
    half = quarter // 2
    a, b, give_a, give_b, keep_c, keep_d, mine = kernel_call(
        parity_first_kernel,
        "parity_first_" + name,
        (flat(half),) * 6 + (flat(quarter),),
        [SMEM, SMEM, VMEM],
        (VMEM,) * 7,
        cost=2 << 20,
    )(*key, moved)
    back_a, back_b = swap(a, 0, members), swap(b, 1, members)
    stay_a, stay_b = swap(give_a, 0, members), swap(give_b, 1, members)
    send_c, send_d = second("parity_" + name, 0, 1 << 33, keep_c, keep_d, back_a, back_b)
    back_c, back_d = swap(send_c, 1, members), swap(send_d, 0, members)
    out = kernel_call(copy_kernel, "emit_" + name, flat(slots), [VMEM], VMEM, cost=2 << 20)(moved)
    parity = kernel_call(
        parity_last_kernel, "parity_last_" + name, flat(quarter), [VMEM] * 5, VMEM, cost=1 << 20
    )(mine, stay_a, stay_b, back_c, back_d)
    return out, parity


def parity_direct(name, key, shard, got, shards, members):
    slots = got.shape[0]
    quarter = slots // members
    side = kernel_call(
        other_core_kernel, "other_core_" + name, flat(slots // 2), [SMEM, VMEM], VMEM, cost=1 << 20
    )(shard, got)
    side = lax.ppermute(side, "shard", [(i, i ^ 1) for i in range(shards)])
    out, mine, *sends = kernel_call(
        emit_kernel,
        "emit_" + name,
        (flat(slots),) + (flat(quarter),) * members,
        [SMEM, SMEM, SMEM, VMEM, VMEM],
        (VMEM,) * (members + 1),
        cost=3 << 20,
    )(*key, shard, got, side)
    gots = {k: turn(sends[k - 1], k, members) for k in (2, 1, 3)}
    parity = kernel_call(
        parity_sum_kernel, "parity_sum_" + name, flat(quarter), [VMEM] * members, VMEM, cost=1 << 20
    )(mine, gots[1], gots[2], gots[3])
    return out, parity


def per_device(
    table_rows, adagrad_sums, lost_member, code_weight, new_owner, pending_rows, pending_grads
):
    members = lax.axis_size("code")
    shards = lax.axis_size("shard")
    member = lax.axis_index("code").astype(jnp.int32)[None]
    share = table_rows.shape[0] // members
    capacity = max(2, (2 * share + shards - 1) // shards)
    slots = shards * capacity
    half = share // 2
    entries = pending_grads.shape[0]
    scalars = [SMEM, SMEM, SMEM]
    key = (lost_member, pltpu.with_memory_space_constraint(code_weight, pltpu.HBM), member)
    owner = new_owner[:, 0]

    def buffers(count):
        return [pltpu.VMEM((count, half, 128), jnp.float32), pltpu.SemaphoreType.DMA((count,))]

    def keep_out(array):
        return pltpu.with_memory_space_constraint(array, pltpu.HBM)

    part = entries // 2 + 8
    send_a, send_b = kernel_call(
        front_kernel,
        "front_send",
        (flat(half + 2 * part), flat(half + 2 * part)),
        [SMEM, HBM, SMEM, HBM, HBM, HBM],
        (VMEM, VMEM),
        cost=3 << 20,
        scratch_shapes=buffers(2)
        + [pltpu.SemaphoreType.DMA((4,)), pltpu.VMEM((entries // 128, 128), jnp.int32)]
        + [pltpu.SMEM((members,), jnp.float32), pltpu.SemaphoreType.DMA((2,))],
    )(*key, keep_out(adagrad_sums), keep_out(pending_grads), keep_out(pending_rows.reshape(-1, 128)))
    got_a, got_b = swap(send_a, 0, members), swap(send_b, 1, members)

    give_a, give_b, keep_c, keep_d, mine_sums = kernel_call(
        keep_kernel,
        "keep_sums",
        (flat(half), flat(half), flat(half), flat(half), flat(share)),
        scalars + [HBM],
        (VMEM,) * 5,
        cost=3 << 20,
        scratch_shapes=buffers(6),
    )(*key, keep_out(adagrad_sums))
    row_a, row_b, row_give_a, row_give_b = kernel_call(
        send_kernel,
        "send_rows",
        (flat(half),) * 4,
        scalars + [HBM],
        (VMEM,) * 4,
        cost=2 << 20,
        scratch_shapes=buffers(4),
    )(*key, keep_out(table_rows))
    give_a, give_b, row_a, row_b = lax.optimization_barrier((give_a, give_b, row_a, row_b))
    kept_a, kept_b = swap(give_a, 0, members), swap(give_b, 1, members)
    earlier = jnp.tril(owner[:, None] == owner[None, :], -1)
    rank = jnp.sum(earlier.astype(jnp.int32), axis=1)
    place = (owner * capacity + rank)[None, :]

    send_c, send_d = second("sums", part, 1 << 38, keep_c, keep_d, got_a, got_b)
    got_c, got_d = swap(send_c, 1, members), swap(send_d, 0, members)
    kept_a, kept_b, got_a, got_b = lax.optimization_barrier((kept_a, kept_b, got_a, got_b))
    part_totals, base_sums = kernel_call(
        totals_kernel, "pending_totals", (flat(share), flat(share)), [SMEM] + [VMEM] * 6, (VMEM, VMEM), cost=4 << 20
    )(member, send_a, got_a, got_b, mine_sums, kept_a, kept_b)
    row_a, row_b, row_give_a, row_give_b, got_c, got_d, part_totals, place, late_rows = lax.optimization_barrier(
        (row_a, row_b, row_give_a, row_give_b, got_c, got_d, part_totals, place, table_rows)
    )
    back_a, back_b = swap(row_a, 0, members), swap(row_b, 1, members)
    stay_a, stay_b = swap(row_give_a, 0, members), swap(row_give_b, 1, members)

    scratch = [
        pltpu.VMEM((share, 256), jnp.bfloat16),
        pltpu.VMEM((slots, 128), jnp.float32),
        pltpu.SemaphoreType.DMA((4,)),
    ]
    out_sums, new_sums, totals = kernel_call(
        sums_kernel,
        "place_sums",
        (flat(slots), flat(share), flat(share)),
        [SMEM] + [VMEM] * 5,
        (HBM, VMEM, VMEM),
        cost=6 << 20,
        scratch_shapes=scratch,
    )(member, place, base_sums, got_c, got_d, part_totals)
    same_core = [list(range(core, shards, 2)) for core in range(2)]
    got_sums = lax.all_to_all(out_sums, "shard", 0, 0, tiled=True, axis_index_groups=same_core)

    row_c, row_d, mine_rows = kernel_call(
        stay_kernel,
        "stay_rows",
        (flat(half), flat(half), flat(share)),
        scalars + [HBM],
        (VMEM,) * 3,
        cost=2 << 20,
        scratch_shapes=buffers(4),
    )(*key, keep_out(late_rows))
    send_c, send_d = second("rows", 0, 1 << 33, row_c, row_d, back_a, back_b)
    back_c, back_d = swap(send_c, 1, members), swap(send_d, 0, members)
    out_rows = kernel_call(
        rows_kernel, "place_rows", flat(slots), [VMEM] * 8, HBM, cost=6 << 20, scratch_shapes=scratch
    )(place, mine_rows, stay_a, stay_b, back_c, back_d, totals, new_sums)
    moved_rows = lax.all_to_all(out_rows, "shard", 0, 0, tiled=True)

    shard = lax.axis_index("shard").astype(jnp.int32)[None]
    final_sums, parity_sums = parity_direct("sums", (code_weight, member), shard, got_sums, shards, members)
    moved_rows, final_sums, parity_sums = lax.optimization_barrier((moved_rows, final_sums, parity_sums))
    final_rows, parity_rows = parity_relayed("rows", (code_weight, member), moved_rows, members)
    return (final_rows, final_sums, parity_rows, parity_sums)


def solution(mesh):
    in_specs = (
        P(("shard", "code"), None),
        P(("shard", "code"), None),
        P("shard"),
        P(),
        P(("shard", "code"), None),
        P(("shard", "code")),
        P(("shard", "code"), None),
    )
    out_specs = (
        P(("shard", "code"), None),
        P(("shard", "code"), None),
        P(("shard", "code"), None),
        P(("shard", "code"), None),
    )
    return jax.shard_map(
        per_device, mesh=mesh, in_specs=in_specs, out_specs=out_specs, check_vma=False
    )
```

```python
import jax
import jax.numpy as jnp
from jax import lax
from jax.experimental import pallas as pl
from jax.experimental.pallas import tpu as pltpu
from jax.sharding import PartitionSpec as P

step_size = 0.5
epsilon = 1e-08
MEMBERS = 4
TOP = float(jnp.finfo(jnp.bfloat16).max)
SLOT = 32
SMEM = pl.BlockSpec(memory_space=pltpu.SMEM)
VMEM = pl.BlockSpec(memory_space=pltpu.VMEM)
HBM = pl.BlockSpec(memory_space=pltpu.HBM)
PARAMS = pltpu.CompilerParams(vmem_limit_bytes=16 * 1024 * 1024)


def decode_weights(lost_ref, weight_ref):
    which = lost_ref[0]
    rows = [jnp.full((1, 128), weight_ref[c], jnp.float32) for c in range(MEMBERS)]
    parity_lost = which == 3
    divisor = jnp.where(which == 0, rows[0], jnp.where(which == 1, rows[1], rows[2]))
    divisor = jnp.where(parity_lost, jnp.ones_like(divisor), divisor)
    out = []
    for c in range(3):
        solved = jnp.where(parity_lost, rows[c], -rows[c] / divisor)
        out.append(jnp.where(which == c, jnp.zeros_like(solved), solved))
    out.append(jnp.where(parity_lost, jnp.zeros_like(divisor), 1.0 / divisor))
    return out


def split_halves(value):
    high = jnp.clip(value, -TOP, TOP).astype(jnp.bfloat16)
    low = (value - high.astype(jnp.float32)).astype(jnp.bfloat16)
    return high, low


def own_row(weights, member):
    own = weights[3]
    for c in range(3):
        own = jnp.where(member == c, weights[c], own)
    return own


def kernel_call(body, name, out_shape, in_specs, out_specs, cost=0, **kwargs):
    return pl.pallas_call(
        body,
        in_specs=in_specs,
        out_specs=out_specs,
        out_shape=out_shape,
        compiler_params=PARAMS,
        cost_estimate=pl.CostEstimate(flops=cost, bytes_accessed=cost, transcendentals=0),
        name=name,
        **kwargs,
    )


def flat(rows):
    return jax.ShapeDtypeStruct((rows, 128), jnp.float32)


def near(member):
    return member + 1 - 2 * lax.rem(member, 2), 3 - member


def scaled_pieces(table_ref, own, where, outs, buf_ref, sem_ref, others=()):
    half = buf_ref.shape[1]
    copies = []
    for i, (quarter, part) in enumerate(where):
        rows = pl.ds(pl.multiple_of(quarter * (2 * half) + part * half, 8), half)
        copies.append(pltpu.make_async_copy(table_ref.at[rows, :], buf_ref.at[i], sem_ref.at[i]))
        copies[-1].start()
    for copy in others:
        copy.start()
    own = own()
    for i, (out_ref, start) in enumerate(outs):
        copies[i].wait()
        out_ref[start : start + half, :] = own * buf_ref[i]
    for copy in others:
        copy.wait()


def passed_pieces(member):
    one, two = near(member)
    return [(3 - one, 0), (near(two)[0], 1)]


def given_pieces(member):
    one, two = near(member)
    return [(one, 0), (two, 1)]


def kept_pieces(member):
    one, two = near(member)
    return [(two, 0), (one, 1), (member, 0), (member, 1)]


def front_kernel(
    lost_ref, weight_hbm, member_ref, table_ref, grads_ref, ids_hbm, a_ref, b_ref,
    buf_ref, sem_ref, grad_sem, ids_ref, weight_ref, small_sem
):
    member = member_ref[0]
    part, lines = grads_ref.shape[0] // 2, ids_ref.shape[0] // 2
    half = buf_ref.shape[1]
    copies = [pltpu.make_async_copy(ids_hbm, ids_ref, small_sem.at[0])]
    for i, out_ref in enumerate((a_ref, b_ref)):
        for h in range(2):
            start = half + h * (part + 8)
            source = grads_ref.at[pl.ds(h * part, part), :]
            copies.append(pltpu.make_async_copy(source, out_ref.at[pl.ds(start, part), :], grad_sem.at[2 * i + h]))
    weights = pltpu.make_async_copy(weight_hbm, weight_ref, small_sem.at[1])
    weights.start()

    def own():
        weights.wait()
        return own_row(decode_weights(lost_ref, weight_ref), member)

    scaled_pieces(table_ref, own, passed_pieces(member), [(a_ref, 0), (b_ref, 0)], buf_ref, sem_ref, copies)
    ids = ids_ref[...].astype(jnp.float32)
    for out_ref in (a_ref, b_ref):
        for h in range(2):
            start = half + h * (part + 8) + part
            out_ref[start : start + lines, :] = ids[h * lines : (h + 1) * lines, :]
            out_ref[start + lines : start + 8, :] = jnp.zeros((8 - lines, 128), jnp.float32)


def keep_kernel(
    lost_ref, weight_ref, member_ref, table_ref, a_ref, b_ref, c_ref, d_ref, mine_ref, buf_ref, sem_ref
):
    member = member_ref[0]
    own = lambda: own_row(decode_weights(lost_ref, weight_ref), member)
    half = buf_ref.shape[1]
    outs = [(a_ref, 0), (b_ref, 0), (c_ref, 0), (d_ref, 0), (mine_ref, 0), (mine_ref, half)]
    scaled_pieces(table_ref, own, given_pieces(member) + kept_pieces(member), outs, buf_ref, sem_ref)


def send_kernel(lost_ref, weight_ref, member_ref, table_ref, a_ref, b_ref, give_a_ref, give_b_ref, buf_ref, sem_ref):
    member = member_ref[0]
    own = lambda: own_row(decode_weights(lost_ref, weight_ref), member)
    outs = [(ref, 0) for ref in (a_ref, b_ref, give_a_ref, give_b_ref)]
    scaled_pieces(table_ref, own, passed_pieces(member) + given_pieces(member), outs, buf_ref, sem_ref)


def stay_kernel(lost_ref, weight_ref, member_ref, table_ref, c_ref, d_ref, mine_ref, code_ref, buf_ref, sem_ref):
    member = member_ref[0]
    code_ref[...] = jnp.full(code_ref.shape, own_code_weight(weight_ref, member), jnp.float32)
    own = lambda: own_row(decode_weights(lost_ref, weight_ref), member)
    half = buf_ref.shape[1]
    outs = [(c_ref, 0), (d_ref, 0), (mine_ref, 0), (mine_ref, half)]
    scaled_pieces(table_ref, own, kept_pieces(member), outs, buf_ref, sem_ref)


def second_kernel(c_ref, d_ref, a_ref, b_ref, out_c_ref, out_d_ref):
    half = c_ref.shape[0]
    out_c_ref[:half, :] = c_ref[...] + a_ref[:half, :]
    out_d_ref[:half, :] = d_ref[...] + b_ref[:half, :]
    extra = out_c_ref.shape[0] - half
    if extra:
        out_c_ref[half:, :] = a_ref[half : half + extra, :]
        out_d_ref[half:, :] = b_ref[half + extra :, :]


def swap(array, which, members):
    pairs = [(i, i ^ 1) for i in range(members)] if which == 0 else [(i, 3 - i) for i in range(members)]
    return lax.ppermute(array, "code", pairs)


def finish(mine_ref, a_ref, b_ref, c_ref, d_ref):
    half = mine_ref.shape[0] // 2
    first = (mine_ref[:half, :] + a_ref[a_ref.shape[0] - half :, :]) + c_ref[:half, :]
    last = (mine_ref[half:, :] + b_ref[b_ref.shape[0] - half :, :]) + d_ref[:half, :]
    return jnp.concatenate([first, last], axis=0)


def add_hits(total, first, part_ref, start, entries):
    high, low = split_halves(part_ref[start : start + entries, :])
    both = jnp.concatenate([high, low], axis=1)
    targets = (lax.broadcasted_iota(jnp.int32, (total.shape[0], 128), 0) + first).astype(jnp.float32)
    lines = [part_ref[start + entries + j : start + entries + j + 1, :] for j in range(entries // 128)]
    hits = [jnp.where(targets == line, 1.0, 0.0).astype(jnp.bfloat16) for line in lines]
    return total + jnp.dot(jnp.concatenate(hits, axis=1), both, preferred_element_type=jnp.float32)


def totals_kernel(member_ref, own_ref, a_ref, b_ref, mine_ref, kept_a_ref, kept_b_ref, out_ref, base_ref):
    count = out_ref.shape[0]
    half = count // 2
    size = (own_ref.shape[0] - half) // 2
    total = jnp.zeros((count, 256), jnp.float32)
    for ref in (own_ref, a_ref, b_ref):
        for h in range(2):
            total = add_hits(total, member_ref[0] * count, ref, half + h * size, size - 8)
    out_ref[...] = total[:, :128] + total[:, 128:]
    base_ref[:half, :] = mine_ref[:half, :] + kept_a_ref[...]
    base_ref[half:, :] = mine_ref[half:, :] + kept_b_ref[...]


def spread(place_ref, values, out_ref, both_ref, stage_ref, sem_ref):
    high, low = split_halves(values)
    both_ref[:, :128] = high
    both_ref[:, 128:] = low
    slots, rows = out_ref.shape[0], values.shape[0]
    step = slots // sem_ref.shape[0]
    place = place_ref[...]
    copies = []
    for i in range(sem_ref.shape[0]):
        here = lax.broadcasted_iota(jnp.int32, (step, rows), 0) + i * step
        pick = jnp.where(here == place, 1.0, 0.0).astype(jnp.bfloat16)
        got = jnp.dot(pick, both_ref[...], preferred_element_type=jnp.float32)
        block = pl.ds(i * step, step)
        stage_ref[block, :] = got[:, :128] + got[:, 128:]
        copies.append(pltpu.make_async_copy(stage_ref.at[block, :], out_ref.at[block, :], sem_ref.at[i]))
        copies[-1].start()
    for copy in copies:
        copy.wait()


def sums_kernel(
    place_ref, base_ref, c_ref, d_ref, part_ref, out_ref, new_ref, total_ref, both_ref, stage_ref, sem_ref
):
    count = base_ref.shape[0]
    half = count // 2
    more = jnp.zeros((count, 256), jnp.float32)
    for ref in (c_ref, d_ref):
        more = add_hits(more, lax.axis_index("code") * count, ref, half, ref.shape[0] - half - 8)
    total = part_ref[...] + (more[:, :128] + more[:, 128:])
    total_ref[...] = total
    new = base_ref[...] + jnp.concatenate([c_ref[:half, :], d_ref[:half, :]], axis=0) + total * total
    new_ref[...] = new
    spread(place_ref, new, out_ref, both_ref, stage_ref, sem_ref)


def rows_kernel(
    place_ref, mine_ref, a_ref, b_ref, c_ref, d_ref, total_ref, sums_ref, out_ref, both_ref, stage_ref, sem_ref
):
    mine = finish(mine_ref, a_ref, b_ref, c_ref, d_ref)
    new = mine - step_size * total_ref[...] / (jnp.sqrt(sums_ref[...]) + epsilon)
    spread(place_ref, new, out_ref, both_ref, stage_ref, sem_ref)


def own_code_weight(weight_ref, member):
    own = weight_ref[3]
    for c in range(3):
        own = jnp.where(member == c, weight_ref[c], own)
    return own


def copy_kernel(moved_ref, out_ref):
    out_ref[...] = moved_ref[...]


def quarter_of(which, count):
    return pl.ds(pl.multiple_of(lax.rem(which, MEMBERS) * count, 8), count)


def parity_send_kernel(weight_ref, member_ref, moved_ref, mine_ref, *out_refs):
    member = member_ref[0]
    own = own_code_weight(weight_ref, member)
    count = mine_ref.shape[0]
    for k, out_ref in enumerate(out_refs):
        out_ref[...] = own * moved_ref[quarter_of(member + k + 1, count), :]
    mine_ref[...] = own * moved_ref[quarter_of(member, count), :]


def other_core_kernel(shard_ref, got_ref, out_ref):
    core = lax.rem(shard_ref[0], 2)
    for i in range(out_ref.shape[0] // SLOT):
        start = pl.multiple_of((2 * i + 1 - core) * SLOT, 8)
        out_ref[i * SLOT : (i + 1) * SLOT, :] = got_ref[pl.ds(start, SLOT), :]


def emit_kernel(weight_ref, member_ref, shard_ref, got_ref, side_ref, out_ref, mine_ref, *send_refs):
    core = lax.rem(shard_ref[0], 2)
    for i in range(side_ref.shape[0] // SLOT):
        start = pl.multiple_of((2 * i + core) * SLOT, 8)
        out_ref[pl.ds(start, SLOT), :] = got_ref[pl.ds(start, SLOT), :]
        start = pl.multiple_of((2 * i + 1 - core) * SLOT, 8)
        out_ref[pl.ds(start, SLOT), :] = side_ref[i * SLOT : (i + 1) * SLOT, :]
    parity_send_kernel(weight_ref, member_ref, out_ref, mine_ref, *send_refs)


def parity_sum_kernel(mine_ref, a_ref, b_ref, c_ref, out_ref):
    out_ref[...] = (mine_ref[...] + a_ref[...]) + (b_ref[...] + c_ref[...])


def parity_first_kernel(code_ref, moved_ref, *refs):
    member = lax.axis_index("code")
    own = code_ref[0:1, :]
    half = refs[0].shape[0]
    outs = [(ref, 0) for ref in refs] + [(refs[-1], half)]
    where = passed_pieces(member) + given_pieces(member) + kept_pieces(member)
    for (out_ref, start), (quarter, part) in zip(outs, where):
        rows = pl.ds(pl.multiple_of(quarter * (2 * half) + part * half, 8), half)
        out_ref[start : start + half, :] = own * moved_ref[rows, :]


def parity_last_kernel(mine_ref, a_ref, b_ref, c_ref, d_ref, out_ref):
    out_ref[...] = finish(mine_ref, a_ref, b_ref, c_ref, d_ref)


def turn(array, k, members):
    return lax.ppermute(array, "code", [(i, (i + k) % members) for i in range(members)])


def second(name, extra, hint, *args):
    half = args[0].shape[0]
    return kernel_call(
        second_kernel,
        "second_" + name,
        (flat(half + extra), flat(half + extra)),
        [VMEM] * 4,
        (VMEM, VMEM),
        cost=hint,
    )(*args)


def parity_relayed(name, code_row, moved, members):
    slots = moved.shape[0]
    quarter = slots // members
    half = quarter // 2
    a, b, give_a, give_b, keep_c, keep_d, mine = kernel_call(
        parity_first_kernel,
        "parity_first_" + name,
        (flat(half),) * 6 + (flat(quarter),),
        [VMEM, VMEM],
        (VMEM,) * 7,
        cost=2 << 20,
    )(code_row, moved)
    back_a, back_b = swap(a, 0, members), swap(b, 1, members)
    stay_a, stay_b = swap(give_a, 0, members), swap(give_b, 1, members)
    send_c, send_d = second("parity_" + name, 0, 1 << 33, keep_c, keep_d, back_a, back_b)
    back_c, back_d = swap(send_c, 1, members), swap(send_d, 0, members)
    out = kernel_call(copy_kernel, "emit_" + name, flat(slots), [VMEM], VMEM, cost=2 << 20)(moved)
    parity = kernel_call(
        parity_last_kernel, "parity_last_" + name, flat(quarter), [VMEM] * 5, VMEM, cost=1 << 20
    )(mine, stay_a, stay_b, back_c, back_d)
    return out, parity


def parity_direct(name, key, shard, got, shards, members):
    slots = got.shape[0]
    quarter = slots // members
    side = kernel_call(
        other_core_kernel, "other_core_" + name, flat(slots // 2), [SMEM, VMEM], VMEM, cost=1 << 20
    )(shard, got)
    side = lax.ppermute(side, "shard", [(i, i ^ 1) for i in range(shards)])
    out, mine, *sends = kernel_call(
        emit_kernel,
        "emit_" + name,
        (flat(slots),) + (flat(quarter),) * members,
        [SMEM, SMEM, SMEM, VMEM, VMEM],
        (VMEM,) * (members + 1),
        cost=3 << 20,
    )(*key, shard, got, side)
    gots = {k: turn(sends[k - 1], k, members) for k in (2, 1, 3)}
    parity = kernel_call(
        parity_sum_kernel, "parity_sum_" + name, flat(quarter), [VMEM] * members, VMEM, cost=1 << 20
    )(mine, gots[1], gots[2], gots[3])
    return out, parity


def per_device(
    table_rows, adagrad_sums, lost_member, code_weight, new_owner, pending_rows, pending_grads
):
    members = lax.axis_size("code")
    shards = lax.axis_size("shard")
    member = lax.axis_index("code").astype(jnp.int32)[None]
    share = table_rows.shape[0] // members
    capacity = max(2, (2 * share + shards - 1) // shards)
    slots = shards * capacity
    half = share // 2
    entries = pending_grads.shape[0]
    scalars = [SMEM, SMEM, SMEM]
    key = (lost_member, pltpu.with_memory_space_constraint(code_weight, pltpu.HBM), member)
    owner = new_owner[:, 0]

    def buffers(count):
        return [pltpu.VMEM((count, half, 128), jnp.float32), pltpu.SemaphoreType.DMA((count,))]

    def keep_out(array):
        return pltpu.with_memory_space_constraint(array, pltpu.HBM)

    part = entries // 2 + 8
    send_a, send_b = kernel_call(
        front_kernel,
        "front_send",
        (flat(half + 2 * part), flat(half + 2 * part)),
        [SMEM, HBM, SMEM, HBM, HBM, HBM],
        (VMEM, VMEM),
        cost=3 << 20,
        scratch_shapes=buffers(2)
        + [pltpu.SemaphoreType.DMA((4,)), pltpu.VMEM((entries // 128, 128), jnp.int32)]
        + [pltpu.SMEM((members,), jnp.float32), pltpu.SemaphoreType.DMA((2,))],
    )(*key, keep_out(adagrad_sums), keep_out(pending_grads), keep_out(pending_rows.reshape(-1, 128)))
    got_a, got_b = swap(send_a, 0, members), swap(send_b, 1, members)

    give_a, give_b, keep_c, keep_d, mine_sums = kernel_call(
        keep_kernel,
        "keep_sums",
        (flat(half), flat(half), flat(half), flat(half), flat(share)),
        scalars + [HBM],
        (VMEM,) * 5,
        cost=3 << 20,
        scratch_shapes=buffers(6),
    )(*key, keep_out(adagrad_sums))
    row_a, row_b, row_give_a, row_give_b = kernel_call(
        send_kernel,
        "send_rows",
        (flat(half),) * 4,
        scalars + [HBM],
        (VMEM,) * 4,
        cost=2 << 20,
        scratch_shapes=buffers(4),
    )(*key, keep_out(table_rows))
    give_a, give_b, row_a, row_b = lax.optimization_barrier((give_a, give_b, row_a, row_b))
    kept_a, kept_b = swap(give_a, 0, members), swap(give_b, 1, members)
    earlier = jnp.tril(owner[:, None] == owner[None, :], -1)
    rank = jnp.sum(earlier.astype(jnp.int32), axis=1)
    place = (owner * capacity + rank)[None, :]

    send_c, send_d = second("sums", part, 1 << 38, keep_c, keep_d, got_a, got_b)
    got_c, got_d = swap(send_c, 1, members), swap(send_d, 0, members)
    kept_a, kept_b, got_a, got_b = lax.optimization_barrier((kept_a, kept_b, got_a, got_b))
    part_totals, base_sums = kernel_call(
        totals_kernel, "pending_totals", (flat(share), flat(share)), [SMEM] + [VMEM] * 6, (VMEM, VMEM), cost=4 << 20
    )(member, send_a, got_a, got_b, mine_sums, kept_a, kept_b)
    row_a, row_b, row_give_a, row_give_b, got_c, got_d, part_totals, place, late_rows = lax.optimization_barrier(
        (row_a, row_b, row_give_a, row_give_b, got_c, got_d, part_totals, place, table_rows)
    )
    back_a, back_b = swap(row_a, 0, members), swap(row_b, 1, members)
    stay_a, stay_b = swap(row_give_a, 0, members), swap(row_give_b, 1, members)

    scratch = [
        pltpu.VMEM((share, 256), jnp.bfloat16),
        pltpu.VMEM((slots, 128), jnp.float32),
        pltpu.SemaphoreType.DMA((4,)),
    ]
    out_sums, new_sums, totals = kernel_call(
        sums_kernel,
        "place_sums",
        (flat(slots), flat(share), flat(share)),
        [VMEM] * 5,
        (HBM, VMEM, VMEM),
        cost=6 << 20,
        scratch_shapes=scratch,
    )(place, base_sums, got_c, got_d, part_totals)
    same_core = [list(range(core, shards, 2)) for core in range(2)]
    got_sums = lax.all_to_all(out_sums, "shard", 0, 0, tiled=True, axis_index_groups=same_core)

    row_c, row_d, mine_rows, code_row = kernel_call(
        stay_kernel,
        "stay_rows",
        (flat(half), flat(half), flat(share), flat(8)),
        scalars + [HBM],
        (VMEM,) * 4,
        cost=2 << 20,
        scratch_shapes=buffers(4),
    )(*key, keep_out(late_rows))
    send_c, send_d = second("rows", 0, 1 << 33, row_c, row_d, back_a, back_b)
    back_c, back_d = swap(send_c, 1, members), swap(send_d, 0, members)
    out_rows = kernel_call(
        rows_kernel, "place_rows", flat(slots), [VMEM] * 8, HBM, cost=6 << 20, scratch_shapes=scratch
    )(place, mine_rows, stay_a, stay_b, back_c, back_d, totals, new_sums)
    moved_rows = lax.all_to_all(out_rows, "shard", 0, 0, tiled=True)

    shard = lax.axis_index("shard").astype(jnp.int32)[None]
    final_sums, parity_sums = parity_direct("sums", (code_weight, member), shard, got_sums, shards, members)
    moved_rows, final_sums, parity_sums = lax.optimization_barrier((moved_rows, final_sums, parity_sums))
    final_rows, parity_rows = parity_relayed("rows", code_row, moved_rows, members)
    return (final_rows, final_sums, parity_rows, parity_sums)


def solution(mesh):
    in_specs = (
        P(("shard", "code"), None),
        P(("shard", "code"), None),
        P("shard"),
        P(),
        P(("shard", "code"), None),
        P(("shard", "code")),
        P(("shard", "code"), None),
    )
    out_specs = (
        P(("shard", "code"), None),
        P(("shard", "code"), None),
        P(("shard", "code"), None),
        P(("shard", "code"), None),
    )
    return jax.shard_map(
        per_device, mesh=mesh, in_specs=in_specs, out_specs=out_specs, check_vma=False
    )
```

```python
import jax
import jax.numpy as jnp
from jax import lax
from jax.experimental import pallas as pl
from jax.experimental.pallas import tpu as pltpu
from jax.sharding import PartitionSpec as P

step_size = 0.5
epsilon = 1e-08
MEMBERS = 4
TOP = float(jnp.finfo(jnp.bfloat16).max)
SLOT = 32
SMEM = pl.BlockSpec(memory_space=pltpu.SMEM)
VMEM = pl.BlockSpec(memory_space=pltpu.VMEM)
HBM = pl.BlockSpec(memory_space=pltpu.HBM)
PARAMS = pltpu.CompilerParams(vmem_limit_bytes=16 * 1024 * 1024)


def decode_weights(lost_ref, weight_ref):
    which = lost_ref[0]
    rows = [jnp.full((1, 128), weight_ref[c], jnp.float32) for c in range(MEMBERS)]
    parity_lost = which == 3
    divisor = jnp.where(which == 0, rows[0], jnp.where(which == 1, rows[1], rows[2]))
    divisor = jnp.where(parity_lost, jnp.ones_like(divisor), divisor)
    out = []
    for c in range(3):
        solved = jnp.where(parity_lost, rows[c], -rows[c] / divisor)
        out.append(jnp.where(which == c, jnp.zeros_like(solved), solved))
    out.append(jnp.where(parity_lost, jnp.zeros_like(divisor), 1.0 / divisor))
    return out


def split_halves(value):
    high = jnp.clip(value, -TOP, TOP).astype(jnp.bfloat16)
    low = (value - high.astype(jnp.float32)).astype(jnp.bfloat16)
    return high, low


def own_row(weights, member):
    own = weights[3]
    for c in range(3):
        own = jnp.where(member == c, weights[c], own)
    return own


def kernel_call(body, name, out_shape, in_specs, out_specs, cost=0, **kwargs):
    return pl.pallas_call(
        body,
        in_specs=in_specs,
        out_specs=out_specs,
        out_shape=out_shape,
        compiler_params=PARAMS,
        cost_estimate=pl.CostEstimate(flops=cost, bytes_accessed=cost, transcendentals=0),
        name=name,
        **kwargs,
    )


def flat(rows):
    return jax.ShapeDtypeStruct((rows, 128), jnp.float32)


def near(member):
    return member + 1 - 2 * lax.rem(member, 2), 3 - member


def scaled_pieces(table_ref, own, where, outs, buf_ref, sem_ref, others=()):
    half = buf_ref.shape[1]
    copies = []
    for i, (quarter, part) in enumerate(where):
        rows = pl.ds(pl.multiple_of(quarter * (2 * half) + part * half, 8), half)
        copies.append(pltpu.make_async_copy(table_ref.at[rows, :], buf_ref.at[i], sem_ref.at[i]))
        copies[-1].start()
    for copy in others:
        copy.start()
    own = own()
    for i, (out_ref, start) in enumerate(outs):
        copies[i].wait()
        out_ref[start : start + half, :] = own * buf_ref[i]
    for copy in others:
        copy.wait()


def passed_pieces(member):
    one, two = near(member)
    return [(3 - one, 0), (near(two)[0], 1)]


def given_pieces(member):
    one, two = near(member)
    return [(one, 0), (two, 1)]


def kept_pieces(member):
    one, two = near(member)
    return [(two, 0), (one, 1), (member, 0), (member, 1)]


def front_kernel(
    lost_ref, weight_hbm, table_ref, grads_ref, ids_hbm, a_ref, b_ref,
    buf_ref, sem_ref, grad_sem, ids_ref, weight_ref, small_sem
):
    member = lax.axis_index("code")
    part, lines = grads_ref.shape[0] // 2, ids_ref.shape[0] // 2
    half = buf_ref.shape[1]
    copies = [pltpu.make_async_copy(ids_hbm, ids_ref, small_sem.at[0])]
    for i, out_ref in enumerate((a_ref, b_ref)):
        for h in range(2):
            start = half + h * (part + 8)
            source = grads_ref.at[pl.ds(h * part, part), :]
            copies.append(pltpu.make_async_copy(source, out_ref.at[pl.ds(start, part), :], grad_sem.at[2 * i + h]))
    weights = pltpu.make_async_copy(weight_hbm, weight_ref, small_sem.at[1])
    weights.start()

    def own():
        weights.wait()
        return own_row(decode_weights(lost_ref, weight_ref), member)

    scaled_pieces(table_ref, own, passed_pieces(member), [(a_ref, 0), (b_ref, 0)], buf_ref, sem_ref, copies)
    ids = ids_ref[...].astype(jnp.float32)
    for out_ref in (a_ref, b_ref):
        for h in range(2):
            start = half + h * (part + 8) + part
            out_ref[start : start + lines, :] = ids[h * lines : (h + 1) * lines, :]
            out_ref[start + lines : start + 8, :] = jnp.zeros((8 - lines, 128), jnp.float32)


def keep_kernel(
    lost_ref, weight_ref, member_ref, table_ref, a_ref, b_ref, c_ref, d_ref, mine_ref, buf_ref, sem_ref
):
    member = member_ref[0]
    own = lambda: own_row(decode_weights(lost_ref, weight_ref), member)
    half = buf_ref.shape[1]
    outs = [(a_ref, 0), (b_ref, 0), (c_ref, 0), (d_ref, 0), (mine_ref, 0), (mine_ref, half)]
    scaled_pieces(table_ref, own, given_pieces(member) + kept_pieces(member), outs, buf_ref, sem_ref)


def send_kernel(lost_ref, weight_ref, member_ref, table_ref, a_ref, b_ref, give_a_ref, give_b_ref, buf_ref, sem_ref):
    member = member_ref[0]
    own = lambda: own_row(decode_weights(lost_ref, weight_ref), member)
    outs = [(ref, 0) for ref in (a_ref, b_ref, give_a_ref, give_b_ref)]
    scaled_pieces(table_ref, own, passed_pieces(member) + given_pieces(member), outs, buf_ref, sem_ref)


def stay_kernel(lost_ref, weight_ref, member_ref, table_ref, c_ref, d_ref, mine_ref, code_ref, buf_ref, sem_ref):
    member = member_ref[0]
    code_ref[...] = jnp.full(code_ref.shape, own_code_weight(weight_ref, member), jnp.float32)
    own = lambda: own_row(decode_weights(lost_ref, weight_ref), member)
    half = buf_ref.shape[1]
    outs = [(c_ref, 0), (d_ref, 0), (mine_ref, 0), (mine_ref, half)]
    scaled_pieces(table_ref, own, kept_pieces(member), outs, buf_ref, sem_ref)


def second_kernel(c_ref, d_ref, a_ref, b_ref, out_c_ref, out_d_ref):
    half = c_ref.shape[0]
    out_c_ref[:half, :] = c_ref[...] + a_ref[:half, :]
    out_d_ref[:half, :] = d_ref[...] + b_ref[:half, :]
    extra = out_c_ref.shape[0] - half
    if extra:
        out_c_ref[half:, :] = a_ref[half : half + extra, :]
        out_d_ref[half:, :] = b_ref[half + extra :, :]


def swap(array, which, members):
    pairs = [(i, i ^ 1) for i in range(members)] if which == 0 else [(i, 3 - i) for i in range(members)]
    return lax.ppermute(array, "code", pairs)


def finish(mine_ref, a_ref, b_ref, c_ref, d_ref):
    half = mine_ref.shape[0] // 2
    first = (mine_ref[:half, :] + a_ref[a_ref.shape[0] - half :, :]) + c_ref[:half, :]
    last = (mine_ref[half:, :] + b_ref[b_ref.shape[0] - half :, :]) + d_ref[:half, :]
    return jnp.concatenate([first, last], axis=0)


def add_hits(total, first, part_ref, start, entries):
    high, low = split_halves(part_ref[start : start + entries, :])
    both = jnp.concatenate([high, low], axis=1)
    targets = (lax.broadcasted_iota(jnp.int32, (total.shape[0], 128), 0) + first).astype(jnp.float32)
    lines = [part_ref[start + entries + j : start + entries + j + 1, :] for j in range(entries // 128)]
    hits = [jnp.where(targets == line, 1.0, 0.0).astype(jnp.bfloat16) for line in lines]
    return total + jnp.dot(jnp.concatenate(hits, axis=1), both, preferred_element_type=jnp.float32)


def totals_kernel(member_ref, own_ref, a_ref, b_ref, mine_ref, kept_a_ref, kept_b_ref, out_ref, base_ref):
    count = out_ref.shape[0]
    half = count // 2
    size = (own_ref.shape[0] - half) // 2
    total = jnp.zeros((count, 256), jnp.float32)
    for ref in (own_ref, a_ref, b_ref):
        for h in range(2):
            total = add_hits(total, member_ref[0] * count, ref, half + h * size, size - 8)
    out_ref[...] = total[:, :128] + total[:, 128:]
    base_ref[:half, :] = mine_ref[:half, :] + kept_a_ref[...]
    base_ref[half:, :] = mine_ref[half:, :] + kept_b_ref[...]


def spread(place_ref, values, out_ref, both_ref, stage_ref, sem_ref):
    high, low = split_halves(values)
    both_ref[:, :128] = high
    both_ref[:, 128:] = low
    slots, rows = out_ref.shape[0], values.shape[0]
    step = slots // sem_ref.shape[0]
    place = place_ref[...]
    copies = []
    for i in range(sem_ref.shape[0]):
        here = lax.broadcasted_iota(jnp.int32, (step, rows), 0) + i * step
        pick = jnp.where(here == place, 1.0, 0.0).astype(jnp.bfloat16)
        got = jnp.dot(pick, both_ref[...], preferred_element_type=jnp.float32)
        block = pl.ds(i * step, step)
        stage_ref[block, :] = got[:, :128] + got[:, 128:]
        copies.append(pltpu.make_async_copy(stage_ref.at[block, :], out_ref.at[block, :], sem_ref.at[i]))
        copies[-1].start()
    for copy in copies:
        copy.wait()


def sums_kernel(
    place_ref, base_ref, c_ref, d_ref, part_ref, out_ref, new_ref, total_ref, both_ref, stage_ref, sem_ref
):
    count = base_ref.shape[0]
    half = count // 2
    more = jnp.zeros((count, 256), jnp.float32)
    for ref in (c_ref, d_ref):
        more = add_hits(more, lax.axis_index("code") * count, ref, half, ref.shape[0] - half - 8)
    total = part_ref[...] + (more[:, :128] + more[:, 128:])
    total_ref[...] = total
    new = base_ref[...] + jnp.concatenate([c_ref[:half, :], d_ref[:half, :]], axis=0) + total * total
    new_ref[...] = new
    spread(place_ref, new, out_ref, both_ref, stage_ref, sem_ref)


def rows_kernel(
    place_ref, mine_ref, a_ref, b_ref, c_ref, d_ref, total_ref, sums_ref, out_ref, both_ref, stage_ref, sem_ref
):
    mine = finish(mine_ref, a_ref, b_ref, c_ref, d_ref)
    new = mine - step_size * total_ref[...] / (jnp.sqrt(sums_ref[...]) + epsilon)
    spread(place_ref, new, out_ref, both_ref, stage_ref, sem_ref)


def own_code_weight(weight_ref, member):
    own = weight_ref[3]
    for c in range(3):
        own = jnp.where(member == c, weight_ref[c], own)
    return own


def copy_kernel(moved_ref, out_ref):
    out_ref[...] = moved_ref[...]


def quarter_of(which, count):
    return pl.ds(pl.multiple_of(lax.rem(which, MEMBERS) * count, 8), count)


def parity_send_kernel(weight_ref, member_ref, moved_ref, mine_ref, *out_refs):
    member = member_ref[0]
    own = own_code_weight(weight_ref, member)
    count = mine_ref.shape[0]
    for k, out_ref in enumerate(out_refs):
        out_ref[...] = own * moved_ref[quarter_of(member + k + 1, count), :]
    mine_ref[...] = own * moved_ref[quarter_of(member, count), :]


def other_core_kernel(shard_ref, got_ref, out_ref):
    core = lax.rem(shard_ref[0], 2)
    for i in range(out_ref.shape[0] // SLOT):
        start = pl.multiple_of((2 * i + 1 - core) * SLOT, 8)
        out_ref[i * SLOT : (i + 1) * SLOT, :] = got_ref[pl.ds(start, SLOT), :]


def emit_kernel(weight_ref, member_ref, shard_ref, got_ref, side_ref, out_ref, mine_ref, *send_refs):
    core = lax.rem(shard_ref[0], 2)
    for i in range(side_ref.shape[0] // SLOT):
        start = pl.multiple_of((2 * i + core) * SLOT, 8)
        out_ref[pl.ds(start, SLOT), :] = got_ref[pl.ds(start, SLOT), :]
        start = pl.multiple_of((2 * i + 1 - core) * SLOT, 8)
        out_ref[pl.ds(start, SLOT), :] = side_ref[i * SLOT : (i + 1) * SLOT, :]
    parity_send_kernel(weight_ref, member_ref, out_ref, mine_ref, *send_refs)


def parity_sum_kernel(mine_ref, a_ref, b_ref, c_ref, out_ref):
    out_ref[...] = (mine_ref[...] + a_ref[...]) + (b_ref[...] + c_ref[...])


def parity_first_kernel(code_ref, moved_ref, *refs):
    member = lax.axis_index("code")
    own = code_ref[0:1, :]
    half = refs[0].shape[0]
    outs = [(ref, 0) for ref in refs] + [(refs[-1], half)]
    where = passed_pieces(member) + given_pieces(member) + kept_pieces(member)
    for (out_ref, start), (quarter, part) in zip(outs, where):
        rows = pl.ds(pl.multiple_of(quarter * (2 * half) + part * half, 8), half)
        out_ref[start : start + half, :] = own * moved_ref[rows, :]


def parity_last_kernel(mine_ref, a_ref, b_ref, c_ref, d_ref, out_ref):
    out_ref[...] = finish(mine_ref, a_ref, b_ref, c_ref, d_ref)


def turn(array, k, members):
    return lax.ppermute(array, "code", [(i, (i + k) % members) for i in range(members)])


def second(name, extra, hint, *args):
    half = args[0].shape[0]
    return kernel_call(
        second_kernel,
        "second_" + name,
        (flat(half + extra), flat(half + extra)),
        [VMEM] * 4,
        (VMEM, VMEM),
        cost=hint,
    )(*args)


def parity_relayed(name, code_row, moved, members):
    slots = moved.shape[0]
    quarter = slots // members
    half = quarter // 2
    a, b, give_a, give_b, keep_c, keep_d, mine = kernel_call(
        parity_first_kernel,
        "parity_first_" + name,
        (flat(half),) * 6 + (flat(quarter),),
        [VMEM, VMEM],
        (VMEM,) * 7,
        cost=2 << 20,
    )(code_row, moved)
    back_a, back_b = swap(a, 0, members), swap(b, 1, members)
    stay_a, stay_b = swap(give_a, 0, members), swap(give_b, 1, members)
    send_c, send_d = second("parity_" + name, 0, 1 << 33, keep_c, keep_d, back_a, back_b)
    back_c, back_d = swap(send_c, 1, members), swap(send_d, 0, members)
    out = kernel_call(copy_kernel, "emit_" + name, flat(slots), [VMEM], VMEM, cost=2 << 20)(moved)
    parity = kernel_call(
        parity_last_kernel, "parity_last_" + name, flat(quarter), [VMEM] * 5, VMEM, cost=1 << 20
    )(mine, stay_a, stay_b, back_c, back_d)
    return out, parity


def parity_direct(name, key, shard, got, shards, members):
    slots = got.shape[0]
    quarter = slots // members
    side = kernel_call(
        other_core_kernel, "other_core_" + name, flat(slots // 2), [SMEM, VMEM], VMEM, cost=1 << 20
    )(shard, got)
    side = lax.ppermute(side, "shard", [(i, i ^ 1) for i in range(shards)])
    out, mine, *sends = kernel_call(
        emit_kernel,
        "emit_" + name,
        (flat(slots),) + (flat(quarter),) * members,
        [SMEM, SMEM, SMEM, VMEM, VMEM],
        (VMEM,) * (members + 1),
        cost=3 << 20,
    )(*key, shard, got, side)
    gots = {k: turn(sends[k - 1], k, members) for k in (2, 1, 3)}
    parity = kernel_call(
        parity_sum_kernel, "parity_sum_" + name, flat(quarter), [VMEM] * members, VMEM, cost=1 << 20
    )(mine, gots[1], gots[2], gots[3])
    return out, parity


def per_device(
    table_rows, adagrad_sums, lost_member, code_weight, new_owner, pending_rows, pending_grads
):
    members = lax.axis_size("code")
    shards = lax.axis_size("shard")
    member = lax.axis_index("code").astype(jnp.int32)[None]
    share = table_rows.shape[0] // members
    capacity = max(2, (2 * share + shards - 1) // shards)
    slots = shards * capacity
    half = share // 2
    entries = pending_grads.shape[0]
    scalars = [SMEM, SMEM, SMEM]
    key = (lost_member, pltpu.with_memory_space_constraint(code_weight, pltpu.HBM), member)
    owner = new_owner[:, 0]

    def buffers(count):
        return [pltpu.VMEM((count, half, 128), jnp.float32), pltpu.SemaphoreType.DMA((count,))]

    def keep_out(array):
        return pltpu.with_memory_space_constraint(array, pltpu.HBM)

    part = entries // 2 + 8
    send_a, send_b = kernel_call(
        front_kernel,
        "front_send",
        (flat(half + 2 * part), flat(half + 2 * part)),
        [SMEM, HBM, HBM, HBM, HBM],
        (VMEM, VMEM),
        cost=3 << 20,
        scratch_shapes=buffers(2)
        + [pltpu.SemaphoreType.DMA((4,)), pltpu.VMEM((entries // 128, 128), jnp.int32)]
        + [pltpu.SMEM((members,), jnp.float32), pltpu.SemaphoreType.DMA((2,))],
    )(lost_member, key[1], keep_out(adagrad_sums), keep_out(pending_grads), keep_out(pending_rows.reshape(-1, 128)))
    got_a, got_b = swap(send_a, 0, members), swap(send_b, 1, members)

    give_a, give_b, keep_c, keep_d, mine_sums = kernel_call(
        keep_kernel,
        "keep_sums",
        (flat(half), flat(half), flat(half), flat(half), flat(share)),
        scalars + [HBM],
        (VMEM,) * 5,
        cost=3 << 20,
        scratch_shapes=buffers(6),
    )(*key, keep_out(adagrad_sums))
    row_a, row_b, row_give_a, row_give_b = kernel_call(
        send_kernel,
        "send_rows",
        (flat(half),) * 4,
        scalars + [HBM],
        (VMEM,) * 4,
        cost=2 << 20,
        scratch_shapes=buffers(4),
    )(*key, keep_out(table_rows))
    give_a, give_b, row_a, row_b = lax.optimization_barrier((give_a, give_b, row_a, row_b))
    kept_a, kept_b = swap(give_a, 0, members), swap(give_b, 1, members)
    earlier = jnp.tril(owner[:, None] == owner[None, :], -1)
    rank = jnp.sum(earlier.astype(jnp.int32), axis=1)
    place = (owner * capacity + rank)[None, :]

    send_c, send_d = second("sums", part, 1 << 38, keep_c, keep_d, got_a, got_b)
    got_c, got_d = swap(send_c, 1, members), swap(send_d, 0, members)
    kept_a, kept_b, got_a, got_b = lax.optimization_barrier((kept_a, kept_b, got_a, got_b))
    part_totals, base_sums = kernel_call(
        totals_kernel, "pending_totals", (flat(share), flat(share)), [SMEM] + [VMEM] * 6, (VMEM, VMEM), cost=4 << 20
    )(member, send_a, got_a, got_b, mine_sums, kept_a, kept_b)
    row_a, row_b, row_give_a, row_give_b, got_c, got_d, part_totals, place, late_rows = lax.optimization_barrier(
        (row_a, row_b, row_give_a, row_give_b, got_c, got_d, part_totals, place, table_rows)
    )
    back_a, back_b = swap(row_a, 0, members), swap(row_b, 1, members)
    stay_a, stay_b = swap(row_give_a, 0, members), swap(row_give_b, 1, members)

    scratch = [
        pltpu.VMEM((share, 256), jnp.bfloat16),
        pltpu.VMEM((slots, 128), jnp.float32),
        pltpu.SemaphoreType.DMA((4,)),
    ]
    out_sums, new_sums, totals = kernel_call(
        sums_kernel,
        "place_sums",
        (flat(slots), flat(share), flat(share)),
        [VMEM] * 5,
        (HBM, VMEM, VMEM),
        cost=6 << 20,
        scratch_shapes=scratch,
    )(place, base_sums, got_c, got_d, part_totals)
    same_core = [list(range(core, shards, 2)) for core in range(2)]
    got_sums = lax.all_to_all(out_sums, "shard", 0, 0, tiled=True, axis_index_groups=same_core)

    row_c, row_d, mine_rows, code_row = kernel_call(
        stay_kernel,
        "stay_rows",
        (flat(half), flat(half), flat(share), flat(8)),
        scalars + [HBM],
        (VMEM,) * 4,
        cost=2 << 20,
        scratch_shapes=buffers(4),
    )(*key, keep_out(late_rows))
    send_c, send_d = second("rows", 0, 1 << 33, row_c, row_d, back_a, back_b)
    back_c, back_d = swap(send_c, 1, members), swap(send_d, 0, members)
    out_rows = kernel_call(
        rows_kernel, "place_rows", flat(slots), [VMEM] * 8, HBM, cost=6 << 20, scratch_shapes=scratch
    )(place, mine_rows, stay_a, stay_b, back_c, back_d, totals, new_sums)
    moved_rows = lax.all_to_all(out_rows, "shard", 0, 0, tiled=True)

    shard = lax.axis_index("shard").astype(jnp.int32)[None]
    final_sums, parity_sums = parity_direct("sums", (code_weight, member), shard, got_sums, shards, members)
    moved_rows, final_sums, parity_sums = lax.optimization_barrier((moved_rows, final_sums, parity_sums))
    final_rows, parity_rows = parity_relayed("rows", code_row, moved_rows, members)
    return (final_rows, final_sums, parity_rows, parity_sums)


def solution(mesh):
    in_specs = (
        P(("shard", "code"), None),
        P(("shard", "code"), None),
        P("shard"),
        P(),
        P(("shard", "code"), None),
        P(("shard", "code")),
        P(("shard", "code"), None),
    )
    out_specs = (
        P(("shard", "code"), None),
        P(("shard", "code"), None),
        P(("shard", "code"), None),
        P(("shard", "code"), None),
    )
    return jax.shard_map(
        per_device, mesh=mesh, in_specs=in_specs, out_specs=out_specs, check_vma=False
    )
```

```python
import jax
import jax.numpy as jnp
from jax import lax
from jax.experimental import pallas as pl
from jax.experimental.pallas import tpu as pltpu
from jax.sharding import PartitionSpec as P

step_size = 0.5
epsilon = 1e-08
MEMBERS = 4
TOP = float(jnp.finfo(jnp.bfloat16).max)
SLOT = 32
SMEM = pl.BlockSpec(memory_space=pltpu.SMEM)
VMEM = pl.BlockSpec(memory_space=pltpu.VMEM)
HBM = pl.BlockSpec(memory_space=pltpu.HBM)
PARAMS = pltpu.CompilerParams(vmem_limit_bytes=16 * 1024 * 1024)


def decode_weights(lost_ref, weight_ref):
    which = lost_ref[0]
    rows = [jnp.full((1, 128), weight_ref[c], jnp.float32) for c in range(MEMBERS)]
    parity_lost = which == 3
    divisor = jnp.where(which == 0, rows[0], jnp.where(which == 1, rows[1], rows[2]))
    divisor = jnp.where(parity_lost, jnp.ones_like(divisor), divisor)
    out = []
    for c in range(3):
        solved = jnp.where(parity_lost, rows[c], -rows[c] / divisor)
        out.append(jnp.where(which == c, jnp.zeros_like(solved), solved))
    out.append(jnp.where(parity_lost, jnp.zeros_like(divisor), 1.0 / divisor))
    return out


def split_halves(value):
    high = jnp.clip(value, -TOP, TOP).astype(jnp.bfloat16)
    low = (value - high.astype(jnp.float32)).astype(jnp.bfloat16)
    return high, low


def own_row(weights, member):
    own = weights[3]
    for c in range(3):
        own = jnp.where(member == c, weights[c], own)
    return own


def kernel_call(body, name, out_shape, in_specs, out_specs, cost=0, **kwargs):
    return pl.pallas_call(
        body,
        in_specs=in_specs,
        out_specs=out_specs,
        out_shape=out_shape,
        compiler_params=PARAMS,
        cost_estimate=pl.CostEstimate(flops=cost, bytes_accessed=cost, transcendentals=0),
        name=name,
        **kwargs,
    )


def flat(rows):
    return jax.ShapeDtypeStruct((rows, 128), jnp.float32)


def near(member):
    return member + 1 - 2 * lax.rem(member, 2), 3 - member


def scaled_pieces(table_ref, own, where, outs, buf_ref, sem_ref, others=()):
    half = buf_ref.shape[1]
    copies = []
    for i, (quarter, part) in enumerate(where):
        rows = pl.ds(pl.multiple_of(quarter * (2 * half) + part * half, 8), half)
        copies.append(pltpu.make_async_copy(table_ref.at[rows, :], buf_ref.at[i], sem_ref.at[i]))
        copies[-1].start()
    for copy in others:
        copy.start()
    own = own()
    for i, (out_ref, start) in enumerate(outs):
        copies[i].wait()
        out_ref[start : start + half, :] = own * buf_ref[i]
    for copy in others:
        copy.wait()


def passed_pieces(member):
    one, two = near(member)
    return [(3 - one, 0), (near(two)[0], 1)]


def given_pieces(member):
    one, two = near(member)
    return [(one, 0), (two, 1)]


def kept_pieces(member):
    one, two = near(member)
    return [(two, 0), (one, 1), (member, 0), (member, 1)]


def front_kernel(
    lost_ref, weight_hbm, table_ref, grads_ref, ids_hbm, a_ref, b_ref,
    buf_ref, sem_ref, grad_sem, ids_ref, weight_ref, small_sem
):
    member = lax.axis_index("code")
    part, lines = grads_ref.shape[0] // 2, ids_ref.shape[0] // 2
    half = buf_ref.shape[1]
    copies = [pltpu.make_async_copy(ids_hbm, ids_ref, small_sem.at[0])]
    for i, out_ref in enumerate((a_ref, b_ref)):
        for h in range(2):
            start = half + h * (part + 8)
            source = grads_ref.at[pl.ds(h * part, part), :]
            copies.append(pltpu.make_async_copy(source, out_ref.at[pl.ds(start, part), :], grad_sem.at[2 * i + h]))
    weights = pltpu.make_async_copy(weight_hbm, weight_ref, small_sem.at[1])
    weights.start()

    def own():
        weights.wait()
        return own_row(decode_weights(lost_ref, weight_ref), member)

    scaled_pieces(table_ref, own, passed_pieces(member), [(a_ref, 0), (b_ref, 0)], buf_ref, sem_ref, copies)
    ids = ids_ref[...].astype(jnp.float32)
    for out_ref in (a_ref, b_ref):
        for h in range(2):
            start = half + h * (part + 8) + part
            out_ref[start : start + lines, :] = ids[h * lines : (h + 1) * lines, :]
            out_ref[start + lines : start + 8, :] = jnp.zeros((8 - lines, 128), jnp.float32)


def keep_kernel(
    lost_ref, weight_ref, member_ref, table_ref, a_ref, b_ref, c_ref, d_ref, mine_ref, buf_ref, sem_ref
):
    member = member_ref[0]
    own = lambda: own_row(decode_weights(lost_ref, weight_ref), member)
    half = buf_ref.shape[1]
    outs = [(a_ref, 0), (b_ref, 0), (c_ref, 0), (d_ref, 0), (mine_ref, 0), (mine_ref, half)]
    scaled_pieces(table_ref, own, given_pieces(member) + kept_pieces(member), outs, buf_ref, sem_ref)


def send_kernel(lost_ref, weight_ref, member_ref, table_ref, a_ref, b_ref, give_a_ref, give_b_ref, buf_ref, sem_ref):
    member = member_ref[0]
    own = lambda: own_row(decode_weights(lost_ref, weight_ref), member)
    outs = [(ref, 0) for ref in (a_ref, b_ref, give_a_ref, give_b_ref)]
    scaled_pieces(table_ref, own, passed_pieces(member) + given_pieces(member), outs, buf_ref, sem_ref)


def stay_kernel(lost_ref, weight_ref, member_ref, table_ref, c_ref, d_ref, mine_ref, code_ref, buf_ref, sem_ref):
    member = member_ref[0]
    code_ref[...] = jnp.full(code_ref.shape, own_code_weight(weight_ref, member), jnp.float32)
    own = lambda: own_row(decode_weights(lost_ref, weight_ref), member)
    half = buf_ref.shape[1]
    outs = [(c_ref, 0), (d_ref, 0), (mine_ref, 0), (mine_ref, half)]
    scaled_pieces(table_ref, own, kept_pieces(member), outs, buf_ref, sem_ref)


def second_kernel(c_ref, d_ref, a_ref, b_ref, out_c_ref, out_d_ref):
    half = c_ref.shape[0]
    out_c_ref[:half, :] = c_ref[...] + a_ref[:half, :]
    out_d_ref[:half, :] = d_ref[...] + b_ref[:half, :]
    extra = out_c_ref.shape[0] - half
    if extra:
        out_c_ref[half:, :] = a_ref[half : half + extra, :]
        out_d_ref[half:, :] = b_ref[half + extra :, :]


def swap(array, which, members):
    pairs = [(i, i ^ 1) for i in range(members)] if which == 0 else [(i, 3 - i) for i in range(members)]
    return lax.ppermute(array, "code", pairs)


def finish(mine_ref, a_ref, b_ref, c_ref, d_ref):
    half = mine_ref.shape[0] // 2
    first = (mine_ref[:half, :] + a_ref[a_ref.shape[0] - half :, :]) + c_ref[:half, :]
    last = (mine_ref[half:, :] + b_ref[b_ref.shape[0] - half :, :]) + d_ref[:half, :]
    return jnp.concatenate([first, last], axis=0)


def add_hits(total, first, part_ref, start, entries):
    high, low = split_halves(part_ref[start : start + entries, :])
    both = jnp.concatenate([high, low], axis=1)
    targets = (lax.broadcasted_iota(jnp.int32, (total.shape[0], 128), 0) + first).astype(jnp.float32)
    lines = [part_ref[start + entries + j : start + entries + j + 1, :] for j in range(entries // 128)]
    hits = [jnp.where(targets == line, 1.0, 0.0).astype(jnp.bfloat16) for line in lines]
    return total + jnp.dot(jnp.concatenate(hits, axis=1), both, preferred_element_type=jnp.float32)


def totals_kernel(member_ref, own_ref, a_ref, b_ref, mine_ref, kept_a_ref, kept_b_ref, out_ref, base_ref):
    count = out_ref.shape[0]
    half = count // 2
    size = (own_ref.shape[0] - half) // 2
    total = jnp.zeros((count, 256), jnp.float32)
    for ref in (own_ref, a_ref, b_ref):
        for h in range(2):
            total = add_hits(total, member_ref[0] * count, ref, half + h * size, size - 8)
    out_ref[...] = total[:, :128] + total[:, 128:]
    base_ref[:half, :] = mine_ref[:half, :] + kept_a_ref[...]
    base_ref[half:, :] = mine_ref[half:, :] + kept_b_ref[...]


def spread(place_ref, values, out_ref, both_ref, stage_ref, sem_ref):
    high, low = split_halves(values)
    both_ref[:, :128] = high
    both_ref[:, 128:] = low
    slots, rows = out_ref.shape[0], values.shape[0]
    step = slots // sem_ref.shape[0]
    place = place_ref[...]
    copies = []
    for i in range(sem_ref.shape[0]):
        here = lax.broadcasted_iota(jnp.int32, (step, rows), 0) + i * step
        pick = jnp.where(here == place, 1.0, 0.0).astype(jnp.bfloat16)
        got = jnp.dot(pick, both_ref[...], preferred_element_type=jnp.float32)
        block = pl.ds(i * step, step)
        stage_ref[block, :] = got[:, :128] + got[:, 128:]
        copies.append(pltpu.make_async_copy(stage_ref.at[block, :], out_ref.at[block, :], sem_ref.at[i]))
        copies[-1].start()
    for copy in copies:
        copy.wait()


def sums_kernel(
    place_ref, base_ref, c_ref, d_ref, part_ref, out_ref, new_ref, total_ref, both_ref, stage_ref, sem_ref
):
    count = base_ref.shape[0]
    half = count // 2
    more = jnp.zeros((count, 256), jnp.float32)
    for ref in (c_ref, d_ref):
        more = add_hits(more, lax.axis_index("code") * count, ref, half, ref.shape[0] - half - 8)
    total = part_ref[...] + (more[:, :128] + more[:, 128:])
    total_ref[...] = total
    new = base_ref[...] + jnp.concatenate([c_ref[:half, :], d_ref[:half, :]], axis=0) + total * total
    new_ref[...] = new
    spread(place_ref, new, out_ref, both_ref, stage_ref, sem_ref)


def rows_kernel(
    place_ref, mine_ref, a_ref, b_ref, c_ref, d_ref, total_ref, sums_ref, out_ref, both_ref, stage_ref, sem_ref
):
    mine = finish(mine_ref, a_ref, b_ref, c_ref, d_ref)
    new = mine - step_size * total_ref[...] / (jnp.sqrt(sums_ref[...]) + epsilon)
    spread(place_ref, new, out_ref, both_ref, stage_ref, sem_ref)


def own_code_weight(weight_ref, member):
    own = weight_ref[3]
    for c in range(3):
        own = jnp.where(member == c, weight_ref[c], own)
    return own


def copy_kernel(moved_ref, out_ref):
    out_ref[...] = moved_ref[...]


def quarter_of(which, count):
    return pl.ds(pl.multiple_of(lax.rem(which, MEMBERS) * count, 8), count)


def parity_send_kernel(weight_ref, member_ref, moved_ref, mine_ref, *out_refs):
    member = member_ref[0]
    own = own_code_weight(weight_ref, member)
    count = mine_ref.shape[0]
    for k, out_ref in enumerate(out_refs):
        out_ref[...] = own * moved_ref[quarter_of(member + k + 1, count), :]
    mine_ref[...] = own * moved_ref[quarter_of(member, count), :]


def other_core_kernel(shard_ref, got_ref, out_ref):
    core = lax.rem(shard_ref[0], 2)
    for i in range(out_ref.shape[0] // SLOT):
        start = pl.multiple_of((2 * i + 1 - core) * SLOT, 8)
        out_ref[i * SLOT : (i + 1) * SLOT, :] = got_ref[pl.ds(start, SLOT), :]


def emit_kernel(weight_ref, member_ref, shard_ref, got_ref, side_ref, out_ref, mine_ref, *send_refs):
    core = lax.rem(shard_ref[0], 2)
    for i in range(side_ref.shape[0] // SLOT):
        start = pl.multiple_of((2 * i + core) * SLOT, 8)
        out_ref[pl.ds(start, SLOT), :] = got_ref[pl.ds(start, SLOT), :]
        start = pl.multiple_of((2 * i + 1 - core) * SLOT, 8)
        out_ref[pl.ds(start, SLOT), :] = side_ref[i * SLOT : (i + 1) * SLOT, :]
    parity_send_kernel(weight_ref, member_ref, out_ref, mine_ref, *send_refs)


def parity_sum_kernel(mine_ref, a_ref, b_ref, c_ref, out_ref):
    out_ref[...] = (mine_ref[...] + a_ref[...]) + (b_ref[...] + c_ref[...])


def parity_first_kernel(code_ref, moved_ref, *refs):
    member = lax.axis_index("code")
    own = code_ref[0:1, :]
    half = refs[0].shape[0]
    outs = [(ref, 0) for ref in refs] + [(refs[-1], half)]
    where = passed_pieces(member) + given_pieces(member) + kept_pieces(member)
    for (out_ref, start), (quarter, part) in zip(outs, where):
        rows = pl.ds(pl.multiple_of(quarter * (2 * half) + part * half, 8), half)
        out_ref[start : start + half, :] = own * moved_ref[rows, :]


def parity_last_kernel(mine_ref, a_ref, b_ref, c_ref, d_ref, out_ref):
    out_ref[...] = finish(mine_ref, a_ref, b_ref, c_ref, d_ref)


def turn(array, k, members):
    return lax.ppermute(array, "code", [(i, (i + k) % members) for i in range(members)])


def second(name, extra, hint, *args):
    half = args[0].shape[0]
    return kernel_call(
        second_kernel,
        "second_" + name,
        (flat(half + extra), flat(half + extra)),
        [VMEM] * 4,
        (VMEM, VMEM),
        cost=hint,
    )(*args)


def parity_relayed(name, code_row, moved, members):
    slots = moved.shape[0]
    quarter = slots // members
    half = quarter // 2
    a, b, give_a, give_b, keep_c, keep_d, mine = kernel_call(
        parity_first_kernel,
        "parity_first_" + name,
        (flat(half),) * 6 + (flat(quarter),),
        [VMEM, VMEM],
        (VMEM,) * 7,
        cost=2 << 20,
    )(code_row, moved)
    back_a, back_b = swap(a, 0, members), swap(b, 1, members)
    stay_a, stay_b = swap(give_a, 0, members), swap(give_b, 1, members)
    send_c, send_d = second("parity_" + name, 0, 1 << 33, keep_c, keep_d, back_a, back_b)
    back_c, back_d = swap(send_c, 1, members), swap(send_d, 0, members)
    out = kernel_call(copy_kernel, "emit_" + name, flat(slots), [VMEM], VMEM, cost=2 << 20)(moved)
    parity = kernel_call(
        parity_last_kernel, "parity_last_" + name, flat(quarter), [VMEM] * 5, VMEM, cost=1 << 20
    )(mine, stay_a, stay_b, back_c, back_d)
    return out, parity


def parity_direct(name, key, shard, got, shards, members):
    slots = got.shape[0]
    quarter = slots // members
    side = kernel_call(
        other_core_kernel, "other_core_" + name, flat(slots // 2), [SMEM, VMEM], VMEM, cost=1 << 20
    )(shard, got)
    side = lax.ppermute(side, "shard", [(i, i ^ 1) for i in range(shards)])
    out, mine, *sends = kernel_call(
        emit_kernel,
        "emit_" + name,
        (flat(slots),) + (flat(quarter),) * members,
        [SMEM, SMEM, SMEM, VMEM, VMEM],
        (VMEM,) * (members + 1),
        cost=3 << 20,
    )(*key, shard, got, side)
    gots = {k: turn(sends[k - 1], k, members) for k in (2, 1, 3)}
    parity = kernel_call(
        parity_sum_kernel, "parity_sum_" + name, flat(quarter), [VMEM] * members, VMEM, cost=1 << 20
    )(mine, gots[1], gots[2], gots[3])
    return out, parity


def per_device(
    table_rows, adagrad_sums, lost_member, code_weight, new_owner, pending_rows, pending_grads
):
    members = lax.axis_size("code")
    shards = lax.axis_size("shard")
    member = lax.axis_index("code").astype(jnp.int32)[None]
    share = table_rows.shape[0] // members
    capacity = max(2, (2 * share + shards - 1) // shards)
    slots = shards * capacity
    half = share // 2
    entries = pending_grads.shape[0]
    scalars = [SMEM, SMEM, SMEM]
    key = (lost_member, pltpu.with_memory_space_constraint(code_weight, pltpu.HBM), member)
    owner = new_owner[:, 0]

    def buffers(count):
        return [pltpu.VMEM((count, half, 128), jnp.float32), pltpu.SemaphoreType.DMA((count,))]

    def keep_out(array):
        return pltpu.with_memory_space_constraint(array, pltpu.HBM)

    part = entries // 2 + 8
    send_a, send_b = kernel_call(
        front_kernel,
        "front_send",
        (flat(half + 2 * part), flat(half + 2 * part)),
        [SMEM, HBM, HBM, HBM, HBM],
        (VMEM, VMEM),
        cost=3 << 20,
        scratch_shapes=buffers(2)
        + [pltpu.SemaphoreType.DMA((4,)), pltpu.VMEM((entries // 128, 128), jnp.int32)]
        + [pltpu.SMEM((members,), jnp.float32), pltpu.SemaphoreType.DMA((2,))],
    )(lost_member, key[1], keep_out(adagrad_sums), keep_out(pending_grads), keep_out(pending_rows.reshape(-1, 128)))
    got_a, got_b = swap(send_a, 0, members), swap(send_b, 1, members)

    give_a, give_b, keep_c, keep_d, mine_sums = kernel_call(
        keep_kernel,
        "keep_sums",
        (flat(half), flat(half), flat(half), flat(half), flat(share)),
        scalars + [HBM],
        (VMEM,) * 5,
        cost=3 << 20,
        scratch_shapes=buffers(6),
    )(*key, keep_out(adagrad_sums))
    row_a, row_b, row_give_a, row_give_b = kernel_call(
        send_kernel,
        "send_rows",
        (flat(half),) * 4,
        scalars + [HBM],
        (VMEM,) * 4,
        cost=2 << 20,
        scratch_shapes=buffers(4),
    )(*key, keep_out(table_rows))
    give_a, give_b, row_a, row_b = lax.optimization_barrier((give_a, give_b, row_a, row_b))
    kept_a, kept_b = swap(give_a, 0, members), swap(give_b, 1, members)
    earlier = jnp.tril(owner[:, None] == owner[None, :], -1)
    rank = jnp.sum(earlier.astype(jnp.int32), axis=1)
    place = (owner * capacity + rank)[None, :]

    send_c, send_d = second("sums", part, 1 << 38, keep_c, keep_d, got_a, got_b)
    got_c, got_d = swap(send_c, 1, members), swap(send_d, 0, members)
    kept_a, kept_b, got_a, got_b = lax.optimization_barrier((kept_a, kept_b, got_a, got_b))
    part_totals, base_sums = kernel_call(
        totals_kernel, "pending_totals", (flat(share), flat(share)), [SMEM] + [VMEM] * 6, (VMEM, VMEM), cost=4 << 20
    )(member, send_a, got_a, got_b, mine_sums, kept_a, kept_b)
    row_a, row_b, row_give_a, row_give_b, got_c, got_d, part_totals, place, late_rows = lax.optimization_barrier(
        (row_a, row_b, row_give_a, row_give_b, got_c, got_d, part_totals, place, table_rows)
    )
    back_a, back_b = swap(row_a, 0, members), swap(row_b, 1, members)
    stay_a, stay_b = swap(row_give_a, 0, members), swap(row_give_b, 1, members)

    scratch = [
        pltpu.VMEM((share, 256), jnp.bfloat16),
        pltpu.VMEM((slots, 128), jnp.float32),
        pltpu.SemaphoreType.DMA((2,)),
    ]
    out_sums, new_sums, totals = kernel_call(
        sums_kernel,
        "place_sums",
        (flat(slots), flat(share), flat(share)),
        [VMEM] * 5,
        (HBM, VMEM, VMEM),
        cost=6 << 20,
        scratch_shapes=scratch,
    )(place, base_sums, got_c, got_d, part_totals)
    same_core = [list(range(core, shards, 2)) for core in range(2)]
    got_sums = lax.all_to_all(out_sums, "shard", 0, 0, tiled=True, axis_index_groups=same_core)

    row_c, row_d, mine_rows, code_row = kernel_call(
        stay_kernel,
        "stay_rows",
        (flat(half), flat(half), flat(share), flat(8)),
        scalars + [HBM],
        (VMEM,) * 4,
        cost=2 << 20,
        scratch_shapes=buffers(4),
    )(*key, keep_out(late_rows))
    send_c, send_d = second("rows", 0, 1 << 33, row_c, row_d, back_a, back_b)
    back_c, back_d = swap(send_c, 1, members), swap(send_d, 0, members)
    out_rows = kernel_call(
        rows_kernel, "place_rows", flat(slots), [VMEM] * 8, HBM, cost=6 << 20, scratch_shapes=scratch
    )(place, mine_rows, stay_a, stay_b, back_c, back_d, totals, new_sums)
    moved_rows = lax.all_to_all(out_rows, "shard", 0, 0, tiled=True)

    shard = lax.axis_index("shard").astype(jnp.int32)[None]
    final_sums, parity_sums = parity_direct("sums", (code_weight, member), shard, got_sums, shards, members)
    moved_rows, final_sums, parity_sums = lax.optimization_barrier((moved_rows, final_sums, parity_sums))
    final_rows, parity_rows = parity_relayed("rows", code_row, moved_rows, members)
    return (final_rows, final_sums, parity_rows, parity_sums)


def solution(mesh):
    in_specs = (
        P(("shard", "code"), None),
        P(("shard", "code"), None),
        P("shard"),
        P(),
        P(("shard", "code"), None),
        P(("shard", "code")),
        P(("shard", "code"), None),
    )
    out_specs = (
        P(("shard", "code"), None),
        P(("shard", "code"), None),
        P(("shard", "code"), None),
        P(("shard", "code"), None),
    )
    return jax.shard_map(
        per_device, mesh=mesh, in_specs=in_specs, out_specs=out_specs, check_vma=False
    )
```
